128 devices in a mesh: rows: 8 (over x, core), cols: 16 (over y, z).
Axes of the slice: x: 4, y: 4, z: 4, core: 2. Of those that a mesh axis runs over, the one named last changes fastest.
Arguments:
- grad: float32 [7168, 4096], P('rows', 'cols'), may hold values from -40 to 40
- basis: float32 [7168, 7168], P('rows', 'cols'), may hold values from -0.0625 to 0.0625
- mom_rot: float32 [7168, 4096], P('cols', 'rows'), may hold values from -6 to 6
- var_rot: float32 [7168, 4096], P('cols', 'rows'), may hold values from 0.25 to 4
- mom_plain: float32 [7168, 4096], P('rows', 'cols'), may hold values from -6 to 6
- var_plain: float32 [7168, 4096], P('rows', 'cols'), may hold values from 0.25 to 4
Outputs:
- update: float32 [7168, 4096], P('rows', 'cols')
- new_mom_rot: float32 [7168, 4096], P('cols', 'rows')
- new_var_rot: float32 [7168, 4096], P('cols', 'rows')
- new_mom_plain: float32 [7168, 4096], P('rows', 'cols')
- new_var_plain: float32 [7168, 4096], P('rows', 'cols')
The draws below stay inside these ranges and needn't reach their ends.
All inputs are finite; a program needn't handle non-finite values.
Results may differ from the reference program's by a relative error of at most 0.00007.
Values sent between devices are 32-bit elements; how exact they have to be, the bound alone decides.
A program may use at most 128 MiB of HBM per device.

```python
import math
import jax
import jax.numpy as jnp
from jax import lax

M = 7168
N = 4096
STEP = 10


def draw_grad(key, part):
    key = jax.random.fold_in(key, 1)
    key_base, key_rows, key_cols = jax.random.split(key, 3)
    trend = jnp.exp(math.log(10.0) * jnp.arange(M, dtype=jnp.float32) / M)[:, None]
    rough_rows = jax.random.uniform(key_rows, (M, 1), jnp.float32, 0.5, 2.0)
    rough_cols = jax.random.uniform(key_cols, (1, N), jnp.float32, 0.5, 2.0)
    base = jnp.clip(jax.random.normal(key_base, (M, N), jnp.float32), -3.0, 3.0)
    return (base * trend * rough_rows * rough_cols / 3.0).astype(jnp.float32)


def block_scale(rng, shape, pieces, smallest, largest):
    gain = 1.0
    for position, blocks in pieces:
        steps = jax.random.uniform(jax.random.fold_in(jax.random.fold_in(rng, 6), position), (blocks,), jnp.float32, smallest / len(pieces), largest / len(pieces))
        gain = gain * jnp.repeat(jnp.exp(steps), shape[position] // blocks).reshape((-1,) + (1,) * (len(shape) - 1 - position))
    return gain


def scatter_about(rng, extent, deviation, reach, cuts=(), held_as=jnp.bfloat16):
    drawn = deviation * jax.random.normal(rng, extent, jnp.float32)
    if cuts:
        drawn = drawn * block_scale(rng, extent, cuts, -0.22, 0.18)
    return jnp.clip(drawn, -reach, reach).astype(held_as)


def setup_inputs(seed: int = 0) -> dict:
    seeds = jax.random.split(jax.random.key(seed), 7)
    return {
        "grad": draw_grad(jax.random.fold_in(seeds[6], 71), 0),
        "basis": scatter_about(seeds[1], (M, M), M ** -0.5, 0.0625, ((0, 8), (1, 16)), jnp.float32),
        "mom_rot": scatter_about(seeds[2], (M, N), 1.0, 6.0, ((0, 16), (1, 8)), jnp.float32),
        "var_rot": jnp.clip(jnp.exp(math.log(4.0) - 2.7725887 * jax.random.uniform(seeds[3], (M, N), jnp.float32) ** block_scale(seeds[3], (M, N), ((0, 16), (1, 8)), -0.2, 0.2)), 0.25, 4.0),
        "mom_plain": scatter_about(seeds[4], (M, N), 1.0, 6.0, ((0, 8), (1, 16)), jnp.float32),
        "var_plain": jnp.clip(jnp.exp(math.log(4.0) - 2.7725887 * jax.random.uniform(seeds[5], (M, N), jnp.float32) ** block_scale(seeds[5], (M, N), ((0, 8), (1, 16)), -0.2, 0.2)), 0.25, 4.0),
    }


beta_one = 0.95
beta_two = 0.95
eps_adam = 1e-08

def adam_step(moment, second, values):
    moment_new = beta_one * moment + (1.0 - beta_one) * values
    second_new = beta_two * second + (1.0 - beta_two) * values * values
    corr_one = 1.0 - beta_one ** STEP
    corr_two = 1.0 - beta_two ** STEP
    step_dir = moment_new / corr_one / (jnp.sqrt(second_new / corr_two) + eps_adam)
    return (moment_new, second_new, step_dir)

def reference(grad, basis, mom_rot, var_rot, mom_plain, var_plain):
    rotated = lax.dot_general(basis, grad, (((0,), (0,)), ((), ())), precision=lax.Precision.HIGHEST, preferred_element_type=jnp.float32)
    new_mom_rot, new_var_rot, direction = adam_step(mom_rot, var_rot, rotated)
    back = jnp.dot(basis, direction, precision=lax.Precision.HIGHEST, preferred_element_type=jnp.float32)
    new_mom_plain, new_var_plain, plain = adam_step(mom_plain, var_plain, grad)
    graft = jnp.sqrt(jnp.sum(plain * plain))
    own = jnp.sqrt(jnp.sum(back * back))
    update = back * (graft / (own + 1e-06))
    return (update, new_mom_rot, new_var_rot, new_mom_plain, new_var_plain)
```

```python
import functools

import jax
import jax.numpy as jnp
from jax import lax
from jax.experimental import pallas as pl
from jax.experimental.pallas import tpu as pltpu
from jax.sharding import PartitionSpec as P

STEP = 10
BETA = 0.95
EPS = 1e-08
CORR = 1.0 - BETA**STEP

F32 = jnp.float32
BF16 = jnp.bfloat16

KI = 896
KJ = 448
KN = 256
HJ = KJ // 2
HALF = HJ // 2
OFF = (0, 1, 3, 2)
N_COPIES = 96


def adam(moment, second, values):
    moment_new = BETA * moment + (1.0 - BETA) * values
    second_new = BETA * second + (1.0 - BETA) * values * values
    direction = moment_new / CORR / (jnp.sqrt(second_new / CORR) + EPS)
    return moment_new, second_new, direction


def split(a):
    hi = a.astype(BF16)
    lo = (a - hi.astype(F32)).astype(BF16)
    return hi, lo


def dot3(lh, ll, rh, rl):
    dot = functools.partial(jnp.dot, preferred_element_type=F32)
    return dot(lh, rh) + (dot(lh, rl) + dot(ll, rh))


def kernel(
    grad, basis, mom_rot, var_rot, mom_plain, var_plain,
    update, new_mom_rot, new_var_rot, new_mom_plain, new_var_plain,
    gg, ghi, glo, bg, bhi, blo, bthi, btlo, part, rx, ra, rb, rt, at,
    m2, v2, direc, dd, dhi, dlo, back, ya, yb, mp, vp, norm, nrecv,
    ssem, rsem, lsem,
):
    rows = lax.axis_index("rows")
    cols = lax.axis_index("cols")
    x, c = rows // 2, rows % 2
    y, z = cols // 4, cols % 4
    o = 1 - c

    def dev(dx=0, dc=0, dy=0, dz=0):
        r = (x + dx) % 4 * 2 + (c + dc) % 2
        q = (y + dy) % 4 * 4 + (z + dz) % 4
        return (r, q)

    xp, xm, xo = (x + 1) % 4, (x + 3) % 4, (x + 2) % 4
    yp, ym, yo = (y + 1) % 4, (y + 3) % 4, (y + 2) % 4
    mine = pl.multiple_of(c * HJ, HJ)
    other = pl.multiple_of(o * HJ, HJ)

    partners = [dev(dc=1)]
    for d in (1, 2, 3):
        partners += [dev(dx=d), dev(dy=d), dev(dz=d)]
    barrier = pltpu.get_barrier_semaphore()
    for p in partners:
        pl.semaphore_signal(barrier, inc=1, device_id=p, device_id_type=pl.DeviceIdType.MESH)
    pl.semaphore_wait(barrier, len(partners))

    count = [0, 0]
    started = []

    def send(src, dst, to):
        i = count[0]
        count[0] += 1
        copy = pltpu.make_async_remote_copy(
            src_ref=src, dst_ref=dst, send_sem=ssem.at[i], recv_sem=rsem.at[i],
            device_id=to, device_id_type=pl.DeviceIdType.MESH,
        )
        copy.start()
        started.append(copy)
        return copy

    def local(src, dst):
        i = count[1]
        count[1] += 1
        copy = pltpu.make_async_copy(src, dst, lsem.at[i])
        copy.start()
        return copy

    g_up = send(grad, gg.at[y], dev(dy=1))
    g_dn = send(grad, gg.at[y], dev(dy=3))
    b_up = send(basis, bg.at[2], dev(dz=1))
    b_dn = send(basis, bg.at[1], dev(dz=3))
    own_g = local(grad, gg.at[y])
    own_b = local(basis, bg.at[0])
    own_plain = [local(mom_plain, mp), local(var_plain, vp)]
    moments = []
    for t in range(2):
        for src, dst in ((mom_rot, m2), (var_rot, v2)):
            lanes = pl.ds(t * KN, KN)
            moments.append(send(src.at[pl.ds(other, HJ), lanes], dst.at[2 * c + t], dev(dc=1)))
    moments_own = []
    for t in range(2):
        for src, dst in ((mom_rot, m2), (var_rot, v2)):
            lanes = pl.ds(t * KN, KN)
            moments_own.append(local(src.at[pl.ds(mine, HJ), lanes], dst.at[2 * c + t]))

    own_g.wait()
    for copy in own_plain:
        copy.wait()
    norm[...] = jnp.zeros_like(norm)

    @pl.loop(0, KI // 64)
    def _(i):
        s = pl.ds(pl.multiple_of(i * 64, 64), 64)
        m, v, d = adam(mp[s, :], vp[s, :], gg[y, s, :])
        mp[s, :] = m
        vp[s, :] = v
        norm[0] += jnp.sum((d * d).reshape(8, 8, KN), axis=0)

    out_plain = [local(mp, new_mom_plain), local(vp, new_var_plain)]

    def split_grad(n):
        @pl.loop(0, KI // 128)
        def _(i):
            s = pl.ds(pl.multiple_of(i * 128, 128), 128)
            hi, lo = split(gg[n, s, :])
            ghi[n, s, :] = hi
            glo[n, s, :] = lo

    def turn_basis(r):
        for q in range(0, KJ, 128):
            w = min(128, KJ - q)
            hi, lo = split(bg[r, :, q:q + w].T)
            bthi[q:q + w, :] = hi
            btlo[q:q + w, :] = lo

    def product_one(r):
        @pl.loop(0, 4)
        def _(n):
            part[r, n] = dot3(bthi[...], btlo[...], ghi[n], glo[n])

    split_grad(y)
    own_b.wait()
    turn_basis(0)
    g_up.wait_recv()
    g_dn.wait_recv()
    g_up2 = send(gg.at[ym, pl.ds(0, KI // 2)], gg.at[ym, pl.ds(0, KI // 2)], dev(dy=1))
    g_dn2 = send(gg.at[yp, pl.ds(KI // 2, KI // 2)], gg.at[yp, pl.ds(KI // 2, KI // 2)], dev(dy=3))
    split_grad(ym)
    split_grad(yp)
    g_up2.wait_recv()
    g_dn2.wait_recv()
    split_grad(yo)

    state = {}

    def s0(r):
        if r == 1:
            b_up.wait_recv()
            b_dn.wait_recv()
            top, low = pl.ds(0, KI // 2), pl.ds(KI // 2, KI // 2)
            state["b2"] = (
                send(bg.at[2, top], bg.at[3, top], dev(dz=1)),
                send(bg.at[1, low], bg.at[3, low], dev(dz=3)),
            )
        if r == 3:
            for copy in state["b2"]:
                copy.wait_recv()
        if r:
            turn_basis(r)
        product_one(r)
        state["x", r] = send(part.at[r, :, pl.ds(other, HJ)], rx.at[r], dev(dc=1))

    def s1(r):
        state["x", r].wait_recv()

        @pl.loop(0, 4)
        def _(n):
            part[r, n, pl.ds(mine, HJ), :] += rx[r, n]

        first = part.at[r, xo, pl.ds(mine, HALF)]
        second = part.at[r, xo, pl.ds(mine + HALF, HALF)]
        state["ra", r] = (send(first, ra.at[r, 0], dev(dx=1)), send(second, ra.at[r, 1], dev(dx=3)))

    def s2(r):
        up, dn = state["ra", r]
        up.wait_recv()
        part[r, xp, pl.ds(mine, HALF), :] += ra[r, 0]
        a = send(part.at[r, xp, pl.ds(mine, HJ)], rb.at[r, 0], dev(dx=1))
        dn.wait_recv()
        part[r, xm, pl.ds(mine + HALF, HALF), :] += ra[r, 1]
        b = send(part.at[r, xm, pl.ds(mine, HJ)], rb.at[r, 1], dev(dx=3))
        state["rb", r] = (a, b)

    def s3(r):
        for copy in state["rb", r]:
            copy.wait_recv()
        rt[r] = part[r, x, pl.ds(mine, HJ), :] + rb[r, 0] + rb[r, 1]
        if r:
            state["at", r] = send(rt.at[r], at.at[r], dev(dz=OFF[r]))

    def s4(r):
        if r == 0:
            for copy in moments:
                copy.wait_recv()
            for copy in moments_own:
                copy.wait()
            values = rt[r]
        else:
            state["at", r].wait_recv()
            values = at[r]
        zs = (z + 4 - OFF[r]) % 4
        m, v, d = adam(m2[zs], v2[zs], values)
        m2[zs] = m
        v2[zs] = v
        if r == 0:
            dd[r, x, pl.ds(mine, HJ), :] = d
        else:
            direc[r] = d
            state["d", r] = send(direc.at[r], dd.at[r, x, pl.ds(mine, HJ)], dev(dz=4 - OFF[r]))

    def tile(r, n):
        return dd.at[r, n, pl.ds(mine, HJ)]

    def s5(r):
        if r:
            state["d", r].wait_recv()
        state["ag", r] = (
            send(tile(r, x), tile(r, x), dev(dx=1)),
            send(tile(r, x), tile(r, x), dev(dx=3)),
        )
        state["dc", r] = [send(tile(r, x), tile(r, x), dev(dc=1))]

    def s6(r):
        up, dn = state["ag", r]
        up.wait_recv()
        first = dd.at[r, xm, pl.ds(mine, HALF)]
        a = send(first, first, dev(dx=1))
        dn.wait_recv()
        second = dd.at[r, xp, pl.ds(mine + HALF, HALF)]
        b = send(second, second, dev(dx=3))
        state["ag2", r] = (a, b)
        state["dc", r].append(send(tile(r, xm), tile(r, xm), dev(dc=1)))
        state["dc", r].append(send(tile(r, xp), tile(r, xp), dev(dc=1)))

    def s7(r):
        for copy in state["ag2", r]:
            copy.wait_recv()
        state["dc", r].append(send(tile(r, xo), tile(r, xo), dev(dc=1)))

    def s8(r, first, last):
        for copy in state["dc", r]:
            copy.wait_recv()

        @pl.loop(0, KI // 64)
        def _(i):
            s = pl.ds(pl.multiple_of(i * 64, 64), 64)
            hi, lo = split(bg[r, s, :])
            bhi[s, :] = hi
            blo[s, :] = lo

        @pl.loop(0, 4)
        def _(n):
            hi, lo = split(dd[r, n])
            dhi[n] = hi
            dlo[n] = lo

        def one(n):
            new = dot3(bhi[...], blo[...], dhi[n], dlo[n])
            back[n] = new if first else back[n] + new

        if not last:
            pl.loop(0, 4)(one)
            return
        top, low = pl.ds(0, KI // 2), pl.ds(KI // 2, KI // 2)
        one(yo)
        up = send(back.at[yo, top], ya.at[0], dev(dy=1))
        dn = send(back.at[yo, low], ya.at[1], dev(dy=3))
        one(yp)
        one(ym)
        up.wait_recv()
        back[yp, top, :] += ya[0]
        up2 = send(back.at[yp], yb.at[0], dev(dy=1))
        dn.wait_recv()
        back[ym, low, :] += ya[1]
        dn2 = send(back.at[ym], yb.at[1], dev(dy=3))
        one(y)
        state["yb"] = (up2, dn2)

    order = [
        (s0, 0), (s0, 1), (s1, 0), (s0, 2), (s2, 0), (s1, 1), (s3, 0), (s4, 0), (s5, 0),
        (s2, 1), (s1, 2), (s3, 1), (s2, 2), (s4, 1), (s3, 2), (s6, 0), (s4, 2), (s5, 1), (s5, 2),
        (s0, 3), (s7, 0), (s6, 1), (s1, 3), (s7, 1), (s6, 2), (s2, 3), (s7, 2),
        (s3, 3), (s8, 0), (s4, 3), (s8, 1), (s5, 3), (s8, 2), (s6, 3), (s7, 3), (s8, 3),
    ]
    for stage, r in order:
        if stage is s8:
            s8(r, first=r == 0, last=r == 3)
        else:
            stage(r)

    lanes = [pl.ds(t * KN, KN) for t in range(2)]
    out_rot, out_rot_own = [], []
    for t in range(2):
        for src, dst in ((m2, new_mom_rot), (v2, new_var_rot)):
            out_rot.append(send(src.at[2 * o + t], dst.at[pl.ds(mine, HJ), lanes[t]], dev(dc=1)))
            out_rot_own.append(local(src.at[2 * c + t], dst.at[pl.ds(mine, HJ), lanes[t]]))

    for copy in state["yb"]:
        copy.wait_recv()

    @pl.loop(0, KI // 64)
    def _(i):
        s = pl.ds(pl.multiple_of(i * 64, 64), 64)
        b = back[y, s, :] + yb[0, s, :] + yb[1, s, :]
        back[y, s, :] = b
        norm[1] += jnp.sum((b * b).reshape(8, 8, KN), axis=0)

    slot = 0
    for moves in (
        [dev(dc=1)],
        [dev(dx=d) for d in (1, 2, 3)],
        [dev(dy=d) for d in (1, 2, 3)],
        [dev(dz=d) for d in (1, 2, 3)],
    ):
        copies = []
        for to in moves:
            copies.append((slot, send(norm, nrecv.at[slot], to)))
            slot += 1
        for _, copy in copies:
            copy.wait()
        started[:] = [s for s in started if all(s is not copy for _, copy in copies)]
        total = norm[...]
        for k, _ in copies:
            total += nrecv[k]
        norm[...] = total
    graft = jnp.sqrt(jnp.sum(norm[0], keepdims=True))
    own = jnp.sqrt(jnp.sum(norm[1], keepdims=True))
    scale = graft / (own + 1e-06)

    for copy in out_plain:
        copy.wait()

    @pl.loop(0, KI // 64)
    def _(i):
        s = pl.ds(pl.multiple_of(i * 64, 64), 64)
        mp[s, :] = back[y, s, :] * scale

    last = local(mp, update)
    for copy in started:
        copy.wait_send()
    for copy in out_rot:
        copy.wait_recv()
    for copy in out_rot_own:
        copy.wait()
    last.wait()


def per_device(grad, basis, mom_rot, var_rot, mom_plain, var_plain):
    plain = jax.ShapeDtypeStruct((KI, KN), F32)
    rot = jax.ShapeDtypeStruct((KJ, 2 * KN), F32)
    scratch = [
        pltpu.VMEM((4, KI, KN), F32),
        pltpu.VMEM((4, KI, KN), BF16),
        pltpu.VMEM((4, KI, KN), BF16),
        pltpu.VMEM((4, KI, KJ), F32),
        pltpu.VMEM((KI, KJ), BF16),
        pltpu.VMEM((KI, KJ), BF16),
        pltpu.VMEM((KJ, KI), BF16),
        pltpu.VMEM((KJ, KI), BF16),
        pltpu.VMEM((4, 4, KJ, KN), F32),
        pltpu.VMEM((4, 4, HJ, KN), F32),
        pltpu.VMEM((4, 2, HALF, KN), F32),
        pltpu.VMEM((4, 2, HJ, KN), F32),
        pltpu.VMEM((4, HJ, KN), F32),
        pltpu.VMEM((4, HJ, KN), F32),
        pltpu.VMEM((4, HJ, KN), F32),
        pltpu.VMEM((4, HJ, KN), F32),
        pltpu.VMEM((4, HJ, KN), F32),
        pltpu.VMEM((4, 4, KJ, KN), F32),
        pltpu.VMEM((4, KJ, KN), BF16),
        pltpu.VMEM((4, KJ, KN), BF16),
        pltpu.VMEM((4, KI, KN), F32),
        pltpu.VMEM((2, KI // 2, KN), F32),
        pltpu.VMEM((2, KI, KN), F32),
        pltpu.VMEM((KI, KN), F32),
        pltpu.VMEM((KI, KN), F32),
        pltpu.VMEM((2, 8, KN), F32),
        pltpu.VMEM((10, 2, 8, KN), F32),
        pltpu.SemaphoreType.DMA((N_COPIES,)),
        pltpu.SemaphoreType.DMA((N_COPIES,)),
        pltpu.SemaphoreType.DMA((24,)),
    ]
    return pl.pallas_call(
        kernel,
        out_shape=(plain, rot, rot, plain, plain),
        in_specs=[pl.BlockSpec(memory_space=pl.ANY)] * 6,
        out_specs=[pl.BlockSpec(memory_space=pl.ANY)] * 5,
        scratch_shapes=scratch,
        compiler_params=pltpu.CompilerParams(
            collective_id=0, has_side_effects=True, vmem_limit_bytes=63 * 1024 * 1024
        ),
        cost_estimate=pl.CostEstimate(flops=20_000_000_000, bytes_accessed=12_000_000, transcendentals=0),
    )(grad, basis, mom_rot, var_rot, mom_plain, var_plain)


def solution(mesh):
    return jax.shard_map(
        per_device,
        mesh=mesh,
        in_specs=(
            P("rows", "cols"),
            P("rows", "cols"),
            P("cols", "rows"),
            P("cols", "rows"),
            P("rows", "cols"),
            P("rows", "cols"),
        ),
        out_specs=(
            P("rows", "cols"),
            P("cols", "rows"),
            P("cols", "rows"),
            P("rows", "cols"),
            P("rows", "cols"),
        ),
        check_vma=False,
    )
```

```python
import functools

import jax
import jax.numpy as jnp
from jax import lax
from jax.experimental import pallas as pl
from jax.experimental.pallas import tpu as pltpu
from jax.sharding import PartitionSpec as P

STEP = 10
BETA = 0.95
EPS = 1e-08
CORR = 1.0 - BETA**STEP

F32 = jnp.float32
BF16 = jnp.bfloat16

KI = 896
KJ = 448
KN = 256
QJ = KJ // 2
HN = KN // 2
CJ = QJ // 2
CHUNKS = ((0, 0), (0, 1), (1, 1), (3, 0), (1, 0), (3, 1), (2, 0), (2, 1))
GROUPS = ((0, 2), (2, 4), (4, 6), (6, 7), (7, 8))
N_COPIES = 176


def adam(moment, second, values):
    moment_new = BETA * moment + (1.0 - BETA) * values
    second_new = BETA * second + (1.0 - BETA) * values * values
    direction = moment_new / CORR / (jnp.sqrt(second_new / CORR) + EPS)
    return moment_new, second_new, direction


def split(a):
    hi = a.astype(BF16)
    lo = (a - hi.astype(F32)).astype(BF16)
    return hi, lo


def dot3(lh, ll, rh, rl):
    dot = functools.partial(jnp.dot, preferred_element_type=F32)
    return dot(lh, rh) + (dot(lh, rl) + dot(ll, rh))


def kernel(
    grad, basis_t, mom_rot, var_rot, mom_plain, var_plain,
    out_back, out_norm, new_mom_rot, new_var_rot, new_mom_plain, new_var_plain,
    gg, ghi, glo, bt, lhi, llo, bhi, blo, part, rx, ra, rb, rt, at,
    m2, v2, direc, dd, dhi, dlo, back, ya, yb, mp, vp, norm, nrecv,
    ssem, rsem, lsem,
):
    rows = lax.axis_index("rows")
    cols = lax.axis_index("cols")
    x, c = rows // 2, rows % 2
    y, z = cols // 4, cols % 4
    o = 1 - c

    def dev(dx=0, dc=0, dy=0, dz=0):
        r = (x + dx) % 4 * 2 + (c + dc) % 2
        q = (y + dy) % 4 * 4 + (z + dz) % 4
        return (r, q)

    xp, xm, xo = (x + 1) % 4, (x + 3) % 4, (x + 2) % 4
    yp, ym, yo = (y + 1) % 4, (y + 3) % 4, (y + 2) % 4
    mine = pl.ds(pl.multiple_of(c * CJ, CJ), CJ)
    other = pl.ds(pl.multiple_of(o * CJ, CJ), CJ)
    top, low = pl.ds(0, KI // 2), pl.ds(KI // 2, KI // 2)

    norm_moves = (
        [dev(dc=1)] + [dev(dx=d, dc=e) for d in (1, 2, 3) for e in (0, 1)],
        [dev(dy=d) for d in (1, 2, 3)],
        [dev(dz=d) for d in (1, 2, 3)],
    )
    partners = [p for moves in norm_moves for p in moves]
    barrier = pltpu.get_barrier_semaphore()
    for p in partners:
        pl.semaphore_signal(barrier, inc=1, device_id=p, device_id_type=pl.DeviceIdType.MESH)
    pl.semaphore_wait(barrier, len(partners))

    count = [0, 0]
    started = []

    def send(src, dst, to):
        i = count[0]
        count[0] += 1
        copy = pltpu.make_async_remote_copy(
            src_ref=src, dst_ref=dst, send_sem=ssem.at[i], recv_sem=rsem.at[i],
            device_id=to, device_id_type=pl.DeviceIdType.MESH,
        )
        copy.start()
        started.append(copy)
        return copy

    def local(src, dst):
        i = count[1]
        count[1] += 1
        copy = pltpu.make_async_copy(src, dst, lsem.at[i])
        copy.start()
        return copy

    state = {}

    def arrived(key):
        for copy in state.pop(key, ()):
            copy.wait_recv()

    def chunk(i):
        return bt.at[pl.ds(i * QJ, QJ)]

    def gather_grad(h):
        own = grad.at[:, pl.ds(h * HN, HN)]
        state["g", h] = [send(own, gg.at[h, y], dev(dy=1)), send(own, gg.at[h, y], dev(dy=3))]

    gather_grad(0)
    halves = [basis_t.at[pl.ds(q * QJ, QJ)] for q in range(2)]
    state["b", 3] = [send(halves[0], chunk(3), dev(dz=1))]
    state["b", 2] = [send(halves[1], chunk(2), dev(dz=3))]
    state["b", 5] = [send(halves[1], chunk(5), dev(dz=1))]
    state["b", 4] = [send(halves[0], chunk(4), dev(dz=3))]
    own_g = [local(grad.at[:, pl.ds(h * HN, HN)], gg.at[h, y]) for h in range(2)]
    own_b = [local(basis_t, bt.at[pl.ds(0, KJ)])]
    own_plain = [local(mom_plain, mp), local(var_plain, vp)]
    state["mv"] = [send(src.at[:, other], dst.at[c], dev(dc=1)) for src, dst in ((mom_rot, m2), (var_rot, v2))]
    own_mv = [local(src.at[:, mine], dst.at[c]) for src, dst in ((mom_rot, m2), (var_rot, v2))]

    norm[...] = jnp.zeros_like(norm)
    out_plain = []

    def done(copies):
        while copies:
            copies.pop().wait()

    def plain():
        done(own_g)
        done(own_plain)

        @pl.loop(0, KI // 64)
        def _(i):
            s = pl.ds(pl.multiple_of(i * 64, 64), 64)
            for h in range(2):
                lanes = slice(h * HN, (h + 1) * HN)
                m, v, d = adam(mp[s, lanes], vp[s, lanes], gg[h, y, s, :])
                mp[s, lanes] = m
                vp[s, lanes] = v
                norm[0] += jnp.sum((d * d).reshape(8, 8, HN), axis=0)

        out_plain.append(local(mp, new_mom_plain))
        out_plain.append(local(vp, new_var_plain))

    def split_grad(h, n):
        @pl.loop(0, KI // 128)
        def _(i):
            s = pl.ds(pl.multiple_of(i * 128, 128), 128)
            hi, lo = split(gg[h, n, s, :])
            ghi[h, n, s, :] = hi
            glo[h, n, s, :] = lo

    def gf(h):
        up, dn = state.pop(("g", h))
        up.wait_recv()
        a = send(gg.at[h, ym, top], gg.at[h, ym, top], dev(dy=1))
        dn.wait_recv()
        b = send(gg.at[h, yp, low], gg.at[h, yp, low], dev(dy=3))
        state["g2", h] = [a, b]
        if h == 0:
            gather_grad(1)

    def gs(h):
        done(own_g)
        for n in (y, ym, yp):
            split_grad(h, n)

    def gs2(h):
        arrived(("g2", h))
        split_grad(h, yo)

    def bf(way):
        if way == 0:
            arrived(("b", 3))
            state["b", 6] = [send(chunk(3), chunk(6), dev(dz=1))]
        else:
            arrived(("b", 2))
            state["b", 7] = [send(chunk(2), chunk(7), dev(dz=3))]

    def basis_there(lo, hi):
        for i in range(lo, hi):
            if i < 2:
                done(own_b)
            arrived(("b", i))

    def away(g):
        return [i for i in range(*GROUPS[g]) if CHUNKS[i][0]]

    def ways(g):
        lo, hi = GROUPS[g]
        if hi - lo == 2:
            return [(pl.ds(lo, 1), mine), (pl.ds(lo + 1, 1), mine)]
        start = pl.multiple_of(c * CJ, CJ)
        return [
            (pl.ds(lo, 1), pl.ds(start, CJ // 2)),
            (pl.ds(lo, 1), pl.ds(pl.multiple_of(start + CJ // 2, CJ // 2), CJ // 2)),
        ]

    def ways_share(g):
        lo, hi = GROUPS[g]
        if hi - lo == 2:
            return [(pl.ds(lo, 1), pl.ds(0, CJ)), (pl.ds(lo + 1, 1), pl.ds(0, CJ))]
        return [(pl.ds(lo, 1), pl.ds(0, CJ // 2)), (pl.ds(lo, 1), pl.ds(CJ // 2, CJ // 2))]

    def s0(g, h):
        lo, hi = GROUPS[g]
        basis_there(lo, hi)
        size = (hi - lo) * QJ
        high, rest = split(bt[lo * QJ:hi * QJ, :])
        lhi[:size, :] = high
        llo[:size, :] = rest

        @pl.loop(0, 2)
        def _(p):
            rh = jnp.concatenate([ghi[h, 2 * p], ghi[h, 2 * p + 1]], axis=1)
            rl = jnp.concatenate([glo[h, 2 * p], glo[h, 2 * p + 1]], axis=1)
            new = dot3(lhi[:size, :], llo[:size, :], rh, rl)
            for i in range(hi - lo):
                part[h, 2 * p, lo + i] = new[i * QJ:(i + 1) * QJ, :HN]
                part[h, 2 * p + 1, lo + i] = new[i * QJ:(i + 1) * QJ, HN:]

        group = pl.ds(lo, hi - lo)
        state["x", g, h] = [send(part.at[h, :, group, other], rx.at[h, :, group], dev(dc=1))]

    def s1(g, h):
        lo, hi = GROUPS[g]
        arrived(("x", g, h))
        group = pl.ds(lo, hi - lo)
        for n in range(4):
            part[h, n, group, mine, :] += rx[h, n, group]
        (first, up), (second, dn) = ways(g)
        (first_r, up_r), (second_r, dn_r) = ways_share(g)
        state["ra", g, h] = [
            send(part.at[h, xo, first, up], ra.at[h, 0, first_r, up_r], dev(dx=1)),
            send(part.at[h, xo, second, dn], ra.at[h, 1, second_r, dn_r], dev(dx=3)),
        ]

    def s2(g, h):
        lo, hi = GROUPS[g]
        group = pl.ds(lo, hi - lo)
        (first, up), (second, dn) = ways(g)
        (first_r, up_r), (second_r, dn_r) = ways_share(g)
        a, b = state.pop(("ra", g, h))
        a.wait_recv()
        part[h, xp, first, up, :] += ra[h, 0, first_r, up_r, :]
        a = send(part.at[h, xp, group, mine], rb.at[h, 0, group], dev(dx=1))
        b.wait_recv()
        part[h, xm, second, dn, :] += ra[h, 1, second_r, dn_r, :]
        b = send(part.at[h, xm, group, mine], rb.at[h, 1, group], dev(dx=3))
        state["rb", g, h] = [a, b]

    def s3(g, h):
        lo, hi = GROUPS[g]
        group = pl.ds(lo, hi - lo)
        arrived(("rb", g, h))
        rt[h, group] = part[h, x, group, mine, :] + rb[h, 0, group] + rb[h, 1, group]
        for i in away(g):
            state["at", i, h] = [send(rt.at[h, i], at.at[h, i], dev(dz=CHUNKS[i][0]))]

    def s4(g, h):
        arrived("mv")
        done(own_mv)
        for i in range(*GROUPS[g]):
            off, q = CHUNKS[i]
            arrived(("at", i, h))
            values = at[h, i] if off else rt[h, i]
            zs = (z + 4 - off) % 4
            half = zs // 2
            lanes = pl.ds(pl.multiple_of(zs % 2 * KN + h * HN, HN), HN)
            m, v, d = adam(m2[half, q, :, lanes], v2[half, q, :, lanes], values)
            m2[half, q, :, lanes] = m
            v2[half, q, :, lanes] = v
            if off:
                direc[h, i] = d
                state["d", i, h] = [send(direc.at[h, i], dd.at[h, x, i, mine], dev(dz=4 - off))]
            else:
                dd[h, x, i, mine, :] = d

    def s5(g, h):
        lo, hi = GROUPS[g]
        for i in away(g):
            arrived(("d", i, h))
        t = dd.at[h, x, pl.ds(lo, hi - lo), mine]
        state["ag", g, h] = [send(t, t, dev(dx=1)), send(t, t, dev(dx=3))]

    def s6(g, h):
        (first, up), (second, dn) = ways(g)
        a, b = state.pop(("ag", g, h))
        a.wait_recv()
        t = dd.at[h, xm, first, up]
        a = send(t, t, dev(dx=1))
        b.wait_recv()
        t = dd.at[h, xp, second, dn]
        b = send(t, t, dev(dx=3))
        state["ag2", g, h] = [a, b]

    def s7(g, h):
        lo, hi = GROUPS[g]
        arrived(("ag2", g, h))
        t = dd.at[h, :, pl.ds(lo, hi - lo), mine]
        state["dc", g, h] = [send(t, t, dev(dc=1))]

    def turn(p):
        ends = (0, 3, 7, 10, 14)
        basis_there(0, 2 * p + 2)

        @pl.loop(ends[p], ends[p + 1])
        def _(b):
            s = pl.ds(pl.multiple_of(b * 128, 128), 128)
            hi, lo = split(bt[s, :].T)
            bhi[:, s] = hi
            blo[:, s] = lo

    def split_direction(h, part_of):
        @pl.loop(0, 4)
        def _(n):
            @pl.loop(0, 4)
            def _(i):
                hi, lo = split(dd[h, n, part_of * 4 + i])
                s = pl.ds(pl.multiple_of(i * QJ, QJ), QJ)
                dhi[n, s, :] = hi
                dlo[n, s, :] = lo

    def product_two(h, part_of, n0, n1):
        rh = jnp.concatenate([dhi[n0], dhi[n1]], axis=1)
        rl = jnp.concatenate([dlo[n0], dlo[n1]], axis=1)
        k = slice(part_of * 2 * KJ, (part_of + 1) * 2 * KJ)

        @pl.loop(0, 2)
        def _(i):
            s = pl.ds(pl.multiple_of(i * (KI // 2), KI // 2), KI // 2)
            new = dot3(bhi[s, k], blo[s, k], rh, rl)
            if part_of:
                back[h, n0, s, :] += new[:, :HN]
                back[h, n1, s, :] += new[:, HN:]
            else:
                back[h, n0, s, :] = new[:, :HN]
                back[h, n1, s, :] = new[:, HN:]

    def directions_there(h, lo, hi):
        for g, (first, end) in enumerate(GROUPS):
            if lo <= first and end <= hi:
                arrived(("dc", g, h))

    def ya0(h):
        directions_there(h, 0, 4)
        split_direction(h, 0)
        product_two(h, 0, yo, yp)
        product_two(h, 0, ym, y)

    def y0(h):
        directions_there(h, 4, 8)
        split_direction(h, 1)
        product_two(h, 1, yo, yp)
        state["ya", h] = [
            send(back.at[h, yo, top], ya.at[h, 0], dev(dy=1)),
            send(back.at[h, yo, low], ya.at[h, 1], dev(dy=3)),
        ]

    def y0b(h):
        product_two(h, 1, ym, y)

    def y1(h):
        up, dn = state.pop(("ya", h))
        up.wait_recv()
        back[h, yp, top, :] += ya[h, 0]
        a = send(back.at[h, yp], yb.at[h, 0], dev(dy=1))
        dn.wait_recv()
        back[h, ym, low, :] += ya[h, 1]
        b = send(back.at[h, ym], yb.at[h, 1], dev(dy=3))
        state["yb", h] = [a, b]

    out_back_copies = []

    def y2(h):
        arrived(("yb", h))

        @pl.loop(0, KI // 128)
        def _(i):
            s = pl.ds(pl.multiple_of(i * 128, 128), 128)
            b = back[h, y, s, :] + yb[h, 0, s, :] + yb[h, 1, s, :]
            back[h, y, s, :] = b
            norm[1] += jnp.sum((b * b).reshape(16, 8, HN), axis=0)

        out_back_copies.append(local(back.at[h, y], out_back.at[:, pl.ds(h * HN, HN)]))

    order = (
        (plain,), (turn, 0), (gf, 0), (gs, 0), (gs2, 0), (s0, 0, 0), (bf, 0), (bf, 1), (s0, 1, 0), (turn, 1),
        (s1, 0, 0), (s1, 1, 0), (gf, 1), (gs, 1), (s2, 0, 0), (s2, 1, 0), (s3, 0, 0), (s4, 0, 0), (s5, 0, 0),
        (gs2, 1), (s0, 1, 1), (s0, 2, 0), (s6, 0, 0), (s3, 1, 0), (s0, 2, 1), (s1, 1, 1), (s7, 0, 0),
        (s1, 2, 0), (s0, 0, 1), (s1, 2, 1), (s2, 2, 0), (s2, 1, 1), (turn, 2), (s2, 2, 1), (s0, 3, 0),
        (s0, 4, 0), (s0, 4, 1), (s3, 2, 0), (s1, 3, 0), (s4, 1, 0), (s1, 4, 0), (s0, 3, 1), (s2, 3, 0),
        (s4, 2, 0), (s2, 4, 0), (s5, 1, 0), (s3, 1, 1), (s1, 3, 1), (s3, 3, 0), (s5, 2, 0), (s3, 4, 0),
        (s3, 2, 1), (s1, 4, 1), (turn, 3), (s6, 1, 0), (s2, 3, 1), (s4, 3, 0), (s1, 0, 1), (s4, 4, 0),
        (s4, 1, 1), (s2, 4, 1), (s6, 2, 0), (s7, 1, 0), (s5, 3, 0), (s4, 2, 1), (s3, 3, 1), (s5, 4, 0),
        (s2, 0, 1), (s5, 1, 1), (s3, 4, 1), (ya0, 0), (s6, 3, 0), (s7, 2, 0), (s6, 4, 0), (s4, 4, 1),
        (s4, 3, 1), (s3, 0, 1), (s6, 1, 1), (s7, 3, 0), (s4, 0, 1), (s7, 4, 0), (s5, 0, 1), (s5, 2, 1),
        (s5, 4, 1), (s7, 1, 1), (s5, 3, 1), (y0, 0), (s6, 0, 1), (y0b, 0), (s6, 2, 1), (s6, 3, 1), (s6, 4, 1),
        (s7, 0, 1), (s7, 2, 1), (y1, 0), (s7, 4, 1), (s7, 3, 1), (ya0, 1), (y0, 1), (y0b, 1), (y2, 0),
        (y1, 1), (y2, 1),
    )
    adams_left = 2 * len(GROUPS)
    out_rot, out_rot_own = [], []
    for stage, *step in order:
        stage(*step)
        if stage is s4:
            adams_left -= 1
            if adams_left == 0:
                for src, dst in ((m2, new_mom_rot), (v2, new_var_rot)):
                    out_rot.append(send(src.at[o], dst.at[:, mine], dev(dc=1)))
                    out_rot_own.append(local(src.at[c], dst.at[:, mine]))

    slot = 0
    for moves in norm_moves:
        copies = []
        for to in moves:
            copies.append((slot, send(norm, nrecv.at[slot], to)))
            slot += 1
        for _, copy in copies:
            started.pop()
            copy.wait()
        total = norm[...]
        for k, _ in copies:
            total += nrecv[k]
        norm[...] = total
    last = local(norm, out_norm)
    assert count[0] <= N_COPIES and count[1] <= 16

    for copy in started:
        copy.wait_send()
    for copy in out_rot:
        copy.wait_recv()
    for copy in out_rot_own + out_plain + out_back_copies:
        copy.wait()
    last.wait()


def finish(back, norm, *refs):
    sources, outs = (*refs[:4], back), (*refs[5:9], refs[4])
    held_rot, held, norm_v, in_sems, out_sems = refs[9:]
    norm_in = pltpu.make_async_copy(norm, norm_v, in_sems.at[10])
    norm_in.start()
    pieces = []
    for i in range(5):
        for h in range(2):
            if i < 2:
                src, dst, here = sources[i].at[h], outs[i].at[h], held_rot.at[i, h]
            else:
                s = pl.ds(h * KJ, KJ)
                src, dst, here = sources[i].at[s], outs[i].at[s], held.at[i - 2, h]
            pieces.append((pltpu.make_async_copy(src, here, in_sems.at[2 * i + h]),
                           pltpu.make_async_copy(here, dst, out_sems.at[2 * i + h])))
    for into, _ in pieces:
        into.start()
    norm_in.wait()
    graft = jnp.sqrt(jnp.sum(norm_v[0], keepdims=True))
    own = jnp.sqrt(jnp.sum(norm_v[1], keepdims=True))
    scale = graft / (own + 1e-06)
    for k, (into, out) in enumerate(pieces):
        into.wait()
        if k >= 8:
            held[2, k - 8] = held[2, k - 8] * scale
        out.start()
    for _, out in pieces:
        out.wait()


def per_device(grad, basis, mom_rot, var_rot, mom_plain, var_plain):
    plain = jax.ShapeDtypeStruct((KI, KN), F32)
    rot = jax.ShapeDtypeStruct((2, QJ, 2 * KN), F32)
    norms = jax.ShapeDtypeStruct((2, 8, HN), F32)
    scratch = [
        pltpu.VMEM((2, 4, KI, HN), F32),
        pltpu.VMEM((2, 4, KI, HN), BF16),
        pltpu.VMEM((2, 4, KI, HN), BF16),
        pltpu.VMEM((4 * KJ, KI), F32),
        pltpu.VMEM((KJ, KI), BF16),
        pltpu.VMEM((KJ, KI), BF16),
        pltpu.VMEM((KI, 4 * KJ), BF16),
        pltpu.VMEM((KI, 4 * KJ), BF16),
        pltpu.VMEM((2, 4, 8, QJ, HN), F32),
        pltpu.VMEM((2, 4, 8, CJ, HN), F32),
        pltpu.VMEM((2, 2, 8, CJ, HN), F32),
        pltpu.VMEM((2, 2, 8, CJ, HN), F32),
        pltpu.VMEM((2, 8, CJ, HN), F32),
        pltpu.VMEM((2, 8, CJ, HN), F32),
        pltpu.VMEM((2, 2, CJ, 2 * KN), F32),
        pltpu.VMEM((2, 2, CJ, 2 * KN), F32),
        pltpu.VMEM((2, 8, CJ, HN), F32),
        pltpu.VMEM((2, 4, 8, QJ, HN), F32),
        pltpu.VMEM((4, 2 * KJ, HN), BF16),
        pltpu.VMEM((4, 2 * KJ, HN), BF16),
        pltpu.VMEM((2, 4, KI, HN), F32),
        pltpu.VMEM((2, 2, KI // 2, HN), F32),
        pltpu.VMEM((2, 2, KI, HN), F32),
        pltpu.VMEM((KI, KN), F32),
        pltpu.VMEM((KI, KN), F32),
        pltpu.VMEM((2, 8, HN), F32),
        pltpu.VMEM((13, 2, 8, HN), F32),
        pltpu.SemaphoreType.DMA((N_COPIES,)),
        pltpu.SemaphoreType.DMA((N_COPIES,)),
        pltpu.SemaphoreType.DMA((16,)),
    ]
    anywhere = pl.BlockSpec(memory_space=pl.ANY)
    out = pl.pallas_call(
        kernel,
        out_shape=(plain, norms, rot, rot, plain, plain),
        in_specs=[anywhere] * 6,
        out_specs=[anywhere] * 6,
        scratch_shapes=scratch,
        compiler_params=pltpu.CompilerParams(
            collective_id=0, has_side_effects=True, vmem_limit_bytes=63 * 1024 * 1024
        ),
        cost_estimate=pl.CostEstimate(flops=20_000_000_000, bytes_accessed=12_000_000, transcendentals=0),
    )(grad, basis.T, mom_rot.reshape(2, QJ, 2 * KN), var_rot.reshape(2, QJ, 2 * KN), mom_plain, var_plain)
    update, new_mom_rot, new_var_rot, new_mom_plain, new_var_plain = pl.pallas_call(
        finish,
        out_shape=(plain, rot, rot, plain, plain),
        in_specs=[anywhere] * 6,
        out_specs=[anywhere] * 5,
        scratch_shapes=[
            pltpu.VMEM((2, 2, QJ, 2 * KN), F32),
            pltpu.VMEM((3, 2, KJ, KN), F32),
            pltpu.VMEM((2, 8, HN), F32),
            pltpu.SemaphoreType.DMA((11,)),
            pltpu.SemaphoreType.DMA((10,)),
        ],
        compiler_params=pltpu.CompilerParams(vmem_limit_bytes=60 * 1024 * 1024),
        cost_estimate=pl.CostEstimate(flops=1_000_000, bytes_accessed=9_000_000, transcendentals=0),
    )(*out)
    return (
        update,
        new_mom_rot.reshape(KJ, 2 * KN),
        new_var_rot.reshape(KJ, 2 * KN),
        new_mom_plain,
        new_var_plain,
    )


def solution(mesh):
    return jax.shard_map(
        per_device,
        mesh=mesh,
        in_specs=(
            P("rows", "cols"),
            P("rows", "cols"),
            P("cols", "rows"),
            P("cols", "rows"),
            P("rows", "cols"),
            P("rows", "cols"),
        ),
        out_specs=(
            P("rows", "cols"),
            P("cols", "rows"),
            P("cols", "rows"),
            P("rows", "cols"),
            P("rows", "cols"),
        ),
        check_vma=False,
    )
```

```python
import functools

import jax
import jax.numpy as jnp
from jax import lax
from jax.experimental import pallas as pl
from jax.experimental.pallas import tpu as pltpu
from jax.sharding import PartitionSpec as P

STEP = 10
BETA = 0.95
EPS = 1e-08
CORR = 1.0 - BETA**STEP

F32 = jnp.float32
BF16 = jnp.bfloat16

KI = 896
KJ = 448
KN = 256
QJ = KJ // 2
HN = KN // 2
CJ = QJ // 2
CHUNKS = ((0, 0), (0, 1), (1, 1), (3, 0), (1, 0), (3, 1), (2, 0), (2, 1))
GROUPS = ((0, 2), (2, 4), (4, 6), (6, 7), (7, 8))
N_COPIES = 192


def adam(moment, second, values):
    moment_new = BETA * moment + (1.0 - BETA) * values
    second_new = BETA * second + (1.0 - BETA) * values * values
    direction = moment_new / CORR / (jnp.sqrt(second_new / CORR) + EPS)
    return moment_new, second_new, direction


def split(a):
    hi = a.astype(BF16)
    lo = (a - hi.astype(F32)).astype(BF16)
    return hi, lo


def dot3(lh, ll, rh, rl):
    left = jnp.concatenate([lh, lh, ll], axis=1)
    right = jnp.concatenate([rh, rl, rh], axis=0)
    return jnp.dot(left, right, preferred_element_type=F32)


def kernel(
    grad, basis_t, mom_rot, var_rot, mom_plain, var_plain,
    out_back, out_norm, new_mom_rot, new_var_rot, new_mom_plain, new_var_plain,
    gg, ghi, glo, bt, lhi, llo, bhi, blo, part, rx, ra, rb, rt, at,
    m2, v2, direc, dd, dhi, dlo, back, ya, yb, mp, vp, norm, nrecv,
    ssem, rsem, lsem,
):
    rows = lax.axis_index("rows")
    cols = lax.axis_index("cols")
    x, c = rows // 2, rows % 2
    y, z = cols // 4, cols % 4
    o = 1 - c

    def dev(dx=0, dc=0, dy=0, dz=0):
        r = (x + dx) % 4 * 2 + (c + dc) % 2
        q = (y + dy) % 4 * 4 + (z + dz) % 4
        return (r, q)

    xp, xm, xo = (x + 1) % 4, (x + 3) % 4, (x + 2) % 4
    yp, ym, yo = (y + 1) % 4, (y + 3) % 4, (y + 2) % 4
    mine = pl.ds(pl.multiple_of(c * CJ, CJ), CJ)
    other = pl.ds(pl.multiple_of(o * CJ, CJ), CJ)
    top, low = pl.ds(0, KI // 2), pl.ds(KI // 2, KI // 2)

    norm_moves = (
        [dev(dc=1)] + [dev(dx=d, dc=e) for d in (1, 2, 3) for e in (0, 1)],
        [dev(dy=d) for d in (1, 2, 3)],
        [dev(dz=d) for d in (1, 2, 3)],
    )
    partners = [p for moves in norm_moves for p in moves]
    barrier = pltpu.get_barrier_semaphore()
    for p in partners:
        pl.semaphore_signal(barrier, inc=1, device_id=p, device_id_type=pl.DeviceIdType.MESH)
    pl.semaphore_wait(barrier, len(partners))

    count = [0, 0]
    started = []

    def send(src, dst, to):
        i = count[0]
        count[0] += 1
        copy = pltpu.make_async_remote_copy(
            src_ref=src, dst_ref=dst, send_sem=ssem.at[i], recv_sem=rsem.at[i],
            device_id=to, device_id_type=pl.DeviceIdType.MESH,
        )
        copy.start()
        started.append(copy)
        return copy

    def local(src, dst):
        i = count[1]
        count[1] += 1
        copy = pltpu.make_async_copy(src, dst, lsem.at[i])
        copy.start()
        return copy

    state = {}

    def arrived(key):
        for copy in state.pop(key, ()):
            copy.wait_recv()

    def chunk(i):
        return bt.at[pl.ds(i * QJ, QJ)]

    def gg_send(h):
        lanes = pl.ds(h * HN, HN)
        for way, first, second in ((1, top, low), (3, low, top)):
            state["g", h, way] = [send(grad.at[first, lanes], gg.at[h, y, first], dev(dy=way))]
            state["g_rest", h, way] = [send(grad.at[second, lanes], gg.at[h, y, second], dev(dy=way))]

    gg_send(0)
    halves = [basis_t.at[pl.ds(q * QJ, QJ)] for q in range(2)]
    state["b", 3] = [send(halves[0], chunk(3), dev(dz=1))]
    state["b", 2] = [send(halves[1], chunk(2), dev(dz=3))]
    state["b", 5] = [send(halves[1], chunk(5), dev(dz=1))]
    state["b", 4] = [send(halves[0], chunk(4), dev(dz=3))]
    own_g = [local(grad.at[:, pl.ds(h * HN, HN)], gg.at[h, y]) for h in range(2)]
    own_b = [local(basis_t, bt.at[pl.ds(0, KJ)])]
    own_plain = [local(mom_plain, mp), local(var_plain, vp)]
    state["mv"] = [send(src.at[:, other], dst.at[c], dev(dc=1)) for src, dst in ((mom_rot, m2), (var_rot, v2))]
    own_mv = [local(src.at[:, mine], dst.at[c]) for src, dst in ((mom_rot, m2), (var_rot, v2))]

    norm[...] = jnp.zeros_like(norm)
    out_plain = []

    def done(copies):
        while copies:
            copies.pop().wait()

    def plain():
        done(own_g)
        done(own_plain)

        @pl.loop(0, KI // 64)
        def _(i):
            s = pl.ds(pl.multiple_of(i * 64, 64), 64)
            for h in range(2):
                lanes = slice(h * HN, (h + 1) * HN)
                m, v, d = adam(mp[s, lanes], vp[s, lanes], gg[h, y, s, :])
                mp[s, lanes] = m
                vp[s, lanes] = v
                norm[0] += jnp.sum((d * d).reshape(8, 8, HN), axis=0)

        out_plain.append(local(mp, new_mom_plain))
        out_plain.append(local(vp, new_var_plain))

    def split_grad(h, n):
        @pl.loop(0, KI // 128)
        def _(i):
            s = pl.ds(pl.multiple_of(i * 128, 128), 128)
            hi, lo = split(gg[h, n, s, :])
            ghi[h, n, s, :] = hi
            glo[h, n, s, :] = lo

    def gf(h):
        arrived(("g", h, 1))
        a = send(gg.at[h, ym, top], gg.at[h, ym, top], dev(dy=1))
        arrived(("g", h, 3))
        b = send(gg.at[h, yp, low], gg.at[h, yp, low], dev(dy=3))
        state["g2", h] = [a, b]

    def gs(h):
        done(own_g)
        arrived(("g_rest", h, 1))
        arrived(("g_rest", h, 3))
        for n in (y, ym, yp):
            split_grad(h, n)

    def gs2(h):
        arrived(("g2", h))
        split_grad(h, yo)

    def bf(way):
        if way == 0:
            arrived(("b", 3))
            state["b", 6] = [send(chunk(3), chunk(6), dev(dz=1))]
        else:
            arrived(("b", 2))
            state["b", 7] = [send(chunk(2), chunk(7), dev(dz=3))]

    def basis_there(lo, hi):
        for i in range(lo, hi):
            if i < 2:
                done(own_b)
            arrived(("b", i))

    def away(g):
        return [i for i in range(*GROUPS[g]) if CHUNKS[i][0]]

    def ways(g):
        lo, hi = GROUPS[g]
        if hi - lo == 2:
            return [(pl.ds(lo, 1), mine), (pl.ds(lo + 1, 1), mine)]
        start = pl.multiple_of(c * CJ, CJ)
        return [
            (pl.ds(lo, 1), pl.ds(start, CJ // 2)),
            (pl.ds(lo, 1), pl.ds(pl.multiple_of(start + CJ // 2, CJ // 2), CJ // 2)),
        ]

    def ways_share(g):
        lo, hi = GROUPS[g]
        if hi - lo == 2:
            return [(pl.ds(lo, 1), pl.ds(0, CJ)), (pl.ds(lo + 1, 1), pl.ds(0, CJ))]
        return [(pl.ds(lo, 1), pl.ds(0, CJ // 2)), (pl.ds(lo, 1), pl.ds(CJ // 2, CJ // 2))]

    def s0(g, h):
        lo, hi = GROUPS[g]
        basis_there(lo, hi)
        size = (hi - lo) * QJ
        high, rest = split(bt[lo * QJ:hi * QJ, :])
        lhi[:size, :] = high
        llo[:size, :] = rest

        rh = jnp.concatenate([ghi[h, n] for n in range(4)], axis=1)
        rl = jnp.concatenate([glo[h, n] for n in range(4)], axis=1)
        new = dot3(lhi[:size, :], llo[:size, :], rh, rl)
        for n in range(4):
            for i in range(hi - lo):
                part[h, n, lo + i] = new[i * QJ:(i + 1) * QJ, n * HN:(n + 1) * HN]

        group = pl.ds(lo, hi - lo)
        state["x", g, h] = [send(part.at[h, :, group, other], rx.at[h, :, group], dev(dc=1))]

    def s1(g, h):
        lo, hi = GROUPS[g]
        arrived(("x", g, h))
        group = pl.ds(lo, hi - lo)
        for n in range(4):
            part[h, n, group, mine, :] += rx[h, n, group]
        (first, up), (second, dn) = ways(g)
        (first_r, up_r), (second_r, dn_r) = ways_share(g)
        state["ra", g, h] = [
            send(part.at[h, xo, first, up], ra.at[h, 0, first_r, up_r], dev(dx=1)),
            send(part.at[h, xo, second, dn], ra.at[h, 1, second_r, dn_r], dev(dx=3)),
        ]

    def s2(g, h):
        lo, hi = GROUPS[g]
        group = pl.ds(lo, hi - lo)
        (first, up), (second, dn) = ways(g)
        (first_r, up_r), (second_r, dn_r) = ways_share(g)
        a, b = state.pop(("ra", g, h))
        a.wait_recv()
        part[h, xp, first, up, :] += ra[h, 0, first_r, up_r, :]
        a = send(part.at[h, xp, group, mine], rb.at[h, 0, group], dev(dx=1))
        b.wait_recv()
        part[h, xm, second, dn, :] += ra[h, 1, second_r, dn_r, :]
        b = send(part.at[h, xm, group, mine], rb.at[h, 1, group], dev(dx=3))
        state["rb", g, h] = [a, b]

    def s3(g, h):
        lo, hi = GROUPS[g]
        group = pl.ds(lo, hi - lo)
        arrived(("rb", g, h))
        rt[h, group] = part[h, x, group, mine, :] + rb[h, 0, group] + rb[h, 1, group]
        for i in away(g):
            state["at", i, h] = [send(rt.at[h, i], at.at[h, i], dev(dz=CHUNKS[i][0]))]

    def s4(g, h):
        arrived("mv")
        done(own_mv)
        for i in range(*GROUPS[g]):
            off, q = CHUNKS[i]
            arrived(("at", i, h))
            values = at[h, i] if off else rt[h, i]
            zs = (z + 4 - off) % 4
            half = zs // 2
            lanes = pl.ds(pl.multiple_of(zs % 2 * KN + h * HN, HN), HN)
            m, v, d = adam(m2[half, q, :, lanes], v2[half, q, :, lanes], values)
            m2[half, q, :, lanes] = m
            v2[half, q, :, lanes] = v
            if off:
                direc[h, i] = d
                state["d", i, h] = [send(direc.at[h, i], dd.at[h, x, i, mine], dev(dz=4 - off))]
            else:
                dd[h, x, i, mine, :] = d

    def s5(g, h):
        lo, hi = GROUPS[g]
        for i in away(g):
            arrived(("d", i, h))
        t = dd.at[h, x, pl.ds(lo, hi - lo), mine]
        state["ag", g, h] = [send(t, t, dev(dx=1)), send(t, t, dev(dx=3))]

    def s6(g, h):
        (first, up), (second, dn) = ways(g)
        a, b = state.pop(("ag", g, h))
        a.wait_recv()
        t = dd.at[h, xm, first, up]
        a = send(t, t, dev(dx=1))
        b.wait_recv()
        t = dd.at[h, xp, second, dn]
        b = send(t, t, dev(dx=3))
        state["ag2", g, h] = [a, b]

    def s7(g, h):
        lo, hi = GROUPS[g]
        arrived(("ag2", g, h))
        t = dd.at[h, :, pl.ds(lo, hi - lo), mine]
        state["dc", g, h] = [send(t, t, dev(dc=1))]

    def turn(p):
        ends = (0, 3, 7, 10, 14)
        basis_there(0, 2 * p + 2)

        @pl.loop(ends[p], ends[p + 1])
        def _(b):
            s = pl.ds(pl.multiple_of(b * 128, 128), 128)
            hi, lo = split(bt[s, :].T)
            bhi[:, s] = hi
            blo[:, s] = lo

    def split_direction(h, part_of):
        @pl.loop(0, 4)
        def _(n):
            @pl.loop(0, 4)
            def _(i):
                hi, lo = split(dd[h, n, part_of * 4 + i])
                s = pl.ds(pl.multiple_of(i * QJ, QJ), QJ)
                dhi[n, s, :] = hi
                dlo[n, s, :] = lo

    def product_two(h, part_of, s):
        rh = jnp.concatenate([dhi[n] for n in range(4)], axis=1)
        rl = jnp.concatenate([dlo[n] for n in range(4)], axis=1)
        k = slice(part_of * 2 * KJ, (part_of + 1) * 2 * KJ)
        new = dot3(bhi[s, k], blo[s, k], rh, rl)
        for n in range(4):
            tile = new[:, n * HN:(n + 1) * HN]
            back[h, n, s, :] = back[h, n, s, :] + tile if part_of else tile

    def directions_there(h, lo, hi):
        for g, (first, end) in enumerate(GROUPS):
            if lo <= first and end <= hi:
                arrived(("dc", g, h))

    def ya0(h):
        directions_there(h, 0, 4)
        split_direction(h, 0)
        product_two(h, 0, top)
        product_two(h, 0, low)

    def y0(h):
        directions_there(h, 4, 8)
        split_direction(h, 1)
        product_two(h, 1, top)
        state["ya", h] = [send(back.at[h, yo, top], ya.at[h, 0], dev(dy=1))]
        state["yb", h] = [send(back.at[h, ym, top], yb.at[h, 1, top], dev(dy=3))]

    def y0b(h):
        product_two(h, 1, low)
        state["ya", h].append(send(back.at[h, yo, low], ya.at[h, 1], dev(dy=3)))
        state["yb", h].append(send(back.at[h, yp, low], yb.at[h, 0, low], dev(dy=1)))

    def y1(h):
        up, dn = state.pop(("ya", h))
        up.wait_recv()
        back[h, yp, top, :] += ya[h, 0]
        state["yb", h].append(send(back.at[h, yp, top], yb.at[h, 0, top], dev(dy=1)))
        dn.wait_recv()
        back[h, ym, low, :] += ya[h, 1]
        state["yb", h].append(send(back.at[h, ym, low], yb.at[h, 1, low], dev(dy=3)))

    out_back_copies = []

    def y2(h):
        arrived(("yb", h))

        @pl.loop(0, KI // 128)
        def _(i):
            s = pl.ds(pl.multiple_of(i * 128, 128), 128)
            b = back[h, y, s, :] + yb[h, 0, s, :] + yb[h, 1, s, :]
            back[h, y, s, :] = b
            norm[1] += jnp.sum((b * b).reshape(16, 8, HN), axis=0)

        out_back_copies.append(local(back.at[h, y], out_back.at[:, pl.ds(h * HN, HN)]))

    order = (
        (turn, 0), (plain,), (gf, 0), (gs, 0), (gg_send, 1), (gs2, 0), (s0, 0, 0), (s0, 1, 0), (gf, 1),
        (s1, 0, 0), (bf, 0), (turn, 1), (s2, 0, 0), (s1, 1, 0), (gs, 1), (bf, 1), (gs2, 1), (s0, 1, 1),
        (s0, 0, 1), (s2, 1, 0), (s3, 0, 0), (s4, 0, 0), (s5, 0, 0), (s1, 1, 1), (s0, 2, 0), (s1, 0, 1),
        (s0, 2, 1), (s2, 1, 1), (s1, 2, 0), (s2, 0, 1), (s3, 1, 0), (turn, 2), (s1, 2, 1), (s2, 2, 0),
        (s6, 0, 0), (s3, 1, 1), (s0, 4, 0), (s2, 2, 1), (s0, 3, 0), (s0, 3, 1), (s1, 4, 0), (s3, 2, 0),
        (s0, 4, 1), (s1, 3, 0), (s4, 1, 0), (s2, 4, 0), (s1, 3, 1), (s3, 2, 1), (s2, 3, 0), (s4, 2, 0),
        (s1, 4, 1), (s5, 1, 0), (s3, 4, 0), (s3, 0, 1), (s2, 3, 1), (s3, 3, 0), (s7, 0, 0), (s5, 2, 0),
        (s4, 4, 0), (turn, 3), (s6, 1, 0), (s4, 3, 0), (s3, 3, 1), (s2, 4, 1), (s4, 0, 1), (s4, 2, 1),
        (s5, 4, 0), (s4, 1, 1), (s5, 3, 0), (s7, 1, 0), (s3, 4, 1), (s6, 2, 0), (s4, 3, 1), (s6, 4, 0),
        (s6, 3, 0), (s5, 0, 1), (s5, 2, 1), (s7, 2, 0), (s5, 1, 1), (s7, 4, 0), (s4, 4, 1), (s7, 3, 0),
        (ya0, 0), (s6, 0, 1), (s5, 4, 1), (y0, 0), (s6, 1, 1), (s7, 0, 1), (s5, 3, 1), (s6, 2, 1), (y0b, 0),
        (s7, 1, 1), (s6, 4, 1), (s6, 3, 1), (s7, 2, 1), (s7, 4, 1), (y1, 0), (s7, 3, 1), (ya0, 1), (y0, 1),
        (y0b, 1), (y1, 1), (y2, 0), (y2, 1),
    )
    adams_left = 2 * len(GROUPS)
    out_rot, out_rot_own = [], []
    for stage, *step in order:
        stage(*step)
        if stage is s4:
            adams_left -= 1
            if adams_left == 0:
                for src, dst in ((m2, new_mom_rot), (v2, new_var_rot)):
                    out_rot.append(send(src.at[o], dst.at[:, mine], dev(dc=1)))
                    out_rot_own.append(local(src.at[c], dst.at[:, mine]))

    slot = 0
    for moves in norm_moves:
        copies = []
        for to in moves:
            copies.append((slot, send(norm, nrecv.at[slot], to)))
            slot += 1
        for _, copy in copies:
            started.pop()
            copy.wait()
        total = norm[...]
        for k, _ in copies:
            total += nrecv[k]
        norm[...] = total
    last = local(norm, out_norm)
    assert count[0] <= N_COPIES and count[1] <= 16

    for copy in started:
        copy.wait_send()
    for copy in out_rot:
        copy.wait_recv()
    for copy in out_rot_own + out_plain + out_back_copies:
        copy.wait()
    last.wait()


def finish(back, norm, *refs):
    sources, outs = (*refs[:4], back), (*refs[5:9], refs[4])
    held_rot, held, norm_v, in_sems, out_sems = refs[9:]
    norm_in = pltpu.make_async_copy(norm, norm_v, in_sems.at[10])
    norm_in.start()
    pieces = []
    for i in range(5):
        for h in range(2):
            if i < 2:
                src, dst, here = sources[i].at[h], outs[i].at[h], held_rot.at[i, h]
            else:
                s = pl.ds(h * KJ, KJ)
                src, dst, here = sources[i].at[s], outs[i].at[s], held.at[i - 2, h]
            pieces.append((pltpu.make_async_copy(src, here, in_sems.at[2 * i + h]),
                           pltpu.make_async_copy(here, dst, out_sems.at[2 * i + h])))
    for into, _ in pieces:
        into.start()
    norm_in.wait()
    graft = jnp.sqrt(jnp.sum(norm_v[0], keepdims=True))
    own = jnp.sqrt(jnp.sum(norm_v[1], keepdims=True))
    scale = graft / (own + 1e-06)
    for k, (into, out) in enumerate(pieces):
        into.wait()
        if k >= 8:
            held[2, k - 8] = held[2, k - 8] * scale
        out.start()
    for _, out in pieces:
        out.wait()


def per_device(grad, basis, mom_rot, var_rot, mom_plain, var_plain):
    plain = jax.ShapeDtypeStruct((KI, KN), F32)
    rot = jax.ShapeDtypeStruct((2, QJ, 2 * KN), F32)
    norms = jax.ShapeDtypeStruct((2, 8, HN), F32)
    scratch = [
        pltpu.VMEM((2, 4, KI, HN), F32),
        pltpu.VMEM((2, 4, KI, HN), BF16),
        pltpu.VMEM((2, 4, KI, HN), BF16),
        pltpu.VMEM((4 * KJ, KI), F32),
        pltpu.VMEM((KJ, KI), BF16),
        pltpu.VMEM((KJ, KI), BF16),
        pltpu.VMEM((KI, 4 * KJ), BF16),
        pltpu.VMEM((KI, 4 * KJ), BF16),
        pltpu.VMEM((2, 4, 8, QJ, HN), F32),
        pltpu.VMEM((2, 4, 8, CJ, HN), F32),
        pltpu.VMEM((2, 2, 8, CJ, HN), F32),
        pltpu.VMEM((2, 2, 8, CJ, HN), F32),
        pltpu.VMEM((2, 8, CJ, HN), F32),
        pltpu.VMEM((2, 8, CJ, HN), F32),
        pltpu.VMEM((2, 2, CJ, 2 * KN), F32),
        pltpu.VMEM((2, 2, CJ, 2 * KN), F32),
        pltpu.VMEM((2, 8, CJ, HN), F32),
        pltpu.VMEM((2, 4, 8, QJ, HN), F32),
        pltpu.VMEM((4, 2 * KJ, HN), BF16),
        pltpu.VMEM((4, 2 * KJ, HN), BF16),
        pltpu.VMEM((2, 4, KI, HN), F32),
        pltpu.VMEM((2, 2, KI // 2, HN), F32),
        pltpu.VMEM((2, 2, KI, HN), F32),
        pltpu.VMEM((KI, KN), F32),
        pltpu.VMEM((KI, KN), F32),
        pltpu.VMEM((2, 8, HN), F32),
        pltpu.VMEM((13, 2, 8, HN), F32),
        pltpu.SemaphoreType.DMA((N_COPIES,)),
        pltpu.SemaphoreType.DMA((N_COPIES,)),
        pltpu.SemaphoreType.DMA((16,)),
    ]
    anywhere = pl.BlockSpec(memory_space=pl.ANY)
    out = pl.pallas_call(
        kernel,
        out_shape=(plain, norms, rot, rot, plain, plain),
        in_specs=[anywhere] * 6,
        out_specs=[anywhere] * 6,
        scratch_shapes=scratch,
        compiler_params=pltpu.CompilerParams(
            collective_id=0, has_side_effects=True, vmem_limit_bytes=63 * 1024 * 1024
        ),
        cost_estimate=pl.CostEstimate(flops=20_000_000_000, bytes_accessed=12_000_000, transcendentals=0),
    )(grad, basis.T, mom_rot.reshape(2, QJ, 2 * KN), var_rot.reshape(2, QJ, 2 * KN), mom_plain, var_plain)
    update, new_mom_rot, new_var_rot, new_mom_plain, new_var_plain = pl.pallas_call(
        finish,
        out_shape=(plain, rot, rot, plain, plain),
        in_specs=[anywhere] * 6,
        out_specs=[anywhere] * 5,
        scratch_shapes=[
            pltpu.VMEM((2, 2, QJ, 2 * KN), F32),
            pltpu.VMEM((3, 2, KJ, KN), F32),
            pltpu.VMEM((2, 8, HN), F32),
            pltpu.SemaphoreType.DMA((11,)),
            pltpu.SemaphoreType.DMA((10,)),
        ],
        compiler_params=pltpu.CompilerParams(vmem_limit_bytes=60 * 1024 * 1024),
        cost_estimate=pl.CostEstimate(flops=1_000_000, bytes_accessed=9_000_000, transcendentals=0),
    )(*out)
    return (
        update,
        new_mom_rot.reshape(KJ, 2 * KN),
        new_var_rot.reshape(KJ, 2 * KN),
        new_mom_plain,
        new_var_plain,
    )


def solution(mesh):
    return jax.shard_map(
        per_device,
        mesh=mesh,
        in_specs=(
            P("rows", "cols"),
            P("rows", "cols"),
            P("cols", "rows"),
            P("cols", "rows"),
            P("rows", "cols"),
            P("rows", "cols"),
        ),
        out_specs=(
            P("rows", "cols"),
            P("cols", "rows"),
            P("cols", "rows"),
            P("rows", "cols"),
            P("rows", "cols"),
        ),
        check_vma=False,
    )
```

```python
import functools

import jax
import jax.numpy as jnp
from jax import lax
from jax.experimental import pallas as pl
from jax.experimental.pallas import tpu as pltpu
from jax.sharding import PartitionSpec as P

STEP = 10
BETA = 0.95
EPS = 1e-08
CORR = 1.0 - BETA**STEP

F32 = jnp.float32
BF16 = jnp.bfloat16

KI = 896
KJ = 448
KN = 256
QJ = KJ // 2
HN = KN // 2
CJ = QJ // 2
CHUNKS = ((0, 0), (0, 1), (1, 1), (3, 0), (1, 0), (3, 1), (2, 0), (2, 1))
GROUPS = ((0, 2), (2, 4), (4, 5), (5, 6), (6, 7), (7, 8))
N_COPIES = 224


def adam(moment, second, values):
    moment_new = BETA * moment + (1.0 - BETA) * values
    second_new = BETA * second + (1.0 - BETA) * values * values
    direction = moment_new / CORR / (jnp.sqrt(second_new / CORR) + EPS)
    return moment_new, second_new, direction


def split(a):
    hi = a.astype(BF16)
    lo = (a - hi.astype(F32)).astype(BF16)
    return hi, lo


def dot3(lh, ll, rh, rl):
    left = jnp.concatenate([lh, lh, ll], axis=1)
    right = jnp.concatenate([rh, rl, rh], axis=0)
    return jnp.dot(left, right, preferred_element_type=F32)


def kernel(
    grad, basis_t, mom_rot, var_rot, mom_plain, var_plain,
    out_back, out_norm, new_mom_rot, new_var_rot, new_mom_plain, new_var_plain,
    gg, ghi, glo, bt, lhi, llo, bhi, blo, part, rx, ra, rb, rt, at,
    m2, v2, direc, dd, dhi, dlo, back, ya, yb, mp, vp, norm, nrecv,
    ssem, rsem, lsem,
):
    rows = lax.axis_index("rows")
    cols = lax.axis_index("cols")
    x, c = rows // 2, rows % 2
    y, z = cols // 4, cols % 4
    o = 1 - c

    def dev(dx=0, dc=0, dy=0, dz=0):
        r = (x + dx) % 4 * 2 + (c + dc) % 2
        q = (y + dy) % 4 * 4 + (z + dz) % 4
        return (r, q)

    xp, xm, xo = (x + 1) % 4, (x + 3) % 4, (x + 2) % 4
    yp, ym, yo = (y + 1) % 4, (y + 3) % 4, (y + 2) % 4
    mine = pl.ds(pl.multiple_of(c * CJ, CJ), CJ)
    other = pl.ds(pl.multiple_of(o * CJ, CJ), CJ)
    top, low = pl.ds(0, KI // 2), pl.ds(KI // 2, KI // 2)

    norm_moves = (
        [dev(dc=1)] + [dev(dx=d, dc=e) for d in (1, 2, 3) for e in (0, 1)],
        [dev(dy=d) for d in (1, 2, 3)],
        [dev(dz=d) for d in (1, 2, 3)],
    )
    partners = [p for moves in norm_moves for p in moves]
    barrier = pltpu.get_barrier_semaphore()
    for p in partners:
        pl.semaphore_signal(barrier, inc=1, device_id=p, device_id_type=pl.DeviceIdType.MESH)
    pl.semaphore_wait(barrier, len(partners))

    count = [0, 0]
    started = []

    def send(src, dst, to):
        i = count[0]
        count[0] += 1
        copy = pltpu.make_async_remote_copy(
            src_ref=src, dst_ref=dst, send_sem=ssem.at[i], recv_sem=rsem.at[i],
            device_id=to, device_id_type=pl.DeviceIdType.MESH,
        )
        copy.start()
        started.append(copy)
        return copy

    def local(src, dst):
        i = count[1]
        count[1] += 1
        copy = pltpu.make_async_copy(src, dst, lsem.at[i])
        copy.start()
        return copy

    state = {}

    def arrived(key):
        for copy in state.pop(key, ()):
            copy.wait_recv()

    def chunk(i):
        return bt.at[pl.ds(i * QJ, QJ)]

    def gg_send(h):
        lanes = pl.ds(h * HN, HN)
        for way, first, second in ((1, top, low), (3, low, top)):
            state["g", h, way] = [send(grad.at[first, lanes], gg.at[h, y, first], dev(dy=way))]
            state["g_rest", h, way] = [send(grad.at[second, lanes], gg.at[h, y, second], dev(dy=way))]

    gg_send(0)
    halves = [basis_t.at[pl.ds(q * QJ, QJ)] for q in range(2)]
    state["b", 3] = [send(halves[0], chunk(3), dev(dz=1))]
    state["b", 2] = [send(halves[1], chunk(2), dev(dz=3))]
    own_g = [local(grad.at[:, pl.ds(h * HN, HN)], gg.at[h, y]) for h in range(2)]
    own_b = [local(basis_t, bt.at[pl.ds(0, KJ)])]
    own_plain = [local(mom_plain, mp), local(var_plain, vp)]
    state["mv"] = [send(src.at[:, other], dst.at[c], dev(dc=1)) for src, dst in ((mom_rot, m2), (var_rot, v2))]
    own_mv = [local(src.at[:, mine], dst.at[c]) for src, dst in ((mom_rot, m2), (var_rot, v2))]

    norm[...] = jnp.zeros_like(norm)
    out_plain = []

    def done(copies):
        while copies:
            copies.pop().wait()

    def plain():
        done(own_g)
        done(own_plain)

        @pl.loop(0, KI // 64)
        def _(i):
            s = pl.ds(pl.multiple_of(i * 64, 64), 64)
            for h in range(2):
                lanes = slice(h * HN, (h + 1) * HN)
                m, v, d = adam(mp[s, lanes], vp[s, lanes], gg[h, y, s, :])
                mp[s, lanes] = m
                vp[s, lanes] = v
                norm[0] += jnp.sum((d * d).reshape(8, 8, HN), axis=0)

        out_plain.append(local(mp, new_mom_plain))
        out_plain.append(local(vp, new_var_plain))

    def split_grad(h, n):
        @pl.loop(0, KI // 128)
        def _(i):
            s = pl.ds(pl.multiple_of(i * 128, 128), 128)
            hi, lo = split(gg[h, n, s, :])
            ghi[h, n, s, :] = hi
            glo[h, n, s, :] = lo

    def gf(h):
        arrived(("g", h, 1))
        a = send(gg.at[h, ym, top], gg.at[h, ym, top], dev(dy=1))
        arrived(("g", h, 3))
        b = send(gg.at[h, yp, low], gg.at[h, yp, low], dev(dy=3))
        state["g2", h] = [a, b]

    def gs(h):
        done(own_g)
        arrived(("g_rest", h, 1))
        arrived(("g_rest", h, 3))
        for n in (y, ym, yp):
            split_grad(h, n)

    def gs2(h):
        arrived(("g2", h))
        split_grad(h, yo)

    def bf(way):
        if way == 0:
            arrived(("b", 3))
            state["b", 6] = [send(chunk(3), chunk(6), dev(dz=1))]
        else:
            arrived(("b", 2))
            state["b", 7] = [send(chunk(2), chunk(7), dev(dz=3))]

    def bo(way):
        if way == 0:
            state["b", 5] = [send(halves[1], chunk(5), dev(dz=1))]
        else:
            state["b", 4] = [send(halves[0], chunk(4), dev(dz=3))]

    def basis_there(lo, hi):
        for i in range(lo, hi):
            if i < 2:
                done(own_b)
            arrived(("b", i))

    def away(g):
        return [i for i in range(*GROUPS[g]) if CHUNKS[i][0]]

    def ways(g):
        lo, hi = GROUPS[g]
        if hi - lo == 2:
            return [(pl.ds(lo, 1), mine), (pl.ds(lo + 1, 1), mine)]
        start = pl.multiple_of(c * CJ, CJ)
        return [
            (pl.ds(lo, 1), pl.ds(start, CJ // 2)),
            (pl.ds(lo, 1), pl.ds(pl.multiple_of(start + CJ // 2, CJ // 2), CJ // 2)),
        ]

    def ways_share(g):
        lo, hi = GROUPS[g]
        if hi - lo == 2:
            return [(pl.ds(lo, 1), pl.ds(0, CJ)), (pl.ds(lo + 1, 1), pl.ds(0, CJ))]
        return [(pl.ds(lo, 1), pl.ds(0, CJ // 2)), (pl.ds(lo, 1), pl.ds(CJ // 2, CJ // 2))]

    def s0(g, h):
        lo, hi = GROUPS[g]
        basis_there(lo, hi)
        size = (hi - lo) * QJ
        high, rest = split(bt[lo * QJ:hi * QJ, :])
        lhi[:size, :] = high
        llo[:size, :] = rest

        rh = jnp.concatenate([ghi[h, n] for n in range(4)], axis=1)
        rl = jnp.concatenate([glo[h, n] for n in range(4)], axis=1)
        new = dot3(lhi[:size, :], llo[:size, :], rh, rl)
        for n in range(4):
            for i in range(hi - lo):
                part[h, n, lo + i] = new[i * QJ:(i + 1) * QJ, n * HN:(n + 1) * HN]

        group = pl.ds(lo, hi - lo)
        state["x", g, h] = [send(part.at[h, :, group, other], rx.at[h, :, group], dev(dc=1))]

    def s1(g, h):
        lo, hi = GROUPS[g]
        arrived(("x", g, h))
        group = pl.ds(lo, hi - lo)
        for n in range(4):
            part[h, n, group, mine, :] += rx[h, n, group]
        (first, up), (second, dn) = ways(g)
        (first_r, up_r), (second_r, dn_r) = ways_share(g)
        state["ra", g, h] = [
            send(part.at[h, xo, first, up], ra.at[h, 0, first_r, up_r], dev(dx=1)),
            send(part.at[h, xo, second, dn], ra.at[h, 1, second_r, dn_r], dev(dx=3)),
        ]

    def s2(g, h):
        lo, hi = GROUPS[g]
        group = pl.ds(lo, hi - lo)
        (first, up), (second, dn) = ways(g)
        (first_r, up_r), (second_r, dn_r) = ways_share(g)
        a, b = state.pop(("ra", g, h))
        a.wait_recv()
        part[h, xp, first, up, :] += ra[h, 0, first_r, up_r, :]
        a = send(part.at[h, xp, group, mine], rb.at[h, 0, group], dev(dx=1))
        b.wait_recv()
        part[h, xm, second, dn, :] += ra[h, 1, second_r, dn_r, :]
        b = send(part.at[h, xm, group, mine], rb.at[h, 1, group], dev(dx=3))
        state["rb", g, h] = [a, b]

    def s3(g, h):
        lo, hi = GROUPS[g]
        group = pl.ds(lo, hi - lo)
        arrived(("rb", g, h))
        rt[h, group] = part[h, x, group, mine, :] + rb[h, 0, group] + rb[h, 1, group]
        for i in away(g):
            state["at", i, h] = [send(rt.at[h, i], at.at[h, i], dev(dz=CHUNKS[i][0]))]

    def s4(g, h):
        arrived("mv")
        done(own_mv)
        for i in range(*GROUPS[g]):
            off, q = CHUNKS[i]
            arrived(("at", i, h))
            values = at[h, i] if off else rt[h, i]
            zs = (z + 4 - off) % 4
            half = zs // 2
            lanes = pl.ds(pl.multiple_of(zs % 2 * KN + h * HN, HN), HN)
            m, v, d = adam(m2[half, q, :, lanes], v2[half, q, :, lanes], values)
            m2[half, q, :, lanes] = m
            v2[half, q, :, lanes] = v
            if off:
                direc[h, i] = d
                state["d", i, h] = [send(direc.at[h, i], dd.at[h, 0, i, mine], dev(dz=4 - off))]
            else:
                dd[h, 0, i, mine, :] = d

    def s5(g, h):
        lo, hi = GROUPS[g]
        group = pl.ds(lo, hi - lo)
        for i in away(g):
            arrived(("d", i, h))
        t = dd.at[h, 0, group, mine]
        state["ag", g, h] = [
            send(t, dd.at[h, 2, group, mine], dev(dx=1)),
            send(t, dd.at[h, 1, group, mine], dev(dx=3)),
        ]

    def s6(g, h):
        lo, hi = GROUPS[g]
        (first, up), (second, dn) = ways(g)
        a, b = state.pop(("ag", g, h))
        a.wait_recv()
        a = send(dd.at[h, 2, first, up], dd.at[h, 3, first, up], dev(dx=1))
        b.wait_recv()
        b = send(dd.at[h, 1, second, dn], dd.at[h, 3, second, dn], dev(dx=3))
        state["ag2", g, h] = [a, b]
        t = dd.at[h, pl.ds(0, 3), pl.ds(lo, hi - lo), mine]
        state["dc", g, h] = [send(t, t, dev(dc=1))]

    def s7(g, h):
        lo, hi = GROUPS[g]
        arrived(("ag2", g, h))
        t = dd.at[h, 3, pl.ds(lo, hi - lo), mine]
        state["dc", g, h].append(send(t, t, dev(dc=1)))

    def turn(p):
        ends = (0, 3, 7, 10, 14)
        basis_there(0, 2 * p + 2)

        @pl.loop(ends[p], ends[p + 1])
        def _(b):
            s = pl.ds(pl.multiple_of(b * 128, 128), 128)
            hi, lo = split(bt[s, :].T)
            bhi[:, s] = hi
            blo[:, s] = lo

    def split_direction(h, part_of):
        @pl.loop(0, 4)
        def _(n):
            d = (n + 4 - x) % 4
            place = d + d // 2 * (1 - 2 * (d % 2))

            @pl.loop(0, 4)
            def _(i):
                hi, lo = split(dd[h, place, part_of * 4 + i])
                s = pl.ds(pl.multiple_of(i * QJ, QJ), QJ)
                dhi[n, s, :] = hi
                dlo[n, s, :] = lo

    def product_two(h, part_of, s):
        rh = jnp.concatenate([dhi[n] for n in range(4)], axis=1)
        rl = jnp.concatenate([dlo[n] for n in range(4)], axis=1)
        k = slice(part_of * 2 * KJ, (part_of + 1) * 2 * KJ)
        new = dot3(bhi[s, k], blo[s, k], rh, rl)
        for n in range(4):
            tile = new[:, n * HN:(n + 1) * HN]
            back[h, n, s, :] = back[h, n, s, :] + tile if part_of else tile

    def directions_there(h, lo, hi):
        for g, (first, end) in enumerate(GROUPS):
            if lo <= first and end <= hi:
                arrived(("dc", g, h))

    def ya0(h):
        directions_there(h, 0, 4)
        split_direction(h, 0)
        product_two(h, 0, top)
        product_two(h, 0, low)

    def y0(h):
        directions_there(h, 4, 8)
        split_direction(h, 1)
        product_two(h, 1, top)
        state["ya", h] = [send(back.at[h, yo, top], ya.at[h, 0], dev(dy=1))]
        state["yb", h] = [send(back.at[h, ym, top], yb.at[h, 1, top], dev(dy=3))]

    def y0b(h):
        product_two(h, 1, low)
        state["ya", h].append(send(back.at[h, yo, low], ya.at[h, 1], dev(dy=3)))
        state["yb", h].append(send(back.at[h, yp, low], yb.at[h, 0, low], dev(dy=1)))

    def y1(h):
        up, dn = state.pop(("ya", h))
        up.wait_recv()
        back[h, yp, top, :] += ya[h, 0]
        state["yb", h].append(send(back.at[h, yp, top], yb.at[h, 0, top], dev(dy=1)))
        dn.wait_recv()
        back[h, ym, low, :] += ya[h, 1]
        state["yb", h].append(send(back.at[h, ym, low], yb.at[h, 1, low], dev(dy=3)))

    out_back_copies = []

    def y2(h):
        arrived(("yb", h))

        @pl.loop(0, KI // 128)
        def _(i):
            s = pl.ds(pl.multiple_of(i * 128, 128), 128)
            b = back[h, y, s, :] + yb[h, 0, s, :] + yb[h, 1, s, :]
            back[h, y, s, :] = b
            norm[1] += jnp.sum((b * b).reshape(16, 8, HN), axis=0)

        out_back_copies.append(local(back.at[h, y], out_back.at[:, pl.ds(h * HN, HN)]))

    order = (
        (turn, 0), (gf, 0), (gs, 0), (bo, 1), (bo, 0), (plain,), (gg_send, 1), (gs2, 0), (s0, 0, 0),
        (s1, 0, 0), (s0, 1, 0), (gf, 1), (s2, 0, 0), (turn, 1), (bf, 1), (gs, 1), (s3, 0, 0), (s4, 0, 0),
        (s1, 1, 0), (s5, 0, 0), (gs2, 1), (bf, 0), (s0, 1, 1), (s2, 1, 0), (s0, 3, 0), (s0, 0, 1), (s1, 3, 0),
        (s1, 1, 1), (s6, 0, 0), (s0, 3, 1), (s2, 3, 0), (s1, 0, 1), (s0, 2, 1), (s2, 1, 1), (s0, 2, 0),
        (s1, 3, 1), (s1, 2, 1), (turn, 2), (s3, 3, 0), (s1, 2, 0), (s7, 0, 0), (s2, 3, 1), (s2, 2, 1),
        (s2, 0, 1), (s2, 2, 0), (s3, 1, 1), (s3, 1, 0), (s0, 4, 0), (s4, 3, 0), (s0, 5, 0), (s3, 2, 1),
        (s1, 4, 0), (s3, 2, 0), (s5, 3, 0), (s4, 1, 0), (s1, 5, 0), (s2, 4, 0), (s0, 5, 1), (s6, 3, 0),
        (s2, 5, 0), (s4, 2, 0), (s5, 1, 0), (s3, 4, 0), (s3, 0, 1), (s0, 4, 1), (s3, 5, 0), (s1, 5, 1),
        (s5, 2, 0), (s7, 3, 0), (s3, 3, 1), (s4, 4, 0), (s1, 4, 1), (s6, 1, 0), (s4, 2, 1), (s2, 5, 1),
        (s4, 5, 0), (s4, 0, 1), (s6, 2, 0), (s4, 1, 1), (s5, 4, 0), (turn, 3), (s4, 3, 1), (s5, 5, 0),
        (s7, 1, 0), (s3, 5, 1), (s5, 1, 1), (s2, 4, 1), (s6, 4, 0), (s7, 2, 0), (s6, 5, 0), (s5, 0, 1),
        (ya0, 0), (s7, 4, 0), (s7, 5, 0), (s4, 5, 1), (s5, 3, 1), (s3, 4, 1), (s6, 1, 1), (y0, 0), (s6, 0, 1),
        (s7, 1, 1), (s5, 2, 1), (s4, 4, 1), (s5, 5, 1), (y0b, 0), (s7, 0, 1), (s6, 3, 1), (s5, 4, 1),
        (s6, 2, 1), (s6, 5, 1), (ya0, 1), (s6, 4, 1), (s7, 5, 1), (y1, 0), (s7, 3, 1), (s7, 2, 1), (s7, 4, 1),
        (y0, 1), (y2, 0), (y0b, 1), (y1, 1), (y2, 1),
    )
    adams_left = 2 * len(GROUPS)
    out_rot, out_rot_own = [], []
    for stage, *step in order:
        stage(*step)
        if stage is s4:
            adams_left -= 1
            if adams_left == 0:
                for src, dst in ((m2, new_mom_rot), (v2, new_var_rot)):
                    out_rot.append(send(src.at[o], dst.at[:, mine], dev(dc=1)))
                    out_rot_own.append(local(src.at[c], dst.at[:, mine]))

    slot = 0
    for moves in norm_moves:
        copies = []
        for to in moves:
            copies.append((slot, send(norm, nrecv.at[slot], to)))
            slot += 1
        for _, copy in copies:
            started.pop()
            copy.wait()
        total = norm[...]
        for k, _ in copies:
            total += nrecv[k]
        norm[...] = total
    last = local(norm, out_norm)
    assert count[0] <= N_COPIES and count[1] <= 16

    for copy in started:
        copy.wait_send()
    for copy in out_rot:
        copy.wait_recv()
    for copy in out_rot_own + out_plain + out_back_copies:
        copy.wait()
    last.wait()


def finish(back, norm, *refs):
    sources, outs = (*refs[:4], back), (*refs[5:9], refs[4])
    held_rot, held, norm_v, in_sems, out_sems = refs[9:]
    norm_in = pltpu.make_async_copy(norm, norm_v, in_sems.at[10])
    norm_in.start()
    pieces = []
    for i in range(5):
        for h in range(2):
            if i < 2:
                src, dst, here = sources[i].at[h], outs[i].at[h], held_rot.at[i, h]
            else:
                s = pl.ds(h * KJ, KJ)
                src, dst, here = sources[i].at[s], outs[i].at[s], held.at[i - 2, h]
            pieces.append((pltpu.make_async_copy(src, here, in_sems.at[2 * i + h]),
                           pltpu.make_async_copy(here, dst, out_sems.at[2 * i + h])))
    for into, _ in pieces:
        into.start()
    norm_in.wait()
    graft = jnp.sqrt(jnp.sum(norm_v[0], keepdims=True))
    own = jnp.sqrt(jnp.sum(norm_v[1], keepdims=True))
    scale = graft / (own + 1e-06)
    for k, (into, out) in enumerate(pieces):
        into.wait()
        if k >= 8:
            held[2, k - 8] = held[2, k - 8] * scale
        out.start()
    for _, out in pieces:
        out.wait()


def per_device(grad, basis, mom_rot, var_rot, mom_plain, var_plain):
    plain = jax.ShapeDtypeStruct((KI, KN), F32)
    rot = jax.ShapeDtypeStruct((2, QJ, 2 * KN), F32)
    norms = jax.ShapeDtypeStruct((2, 8, HN), F32)
    scratch = [
        pltpu.VMEM((2, 4, KI, HN), F32),
        pltpu.VMEM((2, 4, KI, HN), BF16),
        pltpu.VMEM((2, 4, KI, HN), BF16),
        pltpu.VMEM((4 * KJ, KI), F32),
        pltpu.VMEM((KJ, KI), BF16),
        pltpu.VMEM((KJ, KI), BF16),
        pltpu.VMEM((KI, 4 * KJ), BF16),
        pltpu.VMEM((KI, 4 * KJ), BF16),
        pltpu.VMEM((2, 4, 8, QJ, HN), F32),
        pltpu.VMEM((2, 4, 8, CJ, HN), F32),
        pltpu.VMEM((2, 2, 8, CJ, HN), F32),
        pltpu.VMEM((2, 2, 8, CJ, HN), F32),
        pltpu.VMEM((2, 8, CJ, HN), F32),
        pltpu.VMEM((2, 8, CJ, HN), F32),
        pltpu.VMEM((2, 2, CJ, 2 * KN), F32),
        pltpu.VMEM((2, 2, CJ, 2 * KN), F32),
        pltpu.VMEM((2, 8, CJ, HN), F32),
        pltpu.VMEM((2, 4, 8, QJ, HN), F32),
        pltpu.VMEM((4, 2 * KJ, HN), BF16),
        pltpu.VMEM((4, 2 * KJ, HN), BF16),
        pltpu.VMEM((2, 4, KI, HN), F32),
        pltpu.VMEM((2, 2, KI // 2, HN), F32),
        pltpu.VMEM((2, 2, KI, HN), F32),
        pltpu.VMEM((KI, KN), F32),
        pltpu.VMEM((KI, KN), F32),
        pltpu.VMEM((2, 8, HN), F32),
        pltpu.VMEM((13, 2, 8, HN), F32),
        pltpu.SemaphoreType.DMA((N_COPIES,)),
        pltpu.SemaphoreType.DMA((N_COPIES,)),
        pltpu.SemaphoreType.DMA((16,)),
    ]
    anywhere = pl.BlockSpec(memory_space=pl.ANY)
    out = pl.pallas_call(
        kernel,
        out_shape=(plain, norms, rot, rot, plain, plain),
        in_specs=[anywhere] * 6,
        out_specs=[anywhere] * 6,
        scratch_shapes=scratch,
        compiler_params=pltpu.CompilerParams(
            collective_id=0, has_side_effects=True, vmem_limit_bytes=63 * 1024 * 1024
        ),
        cost_estimate=pl.CostEstimate(flops=20_000_000_000, bytes_accessed=12_000_000, transcendentals=0),
    )(grad, basis.T, mom_rot.reshape(2, QJ, 2 * KN), var_rot.reshape(2, QJ, 2 * KN), mom_plain, var_plain)
    update, new_mom_rot, new_var_rot, new_mom_plain, new_var_plain = pl.pallas_call(
        finish,
        out_shape=(plain, rot, rot, plain, plain),
        in_specs=[anywhere] * 6,
        out_specs=[anywhere] * 5,
        scratch_shapes=[
            pltpu.VMEM((2, 2, QJ, 2 * KN), F32),
            pltpu.VMEM((3, 2, KJ, KN), F32),
            pltpu.VMEM((2, 8, HN), F32),
            pltpu.SemaphoreType.DMA((11,)),
            pltpu.SemaphoreType.DMA((10,)),
        ],
        compiler_params=pltpu.CompilerParams(vmem_limit_bytes=60 * 1024 * 1024),
        cost_estimate=pl.CostEstimate(flops=1_000_000, bytes_accessed=9_000_000, transcendentals=0),
    )(*out)
    return (
        update,
        new_mom_rot.reshape(KJ, 2 * KN),
        new_var_rot.reshape(KJ, 2 * KN),
        new_mom_plain,
        new_var_plain,
    )


def solution(mesh):
    return jax.shard_map(
        per_device,
        mesh=mesh,
        in_specs=(
            P("rows", "cols"),
            P("rows", "cols"),
            P("cols", "rows"),
            P("cols", "rows"),
            P("rows", "cols"),
            P("rows", "cols"),
        ),
        out_specs=(
            P("rows", "cols"),
            P("cols", "rows"),
            P("cols", "rows"),
            P("rows", "cols"),
            P("rows", "cols"),
        ),
        check_vma=False,
    )
```

```python
import math

import jax
import jax.numpy as jnp
from jax import lax
from jax.experimental import pallas as pl
from jax.experimental.pallas import tpu as pltpu
from jax.sharding import PartitionSpec as P

STEP = 10
BETA = 0.95
EPS = 1e-08
CORR = 1.0 - BETA**STEP

F32 = jnp.float32
BF16 = jnp.bfloat16

KI = 896
KJ = 448
KN = 256
QJ = KJ // 2
HN = KN // 2
CJ = QJ // 2
CHUNKS = ((0, 0), (0, 1), (1, 1), (3, 0), (1, 0), (3, 1), (2, 0), (2, 1))
GROUPS = ((0, 2), (2, 4), (4, 6), (6, 7), (7, 8))
N_COPIES = 128


def adam(moment, second, values):
    moment_new = BETA * moment + (1.0 - BETA) * values
    second_new = BETA * second + (1.0 - BETA) * values * values
    direction = moment_new / CORR / (jnp.sqrt(second_new / CORR) + EPS)
    return moment_new, second_new, direction


def split(a):
    hi = a.astype(BF16)
    lo = (a - hi.astype(F32)).astype(BF16)
    return hi, lo


def dot3(lh, ll, rh, rl):
    left = jnp.concatenate([lh, lh, ll], axis=1)
    right = jnp.concatenate([rh, rl, rh], axis=0)
    return jnp.dot(left, right, preferred_element_type=F32)


def kernel(
    grad, basis_t, mom_rot, var_rot, mom_plain, var_plain,
    out_back, out_norm, new_mom_rot, new_var_rot, new_mom_plain, new_var_plain,
    gg, ghi, glo, bt, lhi, llo, bhi, blo, part, rx, ra, rb, rt, at,
    m2, v2, direc, dd, dhi, dlo, back, ya, yb, mp, vp, norm, nrecv,
    ssem, rsem, lsem,
):
    rows = lax.axis_index("rows")
    cols = lax.axis_index("cols")
    x, c = rows // 2, rows % 2
    y, z = cols // 4, cols % 4
    o = 1 - c

    def dev(dx=0, dc=0, dy=0, dz=0):
        r = (x + dx) % 4 * 2 + (c + dc) % 2
        q = (y + dy) % 4 * 4 + (z + dz) % 4
        return (r, q)

    xp, xm, xo = (x + 1) % 4, (x + 3) % 4, (x + 2) % 4
    yp, ym, yo = (y + 1) % 4, (y + 3) % 4, (y + 2) % 4
    mine = pl.ds(pl.multiple_of(c * CJ, CJ), CJ)
    other = pl.ds(pl.multiple_of(o * CJ, CJ), CJ)
    top, low = pl.ds(0, KI // 2), pl.ds(KI // 2, KI // 2)

    norm_moves = (
        [dev(dc=1)] + [dev(dx=d, dc=e) for d in (1, 2, 3) for e in (0, 1)],
        [dev(dy=d) for d in (1, 2, 3)],
        [dev(dz=d) for d in (1, 2, 3)],
    )
    partners = [p for moves in norm_moves for p in moves]
    barrier = pltpu.get_barrier_semaphore()
    for p in partners:
        pl.semaphore_signal(barrier, inc=1, device_id=p, device_id_type=pl.DeviceIdType.MESH)
    pl.semaphore_wait(barrier, len(partners))

    kinds, sizes, count = [], {}, [0, 0]

    def new_slot():
        count[0] += 1
        return count[0] - 1

    def send(src, dst, to, kind, slot=None):
        if kind not in kinds:
            kinds.append(kind)
            sizes[kind] = 0
        sizes[kind] += math.prod(src.shape)
        copy = pltpu.make_async_remote_copy(
            src_ref=src, dst_ref=dst, send_sem=ssem.at[kinds.index(kind)],
            recv_sem=rsem.at[new_slot() if slot is None else slot],
            device_id=to, device_id_type=pl.DeviceIdType.MESH,
        )
        copy.start()
        return copy

    def whole(ref, slot, kind=0):
        return pltpu.make_async_remote_copy(
            src_ref=ref, dst_ref=ref, send_sem=ssem.at[kind], recv_sem=rsem.at[slot],
            device_id=dev(dc=1), device_id_type=pl.DeviceIdType.MESH,
        )

    def sent(kind, *refs):
        assert sizes.pop(kind) == sum(math.prod(ref.shape) for ref in refs)
        for ref in refs:
            whole(ref, 0, kinds.index(kind)).wait_send()

    def local(src, dst):
        i = count[1]
        count[1] += 1
        copy = pltpu.make_async_copy(src, dst, lsem.at[i])
        copy.start()
        return copy

    state = {}

    def arrived(key):
        for copy in state.pop(key, ()):
            copy.wait_recv()

    def chunk(i):
        return bt.at[pl.ds(i * QJ, QJ)]

    def gg_send(h):
        lanes = pl.ds(h * HN, HN)
        rest = new_slot()
        for way, first, second in ((1, top, low), (3, low, top)):
            state["g", h, way] = [send(grad.at[first, lanes], gg.at[h, y, first], dev(dy=way), "g")]
            send(grad.at[second, lanes], gg.at[h, y, second], dev(dy=way), "g", rest)
        state["g_rest", h] = [whole(gg.at[h, y], rest)]

    gg_send(0)
    halves = [basis_t.at[pl.ds(q * QJ, QJ)] for q in range(2)]
    state["b", 3] = [send(halves[0], chunk(3), dev(dz=1), "b")]
    state["b", 2] = [send(halves[1], chunk(2), dev(dz=3), "b")]
    state["b", 5] = [send(halves[1], chunk(5), dev(dz=1), "b")]
    state["b", 4] = [send(halves[0], chunk(4), dev(dz=3), "b")]
    own_g = [local(grad.at[:, pl.ds(h * HN, HN)], gg.at[h, y]) for h in range(2)]
    own_b = [local(basis_t, bt.at[pl.ds(0, KJ)])]
    own_plain = [local(mom_plain, mp), local(var_plain, vp)]
    state["mv"] = [send(src.at[:, other], dst.at[c], dev(dc=1), "mv") for src, dst in ((mom_rot, m2), (var_rot, v2))]
    own_mv = [local(src.at[:, mine], dst.at[c]) for src, dst in ((mom_rot, m2), (var_rot, v2))]

    norm[0] = jnp.zeros((2, 8, HN), F32)
    out_plain = []

    def done(copies):
        while copies:
            copies.pop().wait()

    def plain():
        done(own_g)
        done(own_plain)

        @pl.loop(0, KI // 64)
        def _(i):
            s = pl.ds(pl.multiple_of(i * 64, 64), 64)
            for h in range(2):
                lanes = slice(h * HN, (h + 1) * HN)
                m, v, d = adam(mp[s, lanes], vp[s, lanes], gg[h, y, s, :])
                mp[s, lanes] = m
                vp[s, lanes] = v
                norm[0, 0] += jnp.sum((d * d).reshape(8, 8, HN), axis=0)

        out_plain.append(local(mp, new_mom_plain))
        out_plain.append(local(vp, new_var_plain))

    def split_grad(h, n):
        @pl.loop(0, KI // 128)
        def _(i):
            s = pl.ds(pl.multiple_of(i * 128, 128), 128)
            hi, lo = split(gg[h, n, s, :])
            ghi[h, n, s, :] = hi
            glo[h, n, s, :] = lo

    def gf(h):
        arrived(("g", h, 1))
        slot = new_slot()
        send(gg.at[h, ym, top], gg.at[h, ym, top], dev(dy=1), "g2", slot)
        arrived(("g", h, 3))
        send(gg.at[h, yp, low], gg.at[h, yp, low], dev(dy=3), "g2", slot)
        state["g2", h] = [whole(gg.at[h, yo], slot)]

    def gs(h):
        done(own_g)
        arrived(("g_rest", h))
        for n in (y, ym, yp):
            split_grad(h, n)

    def gs2(h):
        arrived(("g2", h))
        split_grad(h, yo)

    def bf(way):
        if way == 0:
            arrived(("b", 3))
            state["b", 6] = [send(chunk(3), chunk(6), dev(dz=1), "bf")]
        else:
            arrived(("b", 2))
            state["b", 7] = [send(chunk(2), chunk(7), dev(dz=3), "bf")]

    def basis_there(lo, hi):
        for i in range(lo, hi):
            if i < 2:
                done(own_b)
            arrived(("b", i))

    def away(g):
        return [i for i in range(*GROUPS[g]) if CHUNKS[i][0]]

    def ways(g):
        lo, hi = GROUPS[g]
        if hi - lo == 2:
            return [(pl.ds(lo, 1), mine), (pl.ds(lo + 1, 1), mine)]
        start = pl.multiple_of(c * CJ, CJ)
        return [
            (pl.ds(lo, 1), pl.ds(start, CJ // 2)),
            (pl.ds(lo, 1), pl.ds(pl.multiple_of(start + CJ // 2, CJ // 2), CJ // 2)),
        ]

    def ways_share(g):
        lo, hi = GROUPS[g]
        if hi - lo == 2:
            return [(pl.ds(lo, 1), pl.ds(0, CJ)), (pl.ds(lo + 1, 1), pl.ds(0, CJ))]
        return [(pl.ds(lo, 1), pl.ds(0, CJ // 2)), (pl.ds(lo, 1), pl.ds(CJ // 2, CJ // 2))]

    def s0(g, h):
        lo, hi = GROUPS[g]
        basis_there(lo, hi)
        size = (hi - lo) * QJ
        high, rest = split(bt[lo * QJ:hi * QJ, :])
        lhi[:size, :] = high
        llo[:size, :] = rest

        rh = jnp.concatenate([ghi[h, n] for n in range(4)], axis=1)
        rl = jnp.concatenate([glo[h, n] for n in range(4)], axis=1)
        new = dot3(lhi[:size, :], llo[:size, :], rh, rl)
        for n in range(4):
            for i in range(hi - lo):
                part[h, n, lo + i] = new[i * QJ:(i + 1) * QJ, n * HN:(n + 1) * HN]

        group = pl.ds(lo, hi - lo)
        state["x", g, h] = [send(part.at[h, :, group, other], rx.at[h, :, group], dev(dc=1), "x")]

    def s1(g, h):
        lo, hi = GROUPS[g]
        arrived(("x", g, h))
        group = pl.ds(lo, hi - lo)
        for n in range(4):
            part[h, n, group, mine, :] += rx[h, n, group]
        (first, up), (second, dn) = ways(g)
        (first_r, up_r), (second_r, dn_r) = ways_share(g)
        state["ra", g, h] = [
            send(part.at[h, xo, first, up], ra.at[h, 0, first_r, up_r], dev(dx=1), "ra"),
            send(part.at[h, xo, second, dn], ra.at[h, 1, second_r, dn_r], dev(dx=3), "ra"),
        ]

    def s2(g, h):
        lo, hi = GROUPS[g]
        group = pl.ds(lo, hi - lo)
        (first, up), (second, dn) = ways(g)
        (first_r, up_r), (second_r, dn_r) = ways_share(g)
        a, b = state.pop(("ra", g, h))
        a.wait_recv()
        part[h, xp, first, up, :] += ra[h, 0, first_r, up_r, :]
        slot = new_slot()
        send(part.at[h, xp, group, mine], rb.at[h, 0, group], dev(dx=1), "rb", slot)
        b.wait_recv()
        part[h, xm, second, dn, :] += ra[h, 1, second_r, dn_r, :]
        send(part.at[h, xm, group, mine], rb.at[h, 1, group], dev(dx=3), "rb", slot)
        state["rb", g, h] = [whole(rb.at[h, :, group], slot)]

    def s3(g, h):
        lo, hi = GROUPS[g]
        group = pl.ds(lo, hi - lo)
        arrived(("rb", g, h))
        rt[h, group] = part[h, x, group, mine, :] + rb[h, 0, group] + rb[h, 1, group]
        for i in away(g):
            state["at", i, h] = [send(rt.at[h, i], at.at[h, i], dev(dz=CHUNKS[i][0]), "at")]

    def s4(g, h):
        arrived("mv")
        done(own_mv)
        lo, hi = GROUPS[g]
        if away(g):
            assert away(g) == list(range(lo, hi))
            slot = new_slot()
            state["d", g, h] = [whole(dd.at[h, x, pl.ds(lo, hi - lo), mine], slot)]
        for i in range(lo, hi):
            off, q = CHUNKS[i]
            arrived(("at", i, h))
            values = at[h, i] if off else rt[h, i]
            zs = (z + 4 - off) % 4
            half = zs // 2
            lanes = pl.ds(pl.multiple_of(zs % 2 * KN + h * HN, HN), HN)
            m, v, d = adam(m2[half, q, :, lanes], v2[half, q, :, lanes], values)
            m2[half, q, :, lanes] = m
            v2[half, q, :, lanes] = v
            if off:
                direc[h, i] = d
                send(direc.at[h, i], dd.at[h, x, i, mine], dev(dz=4 - off), "d", slot)
            else:
                dd[h, x, i, mine, :] = d

    def s5(g, h):
        lo, hi = GROUPS[g]
        arrived(("d", g, h))
        t = dd.at[h, x, pl.ds(lo, hi - lo), mine]
        state["ag", g, h] = [send(t, t, dev(dx=1), "ag"), send(t, t, dev(dx=3), "ag")]

    def s6(g, h):
        (first, up), (second, dn) = ways(g)
        a, b = state.pop(("ag", g, h))
        a.wait_recv()
        t = dd.at[h, xm, first, up]
        slot = new_slot()
        send(t, t, dev(dx=1), "ag2", slot)
        b.wait_recv()
        t = dd.at[h, xp, second, dn]
        send(t, t, dev(dx=3), "ag2", slot)
        lo, hi = GROUPS[g]
        state["ag2", g, h] = [whole(dd.at[h, xo, pl.ds(lo, hi - lo), mine], slot)]

    def s7(g, h):
        lo, hi = GROUPS[g]
        arrived(("ag2", g, h))
        t = dd.at[h, :, pl.ds(lo, hi - lo), mine]
        early = hi <= 4
        if ("dc", early, h) not in state:
            slot = new_slot()
            chunks = pl.ds(0, 4) if early else pl.ds(4, 4)
            state["dc", early, h] = [whole(dd.at[h, :, chunks, other], slot)]
            state["dc_slot", early, h] = slot
        send(t, t, dev(dc=1), "dc", state["dc_slot", early, h])

    def turn(p):
        ends = (0, 3, 7, 10, 14)
        basis_there(0, 2 * p + 2)

        @pl.loop(ends[p], ends[p + 1])
        def _(b):
            s = pl.ds(pl.multiple_of(b * 128, 128), 128)
            hi, lo = split(bt[s, :].T)
            bhi[:, s] = hi
            blo[:, s] = lo

    def split_direction(h, part_of):
        @pl.loop(0, 4)
        def _(n):
            @pl.loop(0, 4)
            def _(i):
                hi, lo = split(dd[h, n, part_of * 4 + i])
                s = pl.ds(pl.multiple_of(i * QJ, QJ), QJ)
                dhi[n, s, :] = hi
                dlo[n, s, :] = lo

    def product_two(h, part_of, s):
        rh = jnp.concatenate([dhi[n] for n in range(4)], axis=1)
        rl = jnp.concatenate([dlo[n] for n in range(4)], axis=1)
        k = slice(part_of * 2 * KJ, (part_of + 1) * 2 * KJ)
        new = dot3(bhi[s, k], blo[s, k], rh, rl)
        for n in range(4):
            tile = new[:, n * HN:(n + 1) * HN]
            back[h, n, s, :] = back[h, n, s, :] + tile if part_of else tile

    def directions_there(h, lo, hi):
        arrived(("dc", hi <= 4, h))

    def ya0(h):
        directions_there(h, 0, 4)
        split_direction(h, 0)
        product_two(h, 0, top)
        product_two(h, 0, low)

    def y0(h):
        directions_there(h, 4, 8)
        split_direction(h, 1)
        product_two(h, 1, top)
        state["ya", h] = [send(back.at[h, yo, top], ya.at[h, 0], dev(dy=1), "ya")]
        slot = new_slot()
        state["yb_slot", h] = slot
        state["yb", h] = [whole(yb.at[h], slot)]
        send(back.at[h, ym, top], yb.at[h, 1, top], dev(dy=3), "yb", slot)

    def y0b(h):
        product_two(h, 1, low)
        state["ya", h].append(send(back.at[h, yo, low], ya.at[h, 1], dev(dy=3), "ya"))
        send(back.at[h, yp, low], yb.at[h, 0, low], dev(dy=1), "yb", state["yb_slot", h])

    def y1(h):
        up, dn = state.pop(("ya", h))
        up.wait_recv()
        back[h, yp, top, :] += ya[h, 0]
        slot = state["yb_slot", h]
        send(back.at[h, yp, top], yb.at[h, 0, top], dev(dy=1), "yb", slot)
        dn.wait_recv()
        back[h, ym, low, :] += ya[h, 1]
        send(back.at[h, ym, low], yb.at[h, 1, low], dev(dy=3), "yb", slot)

    out_back_copies = []

    def y2(h):
        arrived(("yb", h))

        @pl.loop(0, KI // 128)
        def _(i):
            s = pl.ds(pl.multiple_of(i * 128, 128), 128)
            b = back[h, y, s, :] + yb[h, 0, s, :] + yb[h, 1, s, :]
            back[h, y, s, :] = b
            norm[0, 1] += jnp.sum((b * b).reshape(16, 8, HN), axis=0)

        out_back_copies.append(local(back.at[h, y], out_back.at[:, pl.ds(h * HN, HN)]))

    order = (
        (turn, 0), (plain,), (gf, 0), (gs, 0), (gg_send, 1), (gs2, 0), (s0, 0, 0), (s0, 1, 0), (gf, 1),
        (s1, 0, 0), (bf, 0), (turn, 1), (s2, 0, 0), (s1, 1, 0), (gs, 1), (bf, 1), (gs2, 1), (s0, 1, 1),
        (s0, 0, 1), (s2, 1, 0), (s3, 0, 0), (s4, 0, 0), (s5, 0, 0), (s1, 1, 1), (s0, 2, 0), (s1, 0, 1),
        (s0, 2, 1), (s2, 1, 1), (s1, 2, 0), (s2, 0, 1), (s3, 1, 0), (turn, 2), (s1, 2, 1), (s2, 2, 0),
        (s6, 0, 0), (s3, 1, 1), (s0, 4, 0), (s2, 2, 1), (s0, 3, 0), (s0, 3, 1), (s1, 4, 0), (s3, 2, 0),
        (s0, 4, 1), (s1, 3, 0), (s4, 1, 0), (s2, 4, 0), (s1, 3, 1), (s3, 2, 1), (s2, 3, 0), (s4, 2, 0),
        (s1, 4, 1), (s5, 1, 0), (s3, 4, 0), (s3, 0, 1), (s2, 3, 1), (s3, 3, 0), (s7, 0, 0), (s5, 2, 0),
        (s4, 4, 0), (turn, 3), (s6, 1, 0), (s4, 3, 0), (s3, 3, 1), (s2, 4, 1), (s4, 0, 1), (s4, 2, 1),
        (s5, 4, 0), (s4, 1, 1), (s5, 3, 0), (s7, 1, 0), (s3, 4, 1), (s6, 2, 0), (s4, 3, 1), (s6, 4, 0),
        (s6, 3, 0), (s5, 0, 1), (s5, 2, 1), (s7, 2, 0), (s5, 1, 1), (s7, 4, 0), (s4, 4, 1), (s7, 3, 0),
        (ya0, 0), (s6, 0, 1), (s5, 4, 1), (y0, 0), (s6, 1, 1), (s7, 0, 1), (s5, 3, 1), (s6, 2, 1), (y0b, 0),
        (s7, 1, 1), (s6, 4, 1), (s6, 3, 1), (s7, 2, 1), (s7, 4, 1), (y1, 0), (s7, 3, 1), (ya0, 1), (y0, 1),
        (y0b, 1), (y1, 1), (y2, 0), (y2, 1),
    )
    adams_left = 2 * len(GROUPS)
    out_rot, out_rot_own = [], []
    for stage, *step in order:
        stage(*step)
        if stage is s4:
            adams_left -= 1
            if adams_left == 0:
                for src, dst in ((m2, new_mom_rot), (v2, new_var_rot)):
                    out_rot.append(send(src.at[o], dst.at[:, mine], dev(dc=1), "out"))
                    out_rot_own.append(local(src.at[c], dst.at[:, mine]))

    first = 0
    for k, moves in enumerate(norm_moves):
        slot = new_slot()
        end = first + len(moves)
        for i, to in enumerate(moves):
            send(norm.at[k], nrecv.at[first + i], to, ("norm", k), slot)
        whole(nrecv.at[pl.ds(first, len(moves))], slot).wait_recv()
        total = norm[k]
        for i in range(first, end):
            total += nrecv[i]
        norm[k + 1] = total
        first = end
    last = local(norm.at[len(norm_moves)], out_norm)
    assert count[0] <= N_COPIES and count[1] <= 16

    share = rt
    away_share = rt.at[:, pl.ds(2, 6)]
    sent("g", gg.at[:, pl.ds(0, 2)])
    sent("g2", gg.at[:, 0])
    sent("b", bt.at[pl.ds(0, 2 * KJ)])
    sent("bf", bt.at[pl.ds(0, KJ)])
    sent("mv", m2.at[0], v2.at[0])
    sent("x", rx)
    sent("ra", share)
    sent("rb", rb)
    sent("at", away_share)
    sent("d", away_share)
    sent("ag", rb)
    sent("ag2", share)
    sent("dc", rx)
    sent("ya", ya)
    sent("yb", yb)
    sent("out", m2.at[0], v2.at[0])
    first = 0
    for k, moves in enumerate(norm_moves):
        sent(("norm", k), nrecv.at[pl.ds(first, len(moves))])
        first += len(moves)
    assert not sizes
    for copy in out_rot:
        copy.wait_recv()
    for copy in out_rot_own + out_plain + out_back_copies:
        copy.wait()
    last.wait()


def finish(back, norm, *refs):
    sources, outs = (*refs[:4], back), (*refs[5:9], refs[4])
    held_rot, held, norm_v, in_sems, out_sems = refs[9:]
    norm_in = pltpu.make_async_copy(norm, norm_v, in_sems.at[10])
    norm_in.start()
    pieces = []
    for i in range(5):
        for h in range(2):
            if i < 2:
                src, dst, here = sources[i].at[h], outs[i].at[h], held_rot.at[i, h]
            else:
                s = pl.ds(h * KJ, KJ)
                src, dst, here = sources[i].at[s], outs[i].at[s], held.at[i - 2, h]
            pieces.append((pltpu.make_async_copy(src, here, in_sems.at[2 * i + h]),
                           pltpu.make_async_copy(here, dst, out_sems.at[2 * i + h])))
    for into, _ in pieces:
        into.start()
    norm_in.wait()
    graft = jnp.sqrt(jnp.sum(norm_v[0], keepdims=True))
    own = jnp.sqrt(jnp.sum(norm_v[1], keepdims=True))
    scale = graft / (own + 1e-06)
    for k, (into, out) in enumerate(pieces):
        into.wait()
        if k >= 8:
            held[2, k - 8] = held[2, k - 8] * scale
        out.start()
    for _, out in pieces:
        out.wait()


def per_device(grad, basis, mom_rot, var_rot, mom_plain, var_plain):
    plain = jax.ShapeDtypeStruct((KI, KN), F32)
    rot = jax.ShapeDtypeStruct((2, QJ, 2 * KN), F32)
    norms = jax.ShapeDtypeStruct((2, 8, HN), F32)
    scratch = [
        pltpu.VMEM((2, 4, KI, HN), F32),
        pltpu.VMEM((2, 4, KI, HN), BF16),
        pltpu.VMEM((2, 4, KI, HN), BF16),
        pltpu.VMEM((4 * KJ, KI), F32),
        pltpu.VMEM((KJ, KI), BF16),
        pltpu.VMEM((KJ, KI), BF16),
        pltpu.VMEM((KI, 4 * KJ), BF16),
        pltpu.VMEM((KI, 4 * KJ), BF16),
        pltpu.VMEM((2, 4, 8, QJ, HN), F32),
        pltpu.VMEM((2, 4, 8, CJ, HN), F32),
        pltpu.VMEM((2, 2, 8, CJ, HN), F32),
        pltpu.VMEM((2, 2, 8, CJ, HN), F32),
        pltpu.VMEM((2, 8, CJ, HN), F32),
        pltpu.VMEM((2, 8, CJ, HN), F32),
        pltpu.VMEM((2, 2, CJ, 2 * KN), F32),
        pltpu.VMEM((2, 2, CJ, 2 * KN), F32),
        pltpu.VMEM((2, 8, CJ, HN), F32),
        pltpu.VMEM((2, 4, 8, QJ, HN), F32),
        pltpu.VMEM((4, 2 * KJ, HN), BF16),
        pltpu.VMEM((4, 2 * KJ, HN), BF16),
        pltpu.VMEM((2, 4, KI, HN), F32),
        pltpu.VMEM((2, 2, KI // 2, HN), F32),
        pltpu.VMEM((2, 2, KI, HN), F32),
        pltpu.VMEM((KI, KN), F32),
        pltpu.VMEM((KI, KN), F32),
        pltpu.VMEM((4, 2, 8, HN), F32),
        pltpu.VMEM((13, 2, 8, HN), F32),
        pltpu.SemaphoreType.DMA((24,)),
        pltpu.SemaphoreType.DMA((N_COPIES,)),
        pltpu.SemaphoreType.DMA((16,)),
    ]
    anywhere = pl.BlockSpec(memory_space=pl.ANY)
    out = pl.pallas_call(
        kernel,
        out_shape=(plain, norms, rot, rot, plain, plain),
        in_specs=[anywhere] * 6,
        out_specs=[anywhere] * 6,
        scratch_shapes=scratch,
        compiler_params=pltpu.CompilerParams(
            collective_id=0, has_side_effects=True, vmem_limit_bytes=63 * 1024 * 1024
        ),
        cost_estimate=pl.CostEstimate(flops=20_000_000_000, bytes_accessed=12_000_000, transcendentals=0),
    )(grad, basis.T, mom_rot.reshape(2, QJ, 2 * KN), var_rot.reshape(2, QJ, 2 * KN), mom_plain, var_plain)
    update, new_mom_rot, new_var_rot, new_mom_plain, new_var_plain = pl.pallas_call(
        finish,
        out_shape=(plain, rot, rot, plain, plain),
        in_specs=[anywhere] * 6,
        out_specs=[anywhere] * 5,
        scratch_shapes=[
            pltpu.VMEM((2, 2, QJ, 2 * KN), F32),
            pltpu.VMEM((3, 2, KJ, KN), F32),
            pltpu.VMEM((2, 8, HN), F32),
            pltpu.SemaphoreType.DMA((11,)),
            pltpu.SemaphoreType.DMA((10,)),
        ],
        compiler_params=pltpu.CompilerParams(vmem_limit_bytes=60 * 1024 * 1024),
        cost_estimate=pl.CostEstimate(flops=1_000_000, bytes_accessed=9_000_000, transcendentals=0),
    )(*out)
    return (
        update,
        new_mom_rot.reshape(KJ, 2 * KN),
        new_var_rot.reshape(KJ, 2 * KN),
        new_mom_plain,
        new_var_plain,
    )


def solution(mesh):
    return jax.shard_map(
        per_device,
        mesh=mesh,
        in_specs=(
            P("rows", "cols"),
            P("rows", "cols"),
            P("cols", "rows"),
            P("cols", "rows"),
            P("rows", "cols"),
            P("rows", "cols"),
        ),
        out_specs=(
            P("rows", "cols"),
            P("cols", "rows"),
            P("cols", "rows"),
            P("rows", "cols"),
            P("rows", "cols"),
        ),
        check_vma=False,
    )
```

```python
import math

import jax
import jax.numpy as jnp
from jax import lax
from jax.experimental import pallas as pl
from jax.experimental.pallas import tpu as pltpu
from jax.sharding import PartitionSpec as P

STEP = 10
BETA = 0.95
EPS = 1e-08
CORR = 1.0 - BETA**STEP

F32 = jnp.float32
BF16 = jnp.bfloat16

KI = 896
KJ = 448
KN = 256
QJ = KJ // 2
HN = KN // 2
CJ = QJ // 2
CHUNKS = ((0, 0), (0, 1), (1, 1), (3, 0), (1, 0), (3, 1), (2, 0), (2, 1))
GROUPS = ((0, 2), (2, 4), (4, 6), (6, 7), (7, 8))
N_COPIES = 128


def adam(moment, second, values):
    moment_new = BETA * moment + (1.0 - BETA) * values
    second_new = BETA * second + (1.0 - BETA) * values * values
    direction = moment_new / CORR / (jnp.sqrt(second_new / CORR) + EPS)
    return moment_new, second_new, direction


def split(a):
    hi = a.astype(BF16)
    lo = (a - hi.astype(F32)).astype(BF16)
    return hi, lo


def dot3(lh, ll, rh, rl):
    left = jnp.concatenate([lh, lh, ll], axis=1)
    right = jnp.concatenate([rh, rl, rh], axis=0)
    return jnp.dot(left, right, preferred_element_type=F32)


def kernel(
    grad, basis_t, mom_rot, var_rot, mom_plain, var_plain,
    out_back, out_norm, new_mom_rot, new_var_rot, new_mom_plain, new_var_plain,
    gg, ghi, glo, bt, lhi, llo, bhi, blo, part, rx, ra, rb, rt, at,
    m2, v2, direc, dd, dhi, dlo, back, ya, yb, mp, vp, norm, nrecv,
    ssem, rsem, lsem,
):
    rows = lax.axis_index("rows")
    cols = lax.axis_index("cols")
    x, c = rows // 2, rows % 2
    y, z = cols // 4, cols % 4
    o = 1 - c

    def dev(dx=0, dc=0, dy=0, dz=0):
        r = (x + dx) % 4 * 2 + (c + dc) % 2
        q = (y + dy) % 4 * 4 + (z + dz) % 4
        return (r, q)

    xp, xm, xo = (x + 1) % 4, (x + 3) % 4, (x + 2) % 4
    yp, ym, yo = (y + 1) % 4, (y + 3) % 4, (y + 2) % 4
    mine = pl.ds(pl.multiple_of(c * CJ, CJ), CJ)
    other = pl.ds(pl.multiple_of(o * CJ, CJ), CJ)
    top, low = pl.ds(0, KI // 2), pl.ds(KI // 2, KI // 2)

    norm_moves = (
        [dev(dc=1)] + [dev(dx=d, dc=e) for d in (1, 2, 3) for e in (0, 1)],
        [dev(dy=d) for d in (1, 2, 3)],
        [dev(dz=d) for d in (1, 2, 3)],
    )
    partners = [p for moves in norm_moves for p in moves]
    barrier = pltpu.get_barrier_semaphore()
    for p in partners:
        pl.semaphore_signal(barrier, inc=1, device_id=p, device_id_type=pl.DeviceIdType.MESH)
    pl.semaphore_wait(barrier, len(partners))

    kinds, sizes, count = [], {}, [0, 0]

    def new_slot():
        count[0] += 1
        return count[0] - 1

    def send(src, dst, to, kind, slot=None):
        if kind not in kinds:
            kinds.append(kind)
            sizes[kind] = 0
        sizes[kind] += math.prod(src.shape)
        copy = pltpu.make_async_remote_copy(
            src_ref=src, dst_ref=dst, send_sem=ssem.at[kinds.index(kind)],
            recv_sem=rsem.at[new_slot() if slot is None else slot],
            device_id=to, device_id_type=pl.DeviceIdType.MESH,
        )
        copy.start()
        return copy

    def whole(ref, slot, kind=0):
        return pltpu.make_async_remote_copy(
            src_ref=ref, dst_ref=ref, send_sem=ssem.at[kind], recv_sem=rsem.at[slot],
            device_id=dev(dc=1), device_id_type=pl.DeviceIdType.MESH,
        )

    def sent(kind, *refs):
        assert sizes.pop(kind) == sum(math.prod(ref.shape) for ref in refs)
        for ref in refs:
            whole(ref, 0, kinds.index(kind)).wait_send()

    def local(src, dst):
        i = count[1]
        count[1] += 1
        copy = pltpu.make_async_copy(src, dst, lsem.at[i])
        copy.start()
        return copy

    state = {}

    def arrived(key):
        for copy in state.pop(key, ()):
            copy.wait_recv()

    def chunk(i):
        return bt.at[pl.ds(i * QJ, QJ)]

    def gg_send(h):
        lanes = pl.ds(h * HN, HN)
        rest = new_slot()
        for way, first, second in ((1, top, low), (3, low, top)):
            state["g", h, way] = [send(grad.at[first, lanes], gg.at[h, y, first], dev(dy=way), "g")]
            send(grad.at[second, lanes], gg.at[h, y, second], dev(dy=way), "g", rest)
        state["g_rest", h] = [whole(gg.at[h, y], rest)]

    gg_send(0)
    halves = [basis_t.at[pl.ds(q * QJ, QJ)] for q in range(2)]
    state["b", 3] = [send(halves[0], chunk(3), dev(dz=1), "b")]
    state["b", 2] = [send(halves[1], chunk(2), dev(dz=3), "b")]
    state["b", 5] = [send(halves[1], chunk(5), dev(dz=1), "b")]
    state["b", 4] = [send(halves[0], chunk(4), dev(dz=3), "b")]
    own_g = [local(grad.at[:, pl.ds(h * HN, HN)], gg.at[h, y]) for h in range(2)]
    own_b = [local(basis_t, bt.at[pl.ds(0, KJ)])]
    own_plain = [local(mom_plain, mp), local(var_plain, vp)]
    state["mv"] = [send(src.at[:, other], dst.at[c], dev(dc=1), "mv") for src, dst in ((mom_rot, m2), (var_rot, v2))]
    own_mv = [local(src.at[:, mine], dst.at[c]) for src, dst in ((mom_rot, m2), (var_rot, v2))]

    norm[0] = jnp.zeros((2, 8, HN), F32)
    out_plain = []

    def done(copies):
        while copies:
            copies.pop().wait()

    def plain():
        done(own_g)
        done(own_plain)

        @pl.loop(0, KI // 64)
        def _(i):
            s = pl.ds(pl.multiple_of(i * 64, 64), 64)
            for h in range(2):
                lanes = slice(h * HN, (h + 1) * HN)
                m, v, d = adam(mp[s, lanes], vp[s, lanes], gg[h, y, s, :])
                mp[s, lanes] = m
                vp[s, lanes] = v
                norm[0, 0] += jnp.sum((d * d).reshape(8, 8, HN), axis=0)

        out_plain.append(local(mp, new_mom_plain))
        out_plain.append(local(vp, new_var_plain))

    def split_grad(h, n):
        @pl.loop(0, KI // 128)
        def _(i):
            s = pl.ds(pl.multiple_of(i * 128, 128), 128)
            hi, lo = split(gg[h, n, s, :])
            ghi[h, n, s, :] = hi
            glo[h, n, s, :] = lo

    def gf(h):
        arrived(("g", h, 1))
        slot = new_slot()
        send(gg.at[h, ym, top], gg.at[h, ym, top], dev(dy=1), "g2", slot)
        arrived(("g", h, 3))
        send(gg.at[h, yp, low], gg.at[h, yp, low], dev(dy=3), "g2", slot)
        state["g2", h] = [whole(gg.at[h, yo], slot)]

    def gs(h):
        done(own_g)
        arrived(("g_rest", h))
        for n in (y, ym, yp):
            split_grad(h, n)

    def gs2(h):
        arrived(("g2", h))
        split_grad(h, yo)

    def bf(way):
        if way == 0:
            arrived(("b", 3))
            state["b", 6] = [send(chunk(3), chunk(6), dev(dz=1), "bf")]
        else:
            arrived(("b", 2))
            state["b", 7] = [send(chunk(2), chunk(7), dev(dz=3), "bf")]

    def basis_there(lo, hi):
        for i in range(lo, hi):
            if i < 2:
                done(own_b)
            arrived(("b", i))

    def away(g):
        return [i for i in range(*GROUPS[g]) if CHUNKS[i][0]]

    def ways(g):
        lo, hi = GROUPS[g]
        if hi - lo == 2:
            return [(pl.ds(lo, 1), mine), (pl.ds(lo + 1, 1), mine)]
        start = pl.multiple_of(c * CJ, CJ)
        return [
            (pl.ds(lo, 1), pl.ds(start, CJ // 2)),
            (pl.ds(lo, 1), pl.ds(pl.multiple_of(start + CJ // 2, CJ // 2), CJ // 2)),
        ]

    def ways_share(g):
        lo, hi = GROUPS[g]
        if hi - lo == 2:
            return [(pl.ds(lo, 1), pl.ds(0, CJ)), (pl.ds(lo + 1, 1), pl.ds(0, CJ))]
        return [(pl.ds(lo, 1), pl.ds(0, CJ // 2)), (pl.ds(lo, 1), pl.ds(CJ // 2, CJ // 2))]

    def s0(g, h):
        lo, hi = GROUPS[g]
        basis_there(lo, hi)
        size = (hi - lo) * QJ
        high, rest = split(bt[lo * QJ:hi * QJ, :])
        lhi[:size, :] = high
        llo[:size, :] = rest

        rh = jnp.concatenate([ghi[h, n] for n in range(4)], axis=1)
        rl = jnp.concatenate([glo[h, n] for n in range(4)], axis=1)
        new = dot3(lhi[:size, :], llo[:size, :], rh, rl)
        for n in range(4):
            for i in range(hi - lo):
                part[h, n, lo + i] = new[i * QJ:(i + 1) * QJ, n * HN:(n + 1) * HN]

        group = pl.ds(lo, hi - lo)
        state["x", g, h] = [send(part.at[h, :, group, other], rx.at[h, :, group], dev(dc=1), "x")]

    def s1(g, h):
        lo, hi = GROUPS[g]
        arrived(("x", g, h))
        group = pl.ds(lo, hi - lo)
        for n in range(4):
            part[h, n, group, mine, :] += rx[h, n, group]
        (first, up), (second, dn) = ways(g)
        (first_r, up_r), (second_r, dn_r) = ways_share(g)
        state["ra", g, h] = [
            send(part.at[h, xo, first, up], ra.at[h, 0, first_r, up_r], dev(dx=1), "ra"),
            send(part.at[h, xo, second, dn], ra.at[h, 1, second_r, dn_r], dev(dx=3), "ra"),
        ]

    def s2(g, h):
        lo, hi = GROUPS[g]
        group = pl.ds(lo, hi - lo)
        (first, up), (second, dn) = ways(g)
        (first_r, up_r), (second_r, dn_r) = ways_share(g)
        a, b = state.pop(("ra", g, h))
        a.wait_recv()
        part[h, xp, first, up, :] += ra[h, 0, first_r, up_r, :]
        slot = new_slot()
        send(part.at[h, xp, group, mine], rb.at[h, 0, group], dev(dx=1), "rb", slot)
        b.wait_recv()
        part[h, xm, second, dn, :] += ra[h, 1, second_r, dn_r, :]
        send(part.at[h, xm, group, mine], rb.at[h, 1, group], dev(dx=3), "rb", slot)
        state["rb", g, h] = [whole(rb.at[h, :, group], slot)]

    def s3(g, h):
        lo, hi = GROUPS[g]
        group = pl.ds(lo, hi - lo)
        arrived(("rb", g, h))
        rt[h, group] = part[h, x, group, mine, :] + rb[h, 0, group] + rb[h, 1, group]
        for i in away(g):
            state["at", i, h] = [send(rt.at[h, i], at.at[h, i], dev(dz=CHUNKS[i][0]), "at")]

    def s4(g, h):
        arrived("mv")
        done(own_mv)
        lo, hi = GROUPS[g]
        if away(g):
            assert away(g) == list(range(lo, hi))
            slot = new_slot()
            state["d", g, h] = [whole(dd.at[h, 0, pl.ds(lo, hi - lo), mine], slot)]
        for i in range(lo, hi):
            off, q = CHUNKS[i]
            arrived(("at", i, h))
            values = at[h, i] if off else rt[h, i]
            zs = (z + 4 - off) % 4
            half = zs // 2
            lanes = pl.ds(pl.multiple_of(zs % 2 * KN + h * HN, HN), HN)
            m, v, d = adam(m2[half, q, :, lanes], v2[half, q, :, lanes], values)
            m2[half, q, :, lanes] = m
            v2[half, q, :, lanes] = v
            if off:
                direc[h, i] = d
                send(direc.at[h, i], dd.at[h, 0, i, mine], dev(dz=4 - off), "d", slot)
            else:
                dd[h, 0, i, mine, :] = d

    def s5(g, h):
        lo, hi = GROUPS[g]
        group = pl.ds(lo, hi - lo)
        arrived(("d", g, h))
        t = dd.at[h, 0, group, mine]
        state["ag", g, h] = [
            send(t, dd.at[h, 2, group, mine], dev(dx=1), "ag"),
            send(t, dd.at[h, 1, group, mine], dev(dx=3), "ag"),
        ]

    def to_other_core(g, h, first, blocks):
        lo, hi = GROUPS[g]
        early = hi <= 4
        if ("dc", early, h) not in state:
            slot = new_slot()
            chunks = pl.ds(0, 4) if early else pl.ds(4, 4)
            state["dc", early, h] = [whole(dd.at[h, :, chunks, other], slot)]
            state["dc_slot", early, h] = slot
        t = dd.at[h, pl.ds(first, blocks), pl.ds(lo, hi - lo), mine]
        send(t, t, dev(dc=1), "dc", state["dc_slot", early, h])

    def s6(g, h):
        lo, hi = GROUPS[g]
        (first, up), (second, dn) = ways(g)
        a, b = state.pop(("ag", g, h))
        slot = new_slot()
        a.wait_recv()
        send(dd.at[h, 2, first, up], dd.at[h, 3, first, up], dev(dx=1), "ag2", slot)
        b.wait_recv()
        send(dd.at[h, 1, second, dn], dd.at[h, 3, second, dn], dev(dx=3), "ag2", slot)
        state["ag2", g, h] = [whole(dd.at[h, 3, pl.ds(lo, hi - lo), mine], slot)]
        to_other_core(g, h, 0, 3)

    def s7(g, h):
        arrived(("ag2", g, h))
        to_other_core(g, h, 3, 1)

    def turn(p):
        ends = (0, 3, 7, 10, 14)
        basis_there(0, 2 * p + 2)

        @pl.loop(ends[p], ends[p + 1])
        def _(b):
            s = pl.ds(pl.multiple_of(b * 128, 128), 128)
            hi, lo = split(bt[s, :].T)
            bhi[:, s] = hi
            blo[:, s] = lo

    def split_direction(h, part_of):
        @pl.loop(0, 4)
        def _(n):
            d = (n + 4 - x) % 4
            place = d + d // 2 * (1 - 2 * (d % 2))

            @pl.loop(0, 4)
            def _(i):
                hi, lo = split(dd[h, place, part_of * 4 + i])
                s = pl.ds(pl.multiple_of(i * QJ, QJ), QJ)
                dhi[n, s, :] = hi
                dlo[n, s, :] = lo

    def product_two(h, part_of, s):
        rh = jnp.concatenate([dhi[n] for n in range(4)], axis=1)
        rl = jnp.concatenate([dlo[n] for n in range(4)], axis=1)
        k = slice(part_of * 2 * KJ, (part_of + 1) * 2 * KJ)
        new = dot3(bhi[s, k], blo[s, k], rh, rl)
        for n in range(4):
            tile = new[:, n * HN:(n + 1) * HN]
            back[h, n, s, :] = back[h, n, s, :] + tile if part_of else tile

    def directions_there(h, lo, hi):
        arrived(("dc", hi <= 4, h))

    def ya0(h):
        directions_there(h, 0, 4)
        split_direction(h, 0)
        product_two(h, 0, top)
        product_two(h, 0, low)

    def y0(h):
        directions_there(h, 4, 8)
        split_direction(h, 1)
        product_two(h, 1, top)
        state["ya", h] = [send(back.at[h, yo, top], ya.at[h, 0], dev(dy=1), "ya")]
        slot = new_slot()
        state["yb_slot", h] = slot
        state["yb", h] = [whole(yb.at[h], slot)]
        send(back.at[h, ym, top], yb.at[h, 1, top], dev(dy=3), "yb", slot)

    def y0b(h):
        product_two(h, 1, low)
        state["ya", h].append(send(back.at[h, yo, low], ya.at[h, 1], dev(dy=3), "ya"))
        send(back.at[h, yp, low], yb.at[h, 0, low], dev(dy=1), "yb", state["yb_slot", h])

    def y1(h):
        up, dn = state.pop(("ya", h))
        up.wait_recv()
        back[h, yp, top, :] += ya[h, 0]
        slot = state["yb_slot", h]
        send(back.at[h, yp, top], yb.at[h, 0, top], dev(dy=1), "yb", slot)
        dn.wait_recv()
        back[h, ym, low, :] += ya[h, 1]
        send(back.at[h, ym, low], yb.at[h, 1, low], dev(dy=3), "yb", slot)

    out_back_copies = []

    def y2(h):
        arrived(("yb", h))

        @pl.loop(0, KI // 128)
        def _(i):
            s = pl.ds(pl.multiple_of(i * 128, 128), 128)
            b = back[h, y, s, :] + yb[h, 0, s, :] + yb[h, 1, s, :]
            back[h, y, s, :] = b
            norm[0, 1] += jnp.sum((b * b).reshape(16, 8, HN), axis=0)

        out_back_copies.append(local(back.at[h, y], out_back.at[:, pl.ds(h * HN, HN)]))

    order = (
        (gf, 0), (gs, 0), (gg_send, 1), (gs2, 0), (s0, 0, 0), (s0, 1, 0), (turn, 0), (bf, 0), (s1, 0, 0),
        (bf, 1), (gf, 1), (s2, 0, 0), (s1, 1, 0), (plain,), (s3, 0, 0), (gs, 1), (s4, 0, 0), (s5, 0, 0),
        (gs2, 1), (s0, 0, 1), (s2, 1, 0), (s0, 1, 1), (s6, 0, 0), (s0, 2, 0), (s1, 0, 1), (s3, 1, 0),
        (s1, 1, 1), (s2, 0, 1), (s0, 2, 1), (s2, 1, 1), (s1, 2, 0), (turn, 1), (s3, 0, 1), (s4, 0, 1),
        (s5, 0, 1), (s1, 2, 1), (s3, 1, 1), (s7, 0, 0), (turn, 2), (s6, 0, 1), (s2, 2, 0), (s2, 2, 1),
        (s0, 3, 0), (s0, 4, 0), (s4, 1, 0), (s0, 3, 1), (s1, 3, 0), (s3, 2, 0), (s1, 4, 0), (s5, 1, 0),
        (s4, 1, 1), (s2, 3, 0), (s3, 2, 1), (s4, 2, 0), (s2, 4, 0), (s0, 4, 1), (s7, 0, 1), (s1, 3, 1),
        (s3, 3, 0), (s6, 1, 0), (s3, 4, 0), (s1, 4, 1), (s2, 3, 1), (s7, 1, 0), (s5, 2, 0), (s4, 3, 0),
        (s2, 4, 1), (s5, 1, 1), (s4, 4, 0), (s3, 3, 1), (ya0, 0), (s5, 4, 0), (s3, 4, 1), (s5, 3, 0),
        (s6, 2, 0), (s4, 2, 1), (s4, 3, 1), (s6, 4, 0), (s4, 4, 1), (s6, 3, 0), (s5, 2, 1), (turn, 3),
        (s7, 2, 0), (s7, 4, 0), (s7, 3, 0), (s5, 3, 1), (s6, 1, 1), (s5, 4, 1), (y0, 0), (s6, 3, 1),
        (s7, 1, 1), (s6, 2, 1), (s6, 4, 1), (y0b, 0), (s7, 3, 1), (s7, 2, 1), (s7, 4, 1), (ya0, 1), (y0, 1),
        (y0b, 1), (y1, 0), (y1, 1), (y2, 0), (y2, 1),
    )
    adams_left = 2 * len(GROUPS)
    out_rot, out_rot_own = [], []
    for stage, *step in order:
        stage(*step)
        if stage is s4:
            adams_left -= 1
            if adams_left == 0:
                for src, dst in ((m2, new_mom_rot), (v2, new_var_rot)):
                    out_rot.append(send(src.at[o], dst.at[:, mine], dev(dc=1), "out"))
                    out_rot_own.append(local(src.at[c], dst.at[:, mine]))

    first = 0
    for k, moves in enumerate(norm_moves):
        slot = new_slot()
        end = first + len(moves)
        for i, to in enumerate(moves):
            send(norm.at[k], nrecv.at[first + i], to, ("norm", k), slot)
        whole(nrecv.at[pl.ds(first, len(moves))], slot).wait_recv()
        total = norm[k]
        for i in range(first, end):
            total += nrecv[i]
        norm[k + 1] = total
        first = end
    last = local(norm.at[len(norm_moves)], out_norm)
    assert count[0] <= N_COPIES and count[1] <= 16

    share = rt
    away_share = rt.at[:, pl.ds(2, 6)]
    sent("g", gg.at[:, pl.ds(0, 2)])
    sent("g2", gg.at[:, 0])
    sent("b", bt.at[pl.ds(0, 2 * KJ)])
    sent("bf", bt.at[pl.ds(0, KJ)])
    sent("mv", m2.at[0], v2.at[0])
    sent("x", rx)
    sent("ra", share)
    sent("rb", rb)
    sent("at", away_share)
    sent("d", away_share)
    sent("ag", rb)
    sent("ag2", share)
    sent("dc", rx)
    sent("ya", ya)
    sent("yb", yb)
    sent("out", m2.at[0], v2.at[0])
    first = 0
    for k, moves in enumerate(norm_moves):
        sent(("norm", k), nrecv.at[pl.ds(first, len(moves))])
        first += len(moves)
    assert not sizes
    for copy in out_rot:
        copy.wait_recv()
    for copy in out_rot_own + out_plain + out_back_copies:
        copy.wait()
    last.wait()


def finish(back, norm, *refs):
    sources, outs = (*refs[:4], back), (*refs[5:9], refs[4])
    held_rot, held, norm_v, in_sems, out_sems = refs[9:]
    norm_in = pltpu.make_async_copy(norm, norm_v, in_sems.at[10])
    norm_in.start()
    pieces = []
    for i in range(5):
        for h in range(2):
            if i < 2:
                src, dst, here = sources[i].at[h], outs[i].at[h], held_rot.at[i, h]
            else:
                s = pl.ds(h * KJ, KJ)
                src, dst, here = sources[i].at[s], outs[i].at[s], held.at[i - 2, h]
            pieces.append((pltpu.make_async_copy(src, here, in_sems.at[2 * i + h]),
                           pltpu.make_async_copy(here, dst, out_sems.at[2 * i + h])))
    for into, _ in pieces:
        into.start()
    norm_in.wait()
    graft = jnp.sqrt(jnp.sum(norm_v[0], keepdims=True))
    own = jnp.sqrt(jnp.sum(norm_v[1], keepdims=True))
    scale = graft / (own + 1e-06)
    for k, (into, out) in enumerate(pieces):
        into.wait()
        if k >= 8:
            held[2, k - 8] = held[2, k - 8] * scale
        out.start()
    for _, out in pieces:
        out.wait()


def per_device(grad, basis, mom_rot, var_rot, mom_plain, var_plain):
    plain = jax.ShapeDtypeStruct((KI, KN), F32)
    rot = jax.ShapeDtypeStruct((2, QJ, 2 * KN), F32)
    norms = jax.ShapeDtypeStruct((2, 8, HN), F32)
    scratch = [
        pltpu.VMEM((2, 4, KI, HN), F32),
        pltpu.VMEM((2, 4, KI, HN), BF16),
        pltpu.VMEM((2, 4, KI, HN), BF16),
        pltpu.VMEM((4 * KJ, KI), F32),
        pltpu.VMEM((KJ, KI), BF16),
        pltpu.VMEM((KJ, KI), BF16),
        pltpu.VMEM((KI, 4 * KJ), BF16),
        pltpu.VMEM((KI, 4 * KJ), BF16),
        pltpu.VMEM((2, 4, 8, QJ, HN), F32),
        pltpu.VMEM((2, 4, 8, CJ, HN), F32),
        pltpu.VMEM((2, 2, 8, CJ, HN), F32),
        pltpu.VMEM((2, 2, 8, CJ, HN), F32),
        pltpu.VMEM((2, 8, CJ, HN), F32),
        pltpu.VMEM((2, 8, CJ, HN), F32),
        pltpu.VMEM((2, 2, CJ, 2 * KN), F32),
        pltpu.VMEM((2, 2, CJ, 2 * KN), F32),
        pltpu.VMEM((2, 8, CJ, HN), F32),
        pltpu.VMEM((2, 4, 8, QJ, HN), F32),
        pltpu.VMEM((4, 2 * KJ, HN), BF16),
        pltpu.VMEM((4, 2 * KJ, HN), BF16),
        pltpu.VMEM((2, 4, KI, HN), F32),
        pltpu.VMEM((2, 2, KI // 2, HN), F32),
        pltpu.VMEM((2, 2, KI, HN), F32),
        pltpu.VMEM((KI, KN), F32),
        pltpu.VMEM((KI, KN), F32),
        pltpu.VMEM((4, 2, 8, HN), F32),
        pltpu.VMEM((13, 2, 8, HN), F32),
        pltpu.SemaphoreType.DMA((24,)),
        pltpu.SemaphoreType.DMA((N_COPIES,)),
        pltpu.SemaphoreType.DMA((16,)),
    ]
    anywhere = pl.BlockSpec(memory_space=pl.ANY)
    out = pl.pallas_call(
        kernel,
        out_shape=(plain, norms, rot, rot, plain, plain),
        in_specs=[anywhere] * 6,
        out_specs=[anywhere] * 6,
        scratch_shapes=scratch,
        compiler_params=pltpu.CompilerParams(
            collective_id=0, has_side_effects=True, vmem_limit_bytes=63 * 1024 * 1024
        ),
        cost_estimate=pl.CostEstimate(flops=20_000_000_000, bytes_accessed=12_000_000, transcendentals=0),
    )(grad, basis.T, mom_rot.reshape(2, QJ, 2 * KN), var_rot.reshape(2, QJ, 2 * KN), mom_plain, var_plain)
    update, new_mom_rot, new_var_rot, new_mom_plain, new_var_plain = pl.pallas_call(
        finish,
        out_shape=(plain, rot, rot, plain, plain),
        in_specs=[anywhere] * 6,
        out_specs=[anywhere] * 5,
        scratch_shapes=[
            pltpu.VMEM((2, 2, QJ, 2 * KN), F32),
            pltpu.VMEM((3, 2, KJ, KN), F32),
            pltpu.VMEM((2, 8, HN), F32),
            pltpu.SemaphoreType.DMA((11,)),
            pltpu.SemaphoreType.DMA((10,)),
        ],
        compiler_params=pltpu.CompilerParams(vmem_limit_bytes=60 * 1024 * 1024),
        cost_estimate=pl.CostEstimate(flops=1_000_000, bytes_accessed=9_000_000, transcendentals=0),
    )(*out)
    return (
        update,
        new_mom_rot.reshape(KJ, 2 * KN),
        new_var_rot.reshape(KJ, 2 * KN),
        new_mom_plain,
        new_var_plain,
    )


def solution(mesh):
    return jax.shard_map(
        per_device,
        mesh=mesh,
        in_specs=(
            P("rows", "cols"),
            P("rows", "cols"),
            P("cols", "rows"),
            P("cols", "rows"),
            P("rows", "cols"),
            P("rows", "cols"),
        ),
        out_specs=(
            P("rows", "cols"),
            P("cols", "rows"),
            P("cols", "rows"),
            P("rows", "cols"),
            P("rows", "cols"),
        ),
        check_vma=False,
    )
```

```python
import math

import jax
import jax.numpy as jnp
from jax import lax
from jax.experimental import pallas as pl
from jax.experimental.pallas import tpu as pltpu
from jax.sharding import PartitionSpec as P

STEP = 10
BETA = 0.95
EPS = 1e-08
CORR = 1.0 - BETA**STEP

F32 = jnp.float32
BF16 = jnp.bfloat16

KI = 896
KJ = 448
KN = 256
QJ = KJ // 2
HN = KN // 2
CJ = QJ // 2
CHUNKS = ((0, 0), (0, 1), (1, 1), (3, 0), (1, 0), (3, 1), (2, 0), (2, 1))
GROUPS = ((0, 2), (2, 4), (4, 6), (6, 7), (7, 8))
PRODUCTS = ((0, 1), (2,), (3, 4))
N_COPIES = 128


def adam(moment, second, values):
    moment_new = BETA * moment + (1.0 - BETA) * values
    second_new = BETA * second + (1.0 - BETA) * values * values
    direction = moment_new / CORR / (jnp.sqrt(second_new / CORR) + EPS)
    return moment_new, second_new, direction


def split(a):
    hi = a.astype(BF16)
    lo = (a - hi.astype(F32)).astype(BF16)
    return hi, lo


def dot3(lh, ll, rh, rl):
    left = jnp.concatenate([lh, lh, ll], axis=1)
    right = jnp.concatenate([rh, rl, rh], axis=0)
    return jnp.dot(left, right, preferred_element_type=F32)


def kernel(
    grad, basis_t, mom_rot, var_rot, mom_plain, var_plain,
    out_back, out_norm, new_mom_rot, new_var_rot, new_mom_plain, new_var_plain,
    gg, ghi, glo, bt, lhi, llo, bhi, blo, part, rx, ra, rb, rt, at,
    m2, v2, direc, dd, dhi, dlo, back, ya, yb, mp, vp, norm, nrecv,
    ssem, rsem, lsem,
):
    rows = lax.axis_index("rows")
    cols = lax.axis_index("cols")
    x, c = rows // 2, rows % 2
    y, z = cols // 4, cols % 4
    o = 1 - c

    def dev(dx=0, dc=0, dy=0, dz=0):
        r = (x + dx) % 4 * 2 + (c + dc) % 2
        q = (y + dy) % 4 * 4 + (z + dz) % 4
        return (r, q)

    xp, xm, xo = (x + 1) % 4, (x + 3) % 4, (x + 2) % 4
    yp, ym, yo = (y + 1) % 4, (y + 3) % 4, (y + 2) % 4
    mine = pl.ds(pl.multiple_of(c * CJ, CJ), CJ)
    other = pl.ds(pl.multiple_of(o * CJ, CJ), CJ)
    top, low = pl.ds(0, KI // 2), pl.ds(KI // 2, KI // 2)

    norm_moves = (
        [dev(dc=1)] + [dev(dx=d, dc=e) for d in (1, 2, 3) for e in (0, 1)],
        [dev(dy=d) for d in (1, 2, 3)],
        [dev(dz=d) for d in (1, 2, 3)],
    )
    partners = [p for moves in norm_moves for p in moves]
    barrier = pltpu.get_barrier_semaphore()
    for p in partners:
        pl.semaphore_signal(barrier, inc=1, device_id=p, device_id_type=pl.DeviceIdType.MESH)
    pl.semaphore_wait(barrier, len(partners))

    kinds, sizes, count = [], {}, [0, 0]

    def new_slot():
        count[0] += 1
        return count[0] - 1

    def send(src, dst, to, kind, slot=None):
        if kind not in kinds:
            kinds.append(kind)
            sizes[kind] = 0
        sizes[kind] += math.prod(src.shape)
        copy = pltpu.make_async_remote_copy(
            src_ref=src, dst_ref=dst, send_sem=ssem.at[kinds.index(kind)],
            recv_sem=rsem.at[new_slot() if slot is None else slot],
            device_id=to, device_id_type=pl.DeviceIdType.MESH,
        )
        copy.start()
        return copy

    def whole(ref, slot, kind=0):
        return pltpu.make_async_remote_copy(
            src_ref=ref, dst_ref=ref, send_sem=ssem.at[kind], recv_sem=rsem.at[slot],
            device_id=dev(dc=1), device_id_type=pl.DeviceIdType.MESH,
        )

    def sent(kind, *refs):
        assert sizes.pop(kind) == sum(math.prod(ref.shape) for ref in refs)
        for ref in refs:
            whole(ref, 0, kinds.index(kind)).wait_send()

    def local(src, dst):
        i = count[1]
        count[1] += 1
        copy = pltpu.make_async_copy(src, dst, lsem.at[i])
        copy.start()
        return copy

    state = {}

    def arrived(key):
        for copy in state.pop(key, ()):
            copy.wait_recv()

    def chunk(i):
        return bt.at[pl.ds(i * QJ, QJ)]

    def gg_send(h):
        lanes = pl.ds(h * HN, HN)
        rest = new_slot()
        for way, first, second in ((1, top, low), (3, low, top)):
            state["g", h, way] = [send(grad.at[first, lanes], gg.at[h, y, first], dev(dy=way), "g")]
            send(grad.at[second, lanes], gg.at[h, y, second], dev(dy=way), "g", rest)
        state["g_rest", h] = [whole(gg.at[h, y], rest)]

    gg_send(0)
    halves = [basis_t.at[pl.ds(q * QJ, QJ)] for q in range(2)]
    state["b", 3] = [send(halves[0], chunk(3), dev(dz=1), "b")]
    state["b", 2] = [send(halves[1], chunk(2), dev(dz=3), "b")]
    state["b", 5] = [send(halves[1], chunk(5), dev(dz=1), "b")]
    state["b", 4] = [send(halves[0], chunk(4), dev(dz=3), "b")]
    own_g = [local(grad.at[:, pl.ds(h * HN, HN)], gg.at[h, y]) for h in range(2)]
    own_b = [local(basis_t, bt.at[pl.ds(0, KJ)])]
    own_plain = [local(mom_plain, mp), local(var_plain, vp)]
    state["mv"] = [send(src.at[:, other], dst.at[c], dev(dc=1), "mv") for src, dst in ((mom_rot, m2), (var_rot, v2))]
    own_mv = [local(src.at[:, mine], dst.at[c]) for src, dst in ((mom_rot, m2), (var_rot, v2))]

    norm[0] = jnp.zeros((2, 8, HN), F32)
    out_plain = []

    def done(copies):
        while copies:
            copies.pop().wait()

    def plain():
        done(own_g)
        done(own_plain)

        @pl.loop(0, KI // 64)
        def _(i):
            s = pl.ds(pl.multiple_of(i * 64, 64), 64)
            for h in range(2):
                lanes = slice(h * HN, (h + 1) * HN)
                m, v, d = adam(mp[s, lanes], vp[s, lanes], gg[h, y, s, :])
                mp[s, lanes] = m
                vp[s, lanes] = v
                norm[0, 0] += jnp.sum((d * d).reshape(8, 8, HN), axis=0)

        out_plain.append(local(mp, new_mom_plain))
        out_plain.append(local(vp, new_var_plain))

    def split_grad(h, n):
        @pl.loop(0, KI // 128)
        def _(i):
            s = pl.ds(pl.multiple_of(i * 128, 128), 128)
            hi, lo = split(gg[h, n, s, :])
            ghi[h, n, s, :] = hi
            glo[h, n, s, :] = lo

    def gf(h):
        arrived(("g", h, 1))
        slot = new_slot()
        send(gg.at[h, ym, top], gg.at[h, ym, top], dev(dy=1), "g2", slot)
        arrived(("g", h, 3))
        send(gg.at[h, yp, low], gg.at[h, yp, low], dev(dy=3), "g2", slot)
        state["g2", h] = [whole(gg.at[h, yo], slot)]

    def gs(h):
        done(own_g)
        arrived(("g_rest", h))
        for n in (y, ym, yp):
            split_grad(h, n)

    def gs2(h):
        arrived(("g2", h))
        split_grad(h, yo)

    def bf(way):
        if way == 0:
            arrived(("b", 3))
            state["b", 6] = [send(chunk(3), chunk(6), dev(dz=1), "bf")]
        else:
            arrived(("b", 2))
            state["b", 7] = [send(chunk(2), chunk(7), dev(dz=3), "bf")]

    def basis_there(lo, hi):
        for i in range(lo, hi):
            if i < 2:
                done(own_b)
            arrived(("b", i))

    def away(g):
        return [i for i in range(*GROUPS[g]) if CHUNKS[i][0]]

    def ways(g):
        lo, hi = GROUPS[g]
        if hi - lo == 2:
            return [(pl.ds(lo, 1), mine), (pl.ds(lo + 1, 1), mine)]
        start = pl.multiple_of(c * CJ, CJ)
        return [
            (pl.ds(lo, 1), pl.ds(start, CJ // 2)),
            (pl.ds(lo, 1), pl.ds(pl.multiple_of(start + CJ // 2, CJ // 2), CJ // 2)),
        ]

    def ways_share(g):
        lo, hi = GROUPS[g]
        if hi - lo == 2:
            return [(pl.ds(lo, 1), pl.ds(0, CJ)), (pl.ds(lo + 1, 1), pl.ds(0, CJ))]
        return [(pl.ds(lo, 1), pl.ds(0, CJ // 2)), (pl.ds(lo, 1), pl.ds(CJ // 2, CJ // 2))]

    def s0(g, h):
        if ("x", g, h) in state:
            return
        groups = next(p for p in PRODUCTS if g in p)
        lo, hi = GROUPS[groups[0]][0], GROUPS[groups[-1]][1]
        basis_there(lo, hi)
        size = (hi - lo) * QJ
        high, rest = split(bt[lo * QJ:hi * QJ, :])
        lhi[:size, :] = high
        llo[:size, :] = rest
        rh = jnp.concatenate([ghi[h, n] for n in range(4)], axis=1)
        rl = jnp.concatenate([glo[h, n] for n in range(4)], axis=1)
        new = dot3(lhi[:size, :], llo[:size, :], rh, rl)
        for n in range(4):
            for i in range(hi - lo):
                part[h, n, lo + i] = new[i * QJ:(i + 1) * QJ, n * HN:(n + 1) * HN]
        for k in groups:
            first, end = GROUPS[k]
            group = pl.ds(first, end - first)
            state["x", k, h] = [send(part.at[h, :, group, other], rx.at[h, :, group], dev(dc=1), "x")]

    def s1(g, h):
        lo, hi = GROUPS[g]
        arrived(("x", g, h))
        group = pl.ds(lo, hi - lo)
        for n in range(4):
            part[h, n, group, mine, :] += rx[h, n, group]
        (first, up), (second, dn) = ways(g)
        (first_r, up_r), (second_r, dn_r) = ways_share(g)
        slot = new_slot()
        state["ra", g, h] = [whole(rt.at[h, pl.ds(lo, hi - lo)], slot)]
        send(part.at[h, xo, first, up], ra.at[h, 0, first_r, up_r], dev(dx=1), "ra", slot)
        send(part.at[h, xo, second, dn], ra.at[h, 1, second_r, dn_r], dev(dx=3), "ra", slot)

    def s2(g, h):
        lo, hi = GROUPS[g]
        group = pl.ds(lo, hi - lo)
        (first, up), (second, dn) = ways(g)
        (first_r, up_r), (second_r, dn_r) = ways_share(g)
        arrived(("ra", g, h))
        part[h, xp, first, up, :] += ra[h, 0, first_r, up_r, :]
        slot = new_slot()
        send(part.at[h, xp, group, mine], rb.at[h, 0, group], dev(dx=1), "rb", slot)
        part[h, xm, second, dn, :] += ra[h, 1, second_r, dn_r, :]
        send(part.at[h, xm, group, mine], rb.at[h, 1, group], dev(dx=3), "rb", slot)
        state["rb", g, h] = [whole(rb.at[h, :, group], slot)]

    def s3(g, h):
        lo, hi = GROUPS[g]
        group = pl.ds(lo, hi - lo)
        arrived(("rb", g, h))
        rt[h, group] = part[h, x, group, mine, :] + rb[h, 0, group] + rb[h, 1, group]
        for i in away(g):
            state["at", i, h] = [send(rt.at[h, i], at.at[h, i], dev(dz=CHUNKS[i][0]), "at")]

    def s4(g, h):
        arrived("mv")
        done(own_mv)
        lo, hi = GROUPS[g]
        if away(g):
            assert away(g) == list(range(lo, hi))
            slot = new_slot()
            state["d", g, h] = [whole(dd.at[h, x, pl.ds(lo, hi - lo), mine], slot)]
        for i in range(lo, hi):
            off, q = CHUNKS[i]
            arrived(("at", i, h))
            values = at[h, i] if off else rt[h, i]
            zs = (z + 4 - off) % 4
            half = zs // 2
            lanes = pl.ds(pl.multiple_of(zs % 2 * KN + h * HN, HN), HN)
            m, v, d = adam(m2[half, q, :, lanes], v2[half, q, :, lanes], values)
            m2[half, q, :, lanes] = m
            v2[half, q, :, lanes] = v
            if off:
                direc[h, i] = d
                send(direc.at[h, i], dd.at[h, x, i, mine], dev(dz=4 - off), "d", slot)
            else:
                dd[h, x, i, mine, :] = d

    def s5(g, h):
        lo, hi = GROUPS[g]
        arrived(("d", g, h))
        t = dd.at[h, x, pl.ds(lo, hi - lo), mine]
        slot = new_slot()
        send(t, t, dev(dx=1), "ag", slot)
        send(t, t, dev(dx=3), "ag", slot)
        state["ag", g, h] = [whole(rb.at[h, :, pl.ds(lo, hi - lo)], slot)]

    def s6(g, h):
        (first, up), (second, dn) = ways(g)
        arrived(("ag", g, h))
        t = dd.at[h, xm, first, up]
        slot = new_slot()
        send(t, t, dev(dx=1), "ag2", slot)
        t = dd.at[h, xp, second, dn]
        send(t, t, dev(dx=3), "ag2", slot)
        lo, hi = GROUPS[g]
        state["ag2", g, h] = [whole(dd.at[h, xo, pl.ds(lo, hi - lo), mine], slot)]

    def s7(g, h):
        lo, hi = GROUPS[g]
        arrived(("ag2", g, h))
        t = dd.at[h, :, pl.ds(lo, hi - lo), mine]
        early = hi <= 4
        if ("dc", early, h) not in state:
            slot = new_slot()
            chunks = pl.ds(0, 4) if early else pl.ds(4, 4)
            state["dc", early, h] = [whole(dd.at[h, :, chunks, other], slot)]
            state["dc_slot", early, h] = slot
        send(t, t, dev(dc=1), "dc", state["dc_slot", early, h])

    def turn(p):
        ends = (0, 3, 7, 10, 14)
        basis_there(0, 2 * p + 2)

        @pl.loop(ends[p], ends[p + 1])
        def _(b):
            s = pl.ds(pl.multiple_of(b * 128, 128), 128)
            hi, lo = split(bt[s, :].T)
            bhi[:, s] = hi
            blo[:, s] = lo

    def split_direction(h, part_of):
        @pl.loop(0, 4)
        def _(n):
            @pl.loop(0, 4)
            def _(i):
                hi, lo = split(dd[h, n, part_of * 4 + i])
                s = pl.ds(pl.multiple_of(i * QJ, QJ), QJ)
                dhi[n, s, :] = hi
                dlo[n, s, :] = lo

    def product_two(h, part_of, s):
        rh = jnp.concatenate([dhi[n] for n in range(4)], axis=1)
        rl = jnp.concatenate([dlo[n] for n in range(4)], axis=1)
        k = slice(part_of * 2 * KJ, (part_of + 1) * 2 * KJ)
        new = dot3(bhi[s, k], blo[s, k], rh, rl)
        for n in range(4):
            tile = new[:, n * HN:(n + 1) * HN]
            back[h, n, s, :] = back[h, n, s, :] + tile if part_of else tile

    def directions_there(h, lo, hi):
        arrived(("dc", hi <= 4, h))

    def ya0(h):
        directions_there(h, 0, 4)
        split_direction(h, 0)
        product_two(h, 0, pl.ds(0, KI))

    def y0(h):
        directions_there(h, 4, 8)
        split_direction(h, 1)
        product_two(h, 1, top)
        state["ya", h] = [send(back.at[h, yo, top], ya.at[h, 0], dev(dy=1), "ya")]
        slot = new_slot()
        state["yb_slot", h] = slot
        state["yb", h] = [whole(yb.at[h], slot)]
        send(back.at[h, ym, top], yb.at[h, 1, top], dev(dy=3), "yb", slot)

    def y0b(h):
        product_two(h, 1, low)
        state["ya", h].append(send(back.at[h, yo, low], ya.at[h, 1], dev(dy=3), "ya"))
        send(back.at[h, yp, low], yb.at[h, 0, low], dev(dy=1), "yb", state["yb_slot", h])

    def y1(h):
        up, dn = state.pop(("ya", h))
        up.wait_recv()
        back[h, yp, top, :] += ya[h, 0]
        slot = state["yb_slot", h]
        send(back.at[h, yp, top], yb.at[h, 0, top], dev(dy=1), "yb", slot)
        dn.wait_recv()
        back[h, ym, low, :] += ya[h, 1]
        send(back.at[h, ym, low], yb.at[h, 1, low], dev(dy=3), "yb", slot)

    out_back_copies = []

    def y2(h):
        arrived(("yb", h))

        @pl.loop(0, KI // 128)
        def _(i):
            s = pl.ds(pl.multiple_of(i * 128, 128), 128)
            b = back[h, y, s, :] + yb[h, 0, s, :] + yb[h, 1, s, :]
            back[h, y, s, :] = b
            norm[0, 1] += jnp.sum((b * b).reshape(16, 8, HN), axis=0)

        out_back_copies.append(local(back.at[h, y], out_back.at[:, pl.ds(h * HN, HN)]))

    order = (
        (turn, 0), (plain,), (gf, 0), (gs, 0), (gg_send, 1), (gs2, 0), (s0, 0, 0), (s0, 1, 0), (gf, 1),
        (s1, 0, 0), (bf, 0), (turn, 1), (s2, 0, 0), (s1, 1, 0), (gs, 1), (bf, 1), (gs2, 1), (s0, 1, 1),
        (s0, 0, 1), (s2, 1, 0), (s3, 0, 0), (s4, 0, 0), (s5, 0, 0), (s1, 1, 1), (s0, 2, 0), (s1, 0, 1),
        (s0, 2, 1), (s2, 1, 1), (s1, 2, 0), (s2, 0, 1), (s3, 1, 0), (turn, 2), (s1, 2, 1), (s2, 2, 0),
        (s6, 0, 0), (s3, 1, 1), (s0, 4, 0), (s2, 2, 1), (s0, 3, 0), (s0, 3, 1), (s1, 4, 0), (s3, 2, 0),
        (s0, 4, 1), (s1, 3, 0), (s4, 1, 0), (s2, 4, 0), (s1, 3, 1), (s3, 2, 1), (s2, 3, 0), (s4, 2, 0),
        (s1, 4, 1), (s5, 1, 0), (s3, 4, 0), (s3, 0, 1), (s2, 3, 1), (s3, 3, 0), (s7, 0, 0), (s5, 2, 0),
        (s4, 4, 0), (turn, 3), (s6, 1, 0), (s4, 3, 0), (s3, 3, 1), (s2, 4, 1), (s4, 0, 1), (s4, 2, 1),
        (s5, 4, 0), (s4, 1, 1), (s5, 3, 0), (s7, 1, 0), (s3, 4, 1), (s6, 2, 0), (s4, 3, 1), (s6, 4, 0),
        (s6, 3, 0), (s5, 0, 1), (s5, 2, 1), (s7, 2, 0), (s5, 1, 1), (s7, 4, 0), (s4, 4, 1), (s7, 3, 0),
        (ya0, 0), (s6, 0, 1), (s5, 4, 1), (y0, 0), (s6, 1, 1), (s7, 0, 1), (s5, 3, 1), (s6, 2, 1), (y0b, 0),
        (s7, 1, 1), (s6, 4, 1), (s6, 3, 1), (s7, 2, 1), (s7, 4, 1), (y1, 0), (s7, 3, 1), (ya0, 1), (y0, 1),
        (y0b, 1), (y1, 1), (y2, 0), (y2, 1),
    )
    adams_left = 2 * len(GROUPS)
    out_rot, out_rot_own = [], []
    for stage, *step in order:
        stage(*step)
        if stage is s4:
            adams_left -= 1
            if adams_left == 0:
                for src, dst in ((m2, new_mom_rot), (v2, new_var_rot)):
                    out_rot.append(send(src.at[o], dst.at[:, mine], dev(dc=1), "out"))
                    out_rot_own.append(local(src.at[c], dst.at[:, mine]))

    first = 0
    for k, moves in enumerate(norm_moves):
        slot = new_slot()
        end = first + len(moves)
        for i, to in enumerate(moves):
            send(norm.at[k], nrecv.at[first + i], to, ("norm", k), slot)
        whole(nrecv.at[pl.ds(first, len(moves))], slot).wait_recv()
        total = norm[k]
        for i in range(first, end):
            total += nrecv[i]
        norm[k + 1] = total
        first = end
    last = local(norm.at[len(norm_moves)], out_norm)
    assert count[0] <= N_COPIES and count[1] <= 16

    share = rt
    away_share = rt.at[:, pl.ds(2, 6)]
    sent("g", gg.at[:, pl.ds(0, 2)])
    sent("g2", gg.at[:, 0])
    sent("b", bt.at[pl.ds(0, 2 * KJ)])
    sent("bf", bt.at[pl.ds(0, KJ)])
    sent("mv", m2.at[0], v2.at[0])
    sent("x", rx)
    sent("ra", share)
    sent("rb", rb)
    sent("at", away_share)
    sent("d", away_share)
    sent("ag", rb)
    sent("ag2", share)
    sent("dc", rx)
    sent("ya", ya)
    sent("yb", yb)
    sent("out", m2.at[0], v2.at[0])
    first = 0
    for k, moves in enumerate(norm_moves):
        sent(("norm", k), nrecv.at[pl.ds(first, len(moves))])
        first += len(moves)
    assert not sizes
    for copy in out_rot:
        copy.wait_recv()
    for copy in out_rot_own + out_plain + out_back_copies:
        copy.wait()
    last.wait()


def finish(back, norm, *refs):
    sources, outs = (*refs[:4], back), (*refs[5:9], refs[4])
    held_rot, held, norm_v, in_sems, out_sems = refs[9:]
    norm_in = pltpu.make_async_copy(norm, norm_v, in_sems.at[10])
    norm_in.start()
    pieces = []
    for i in range(5):
        for h in range(2):
            if i < 2:
                src, dst, here = sources[i].at[h], outs[i].at[h], held_rot.at[i, h]
            else:
                s = pl.ds(h * KJ, KJ)
                src, dst, here = sources[i].at[s], outs[i].at[s], held.at[i - 2, h]
            pieces.append((pltpu.make_async_copy(src, here, in_sems.at[2 * i + h]),
                           pltpu.make_async_copy(here, dst, out_sems.at[2 * i + h])))
    for into, _ in pieces:
        into.start()
    norm_in.wait()
    graft = jnp.sqrt(jnp.sum(norm_v[0], keepdims=True))
    own = jnp.sqrt(jnp.sum(norm_v[1], keepdims=True))
    scale = graft / (own + 1e-06)
    for k, (into, out) in enumerate(pieces):
        into.wait()
        if k >= 8:
            held[2, k - 8] = held[2, k - 8] * scale
        out.start()
    for _, out in pieces:
        out.wait()


def per_device(grad, basis, mom_rot, var_rot, mom_plain, var_plain):
    plain = jax.ShapeDtypeStruct((KI, KN), F32)
    rot = jax.ShapeDtypeStruct((2, QJ, 2 * KN), F32)
    norms = jax.ShapeDtypeStruct((2, 8, HN), F32)
    scratch = [
        pltpu.VMEM((2, 4, KI, HN), F32),
        pltpu.VMEM((2, 4, KI, HN), BF16),
        pltpu.VMEM((2, 4, KI, HN), BF16),
        pltpu.VMEM((4 * KJ, KI), F32),
        pltpu.VMEM((2 * KJ, KI), BF16),
        pltpu.VMEM((2 * KJ, KI), BF16),
        pltpu.VMEM((KI, 4 * KJ), BF16),
        pltpu.VMEM((KI, 4 * KJ), BF16),
        pltpu.VMEM((2, 4, 8, QJ, HN), F32),
        pltpu.VMEM((2, 4, 8, CJ, HN), F32),
        pltpu.VMEM((2, 2, 8, CJ, HN), F32),
        pltpu.VMEM((2, 2, 8, CJ, HN), F32),
        pltpu.VMEM((2, 8, CJ, HN), F32),
        pltpu.VMEM((2, 8, CJ, HN), F32),
        pltpu.VMEM((2, 2, CJ, 2 * KN), F32),
        pltpu.VMEM((2, 2, CJ, 2 * KN), F32),
        pltpu.VMEM((2, 8, CJ, HN), F32),
        pltpu.VMEM((2, 4, 8, QJ, HN), F32),
        pltpu.VMEM((4, 2 * KJ, HN), BF16),
        pltpu.VMEM((4, 2 * KJ, HN), BF16),
        pltpu.VMEM((2, 4, KI, HN), F32),
        pltpu.VMEM((2, 2, KI // 2, HN), F32),
        pltpu.VMEM((2, 2, KI, HN), F32),
        pltpu.VMEM((KI, KN), F32),
        pltpu.VMEM((KI, KN), F32),
        pltpu.VMEM((4, 2, 8, HN), F32),
        pltpu.VMEM((13, 2, 8, HN), F32),
        pltpu.SemaphoreType.DMA((24,)),
        pltpu.SemaphoreType.DMA((N_COPIES,)),
        pltpu.SemaphoreType.DMA((16,)),
    ]
    anywhere = pl.BlockSpec(memory_space=pl.ANY)
    out = pl.pallas_call(
        kernel,
        out_shape=(plain, norms, rot, rot, plain, plain),
        in_specs=[anywhere] * 6,
        out_specs=[anywhere] * 6,
        scratch_shapes=scratch,
        compiler_params=pltpu.CompilerParams(
            collective_id=0, has_side_effects=True, vmem_limit_bytes=63 * 1024 * 1024
        ),
        cost_estimate=pl.CostEstimate(flops=20_000_000_000, bytes_accessed=12_000_000, transcendentals=0),
    )(grad, basis.T, mom_rot.reshape(2, QJ, 2 * KN), var_rot.reshape(2, QJ, 2 * KN), mom_plain, var_plain)
    update, new_mom_rot, new_var_rot, new_mom_plain, new_var_plain = pl.pallas_call(
        finish,
        out_shape=(plain, rot, rot, plain, plain),
        in_specs=[anywhere] * 6,
        out_specs=[anywhere] * 5,
        scratch_shapes=[
            pltpu.VMEM((2, 2, QJ, 2 * KN), F32),
            pltpu.VMEM((3, 2, KJ, KN), F32),
            pltpu.VMEM((2, 8, HN), F32),
            pltpu.SemaphoreType.DMA((11,)),
            pltpu.SemaphoreType.DMA((10,)),
        ],
        compiler_params=pltpu.CompilerParams(vmem_limit_bytes=60 * 1024 * 1024),
        cost_estimate=pl.CostEstimate(flops=1_000_000, bytes_accessed=9_000_000, transcendentals=0),
    )(*out)
    return (
        update,
        new_mom_rot.reshape(KJ, 2 * KN),
        new_var_rot.reshape(KJ, 2 * KN),
        new_mom_plain,
        new_var_plain,
    )


def solution(mesh):
    return jax.shard_map(
        per_device,
        mesh=mesh,
        in_specs=(
            P("rows", "cols"),
            P("rows", "cols"),
            P("cols", "rows"),
            P("cols", "rows"),
            P("rows", "cols"),
            P("rows", "cols"),
        ),
        out_specs=(
            P("rows", "cols"),
            P("cols", "rows"),
            P("cols", "rows"),
            P("rows", "cols"),
            P("rows", "cols"),
        ),
        check_vma=False,
    )
```

```python
import math

import jax
import jax.numpy as jnp
from jax import lax
from jax.experimental import pallas as pl
from jax.experimental.pallas import tpu as pltpu
from jax.sharding import PartitionSpec as P

STEP = 10
BETA = 0.95
EPS = 1e-08
CORR = 1.0 - BETA**STEP

F32 = jnp.float32
BF16 = jnp.bfloat16

KI = 896
KJ = 448
KN = 256
QJ = KJ // 2
HN = KN // 2
CJ = QJ // 2
CHUNKS = ((0, 0), (0, 1), (1, 1), (3, 0), (1, 0), (3, 1), (2, 0), (2, 1))
GROUPS = ((0, 2), (2, 4), (4, 6), (6, 7), (7, 8))
PRODUCTS = ((0,), (1,), (2,), (3, 4))
N_COPIES = 128


def adam(moment, second, values):
    moment_new = BETA * moment + (1.0 - BETA) * values
    second_new = BETA * second + (1.0 - BETA) * values * values
    direction = moment_new / CORR / (jnp.sqrt(second_new / CORR) + EPS)
    return moment_new, second_new, direction


def split(a):
    hi = a.astype(BF16)
    lo = (a - hi.astype(F32)).astype(BF16)
    return hi, lo


def dot3(lh, ll, rh, rl):
    left = jnp.concatenate([lh, lh, ll], axis=1)
    right = jnp.concatenate([rh, rl, rh], axis=0)
    return jnp.dot(left, right, preferred_element_type=F32)


def kernel(
    grad, basis_t, mom_rot, var_rot, mom_plain, var_plain,
    out_back, out_norm, new_mom_rot, new_var_rot, new_mom_plain, new_var_plain,
    gg, ghi, glo, bt, lhi, llo, bhi, blo, part, rx, ra, rb, rt, at,
    m2, v2, direc, dd, dhi, dlo, back, ya, yb, mp, vp, norm, nrecv,
    ssem, rsem, lsem,
):
    rows = lax.axis_index("rows")
    cols = lax.axis_index("cols")
    x, c = rows // 2, rows % 2
    y, z = cols // 4, cols % 4
    o = 1 - c

    def dev(dx=0, dc=0, dy=0, dz=0):
        r = (x + dx) % 4 * 2 + (c + dc) % 2
        q = (y + dy) % 4 * 4 + (z + dz) % 4
        return (r, q)

    yp, ym, yo = (y + 1) % 4, (y + 3) % 4, (y + 2) % 4
    mine = pl.ds(pl.multiple_of(c * CJ, CJ), CJ)
    other = pl.ds(pl.multiple_of(o * CJ, CJ), CJ)
    top, low = pl.ds(0, KI // 2), pl.ds(KI // 2, KI // 2)

    norm_moves = (
        [dev(dc=1)] + [dev(dx=d, dc=e) for d in (1, 2, 3) for e in (0, 1)],
        [dev(dy=d) for d in (1, 2, 3)],
        [dev(dz=d) for d in (1, 2, 3)],
    )
    partners = [p for moves in norm_moves for p in moves]
    barrier = pltpu.get_barrier_semaphore()
    for p in partners:
        pl.semaphore_signal(barrier, inc=1, device_id=p, device_id_type=pl.DeviceIdType.MESH)
    pl.semaphore_wait(barrier, len(partners))

    kinds, sizes, count = [], {}, [0, 0]

    def new_slot():
        count[0] += 1
        return count[0] - 1

    def send(src, dst, to, kind, slot=None):
        if kind not in kinds:
            kinds.append(kind)
            sizes[kind] = 0
        sizes[kind] += math.prod(src.shape)
        copy = pltpu.make_async_remote_copy(
            src_ref=src, dst_ref=dst, send_sem=ssem.at[kinds.index(kind)],
            recv_sem=rsem.at[new_slot() if slot is None else slot],
            device_id=to, device_id_type=pl.DeviceIdType.MESH,
        )
        copy.start()
        return copy

    def whole(ref, slot, kind=0):
        return pltpu.make_async_remote_copy(
            src_ref=ref, dst_ref=ref, send_sem=ssem.at[kind], recv_sem=rsem.at[slot],
            device_id=dev(dc=1), device_id_type=pl.DeviceIdType.MESH,
        )

    def sent(kind, *refs):
        assert sizes.pop(kind) == sum(math.prod(ref.shape) for ref in refs)
        for ref in refs:
            whole(ref, 0, kinds.index(kind)).wait_send()

    def local(src, dst):
        i = count[1]
        count[1] += 1
        copy = pltpu.make_async_copy(src, dst, lsem.at[i])
        copy.start()
        return copy

    state = {}

    def arrived(key):
        for copy in state.pop(key, ()):
            copy.wait_recv()

    def chunk(i):
        return bt.at[pl.ds(i * QJ, QJ)]

    def gg_send(h):
        lanes = pl.ds(h * HN, HN)
        rest = new_slot()
        for way, first, second in ((1, top, low), (3, low, top)):
            state["g", h, way] = [send(grad.at[first, lanes], gg.at[h, y, first], dev(dy=way), "g")]
            send(grad.at[second, lanes], gg.at[h, y, second], dev(dy=way), "g", rest)
        state["g_rest", h] = [whole(gg.at[h, y], rest)]

    gg_send(0)
    halves = [basis_t.at[pl.ds(q * QJ, QJ)] for q in range(2)]
    state["b", 3] = [send(halves[0], chunk(3), dev(dz=1), "b")]
    state["b", 2] = [send(halves[1], chunk(2), dev(dz=3), "b")]
    state["b", 5] = [send(halves[1], chunk(5), dev(dz=1), "b")]
    state["b", 4] = [send(halves[0], chunk(4), dev(dz=3), "b")]
    own_g = [local(grad.at[:, pl.ds(h * HN, HN)], gg.at[h, y]) for h in range(2)]
    own_b = [local(basis_t, bt.at[pl.ds(0, KJ)])]
    own_plain = [local(mom_plain, mp), local(var_plain, vp)]
    state["mv"] = [send(src.at[:, other], dst.at[c], dev(dc=1), "mv") for src, dst in ((mom_rot, m2), (var_rot, v2))]
    own_mv = [local(src.at[:, mine], dst.at[c]) for src, dst in ((mom_rot, m2), (var_rot, v2))]

    norm[0] = jnp.zeros((2, 8, HN), F32)
    out_plain = []

    def done(copies):
        while copies:
            copies.pop().wait()

    def plain():
        done(own_g)
        done(own_plain)

        @pl.loop(0, KI // 64)
        def _(i):
            s = pl.ds(pl.multiple_of(i * 64, 64), 64)
            for h in range(2):
                lanes = slice(h * HN, (h + 1) * HN)
                m, v, d = adam(mp[s, lanes], vp[s, lanes], gg[h, y, s, :])
                mp[s, lanes] = m
                vp[s, lanes] = v
                norm[0, 0] += jnp.sum((d * d).reshape(8, 8, HN), axis=0)

        out_plain.append(local(mp, new_mom_plain))
        out_plain.append(local(vp, new_var_plain))

    def split_grad(h, n):
        @pl.loop(0, KI // 128)
        def _(i):
            s = pl.ds(pl.multiple_of(i * 128, 128), 128)
            hi, lo = split(gg[h, n, s, :])
            ghi[h, n, s, :] = hi
            glo[h, n, s, :] = lo

    def gf(h):
        arrived(("g", h, 1))
        slot = new_slot()
        send(gg.at[h, ym, top], gg.at[h, ym, top], dev(dy=1), "g2", slot)
        arrived(("g", h, 3))
        send(gg.at[h, yp, low], gg.at[h, yp, low], dev(dy=3), "g2", slot)
        state["g2", h] = [whole(gg.at[h, yo], slot)]

    def gs(h):
        done(own_g)
        arrived(("g_rest", h))
        for n in (y, ym, yp):
            split_grad(h, n)

    def gs2(h):
        arrived(("g2", h))
        split_grad(h, yo)

    def bf(way):
        if way == 0:
            arrived(("b", 3))
            state["b", 6] = [send(chunk(3), chunk(6), dev(dz=1), "bf")]
        else:
            arrived(("b", 2))
            state["b", 7] = [send(chunk(2), chunk(7), dev(dz=3), "bf")]

    def basis_there(lo, hi):
        for i in range(lo, hi):
            if i < 2:
                done(own_b)
            arrived(("b", i))

    def away(g):
        return [i for i in range(*GROUPS[g]) if CHUNKS[i][0]]

    def ways(g):
        lo, hi = GROUPS[g]
        if hi - lo == 2:
            return [(pl.ds(lo, 1), mine), (pl.ds(lo + 1, 1), mine)]
        start = pl.multiple_of(c * CJ, CJ)
        return [
            (pl.ds(lo, 1), pl.ds(start, CJ // 2)),
            (pl.ds(lo, 1), pl.ds(pl.multiple_of(start + CJ // 2, CJ // 2), CJ // 2)),
        ]

    def ways_share(g):
        lo, hi = GROUPS[g]
        if hi - lo == 2:
            return [(pl.ds(lo, 1), pl.ds(0, CJ)), (pl.ds(lo + 1, 1), pl.ds(0, CJ))]
        return [(pl.ds(lo, 1), pl.ds(0, CJ // 2)), (pl.ds(lo, 1), pl.ds(CJ // 2, CJ // 2))]

    def place(n):
        d = (n + 4 - x) % 4
        return d + d // 2 * (1 - 2 * (d % 2))

    def s0(g, h):
        if ("x", g, h) in state:
            return
        groups = next(p for p in PRODUCTS if g in p)
        lo, hi = GROUPS[groups[0]][0], GROUPS[groups[-1]][1]
        basis_there(lo, hi)
        size = (hi - lo) * QJ
        high, rest = split(bt[lo * QJ:hi * QJ, :])
        lhi[:size, :] = high
        llo[:size, :] = rest
        rh = jnp.concatenate([ghi[h, n] for n in range(4)], axis=1)
        rl = jnp.concatenate([glo[h, n] for n in range(4)], axis=1)
        new = dot3(lhi[:size, :], llo[:size, :], rh, rl)
        for n in range(4):
            for i in range(hi - lo):
                part[h, place(n), lo + i] = new[i * QJ:(i + 1) * QJ, n * HN:(n + 1) * HN]
        for k in groups:
            first, end = GROUPS[k]
            group = pl.ds(first, end - first)
            state["xo", k, h] = [send(part.at[h, 3, group, other], rx.at[h, 3, group], dev(dc=1), "x")]
            near = pl.ds(0, 3)
            state["x", k, h] = [send(part.at[h, near, group, other], rx.at[h, near, group], dev(dc=1), "x")]

    def s1(g, h):
        lo, hi = GROUPS[g]
        arrived(("xo", g, h))
        group = pl.ds(lo, hi - lo)
        part[h, 3, group, mine, :] += rx[h, 3, group]
        (first, up), (second, dn) = ways(g)
        (first_r, up_r), (second_r, dn_r) = ways_share(g)
        slot = new_slot()
        state["ra", g, h] = [whole(rt.at[h, pl.ds(lo, hi - lo)], slot)]
        send(part.at[h, 3, first, up], ra.at[h, 0, first_r, up_r], dev(dx=1), "ra", slot)
        send(part.at[h, 3, second, dn], ra.at[h, 1, second_r, dn_r], dev(dx=3), "ra", slot)

    def s2(g, h):
        lo, hi = GROUPS[g]
        group = pl.ds(lo, hi - lo)
        (first, up), (second, dn) = ways(g)
        (first_r, up_r), (second_r, dn_r) = ways_share(g)
        arrived(("x", g, h))
        for n in range(3):
            part[h, n, group, mine, :] += rx[h, n, group]
        arrived(("ra", g, h))
        part[h, 1, first, up, :] += ra[h, 0, first_r, up_r, :]
        slot = new_slot()
        send(part.at[h, 1, group, mine], rb.at[h, 0, group], dev(dx=1), "rb", slot)
        part[h, 2, second, dn, :] += ra[h, 1, second_r, dn_r, :]
        send(part.at[h, 2, group, mine], rb.at[h, 1, group], dev(dx=3), "rb", slot)
        state["rb", g, h] = [whole(rb.at[h, :, group], slot)]

    def s3(g, h):
        lo, hi = GROUPS[g]
        group = pl.ds(lo, hi - lo)
        arrived(("rb", g, h))
        rt[h, group] = part[h, 0, group, mine, :] + rb[h, 0, group] + rb[h, 1, group]
        for i in away(g):
            state["at", i, h] = [send(rt.at[h, i], at.at[h, i], dev(dz=CHUNKS[i][0]), "at")]

    def s4(g, h):
        arrived("mv")
        done(own_mv)
        lo, hi = GROUPS[g]
        if away(g):
            assert away(g) == list(range(lo, hi))
            slot = new_slot()
            state["d", g, h] = [whole(dd.at[h, 0, pl.ds(lo, hi - lo), mine], slot)]
        for i in range(lo, hi):
            off, q = CHUNKS[i]
            arrived(("at", i, h))
            values = at[h, i] if off else rt[h, i]
            zs = (z + 4 - off) % 4
            half = zs // 2
            lanes = pl.ds(pl.multiple_of(zs % 2 * KN + h * HN, HN), HN)
            m, v, d = adam(m2[half, q, :, lanes], v2[half, q, :, lanes], values)
            m2[half, q, :, lanes] = m
            v2[half, q, :, lanes] = v
            if off:
                direc[h, i] = d
                send(direc.at[h, i], dd.at[h, 0, i, mine], dev(dz=4 - off), "d", slot)
            else:
                dd[h, 0, i, mine, :] = d

    def s5(g, h):
        lo, hi = GROUPS[g]
        group = pl.ds(lo, hi - lo)
        arrived(("d", g, h))
        t = dd.at[h, 0, group, mine]
        slot = new_slot()
        send(t, dd.at[h, 2, group, mine], dev(dx=1), "ag", slot)
        send(t, dd.at[h, 1, group, mine], dev(dx=3), "ag", slot)
        state["ag", g, h] = [whole(dd.at[h, pl.ds(1, 2), group, mine], slot)]

    def to_other_core(g, h, first, blocks):
        lo, hi = GROUPS[g]
        early = hi <= 4
        if ("dc", early, h) not in state:
            slot = new_slot()
            chunks = pl.ds(0, 4) if early else pl.ds(4, 4)
            state["dc", early, h] = [whole(dd.at[h, :, chunks, other], slot)]
            state["dc_slot", early, h] = slot
        t = dd.at[h, pl.ds(first, blocks), pl.ds(lo, hi - lo), mine]
        send(t, t, dev(dc=1), "dc", state["dc_slot", early, h])

    def s6(g, h):
        lo, hi = GROUPS[g]
        (first, up), (second, dn) = ways(g)
        arrived(("ag", g, h))
        slot = new_slot()
        send(dd.at[h, 2, first, up], dd.at[h, 3, first, up], dev(dx=1), "ag2", slot)
        send(dd.at[h, 1, second, dn], dd.at[h, 3, second, dn], dev(dx=3), "ag2", slot)
        state["ag2", g, h] = [whole(dd.at[h, 3, pl.ds(lo, hi - lo), mine], slot)]
        to_other_core(g, h, 0, 3)

    def s7(g, h):
        arrived(("ag2", g, h))
        to_other_core(g, h, 3, 1)

    def turn(p):
        ends = (0, 3, 7, 10, 14)
        basis_there(0, 2 * p + 2)

        @pl.loop(ends[p], ends[p + 1])
        def _(b):
            s = pl.ds(pl.multiple_of(b * 128, 128), 128)
            hi, lo = split(bt[s, :].T)
            bhi[:, s] = hi
            blo[:, s] = lo

    def split_direction(h, part_of):
        @pl.loop(0, 4)
        def _(n):
            here = place(n)

            @pl.loop(0, 4)
            def _(i):
                hi, lo = split(dd[h, here, part_of * 4 + i])
                s = pl.ds(pl.multiple_of(i * QJ, QJ), QJ)
                dhi[n, s, :] = hi
                dlo[n, s, :] = lo

    def product_two(h, part_of, s):
        rh = jnp.concatenate([dhi[n] for n in range(4)], axis=1)
        rl = jnp.concatenate([dlo[n] for n in range(4)], axis=1)
        k = slice(part_of * 2 * KJ, (part_of + 1) * 2 * KJ)
        new = dot3(bhi[s, k], blo[s, k], rh, rl)
        for n in range(4):
            tile = new[:, n * HN:(n + 1) * HN]
            back[h, n, s, :] = back[h, n, s, :] + tile if part_of else tile

    def directions_there(h, lo, hi):
        arrived(("dc", hi <= 4, h))

    def ya0(h):
        directions_there(h, 0, 4)
        split_direction(h, 0)
        product_two(h, 0, pl.ds(0, KI))

    def y0(h):
        directions_there(h, 4, 8)
        split_direction(h, 1)
        product_two(h, 1, top)
        state["ya", h] = [send(back.at[h, yo, top], ya.at[h, 0], dev(dy=1), "ya")]
        slot = new_slot()
        state["yb_slot", h] = slot
        state["yb", h] = [whole(yb.at[h], slot)]
        send(back.at[h, ym, top], yb.at[h, 1, top], dev(dy=3), "yb", slot)

    def y0b(h):
        product_two(h, 1, low)
        state["ya", h].append(send(back.at[h, yo, low], ya.at[h, 1], dev(dy=3), "ya"))
        send(back.at[h, yp, low], yb.at[h, 0, low], dev(dy=1), "yb", state["yb_slot", h])

    def y1(h):
        up, dn = state.pop(("ya", h))
        up.wait_recv()
        back[h, yp, top, :] += ya[h, 0]
        slot = state["yb_slot", h]
        send(back.at[h, yp, top], yb.at[h, 0, top], dev(dy=1), "yb", slot)
        dn.wait_recv()
        back[h, ym, low, :] += ya[h, 1]
        send(back.at[h, ym, low], yb.at[h, 1, low], dev(dy=3), "yb", slot)

    out_back_copies = []

    def y2(h):
        arrived(("yb", h))

        @pl.loop(0, KI // 128)
        def _(i):
            s = pl.ds(pl.multiple_of(i * 128, 128), 128)
            b = back[h, y, s, :] + yb[h, 0, s, :] + yb[h, 1, s, :]
            back[h, y, s, :] = b
            norm[0, 1] += jnp.sum((b * b).reshape(16, 8, HN), axis=0)

        out_back_copies.append(local(back.at[h, y], out_back.at[:, pl.ds(h * HN, HN)]))

    order = (
        (gf, 0), (turn, 0), (gg_send, 1), (gs, 0), (gs2, 0), (s0, 0, 0), (bf, 1), (s1, 0, 0), (gf, 1),
        (s2, 0, 0), (turn, 1), (s0, 1, 0), (s3, 0, 0), (s1, 1, 0), (gs, 1), (s4, 0, 0), (s5, 0, 0), (gs2, 1),
        (s0, 0, 1), (s2, 1, 0), (bf, 0), (s0, 1, 1), (s1, 0, 1), (s0, 2, 0), (s6, 0, 0), (s1, 1, 1),
        (s2, 0, 1), (s1, 2, 0), (s2, 1, 1), (s0, 2, 1), (turn, 2), (s3, 0, 1), (s3, 1, 0), (s1, 2, 1),
        (s7, 0, 0), (s2, 2, 0), (s4, 0, 1), (s5, 0, 1), (s3, 1, 1), (s2, 2, 1), (s3, 2, 0), (s0, 3, 0),
        (s0, 4, 0), (s1, 3, 0), (s4, 1, 0), (s3, 2, 1), (s1, 4, 0), (s2, 3, 0), (s4, 2, 0), (s2, 4, 0),
        (s5, 1, 0), (s3, 3, 0), (s0, 4, 1), (s5, 2, 0), (s3, 4, 0), (s0, 3, 1), (s4, 3, 0), (turn, 3),
        (s6, 1, 0), (s1, 4, 1), (s4, 4, 0), (s4, 1, 1), (s4, 2, 1), (s5, 3, 0), (s1, 3, 1), (s7, 1, 0),
        (s2, 4, 1), (s5, 4, 0), (s6, 2, 0), (s6, 3, 0), (ya0, 0), (s6, 4, 0), (s2, 3, 1), (s7, 2, 0),
        (s3, 4, 1), (s5, 1, 1), (s7, 3, 0), (s7, 4, 0), (s6, 0, 1), (s3, 3, 1), (y0, 0), (s6, 1, 1),
        (s4, 4, 1), (s4, 3, 1), (s5, 2, 1), (y0b, 0), (s7, 1, 1), (s7, 0, 1), (s5, 4, 1), (s6, 2, 1),
        (s5, 3, 1), (ya0, 1), (s7, 2, 1), (s6, 3, 1), (s6, 4, 1), (y1, 0), (s7, 3, 1), (s7, 4, 1), (y0, 1),
        (y2, 0), (y0b, 1), (y1, 1), (plain,), (y2, 1),
    )
    adams_left = 2 * len(GROUPS)
    out_rot, out_rot_own = [], []
    for stage, *step in order:
        stage(*step)
        if stage is s4:
            adams_left -= 1
            if adams_left == 0:
                for src, dst in ((m2, new_mom_rot), (v2, new_var_rot)):
                    out_rot.append(send(src.at[o], dst.at[:, mine], dev(dc=1), "out"))
                    out_rot_own.append(local(src.at[c], dst.at[:, mine]))

    first = 0
    for k, moves in enumerate(norm_moves):
        slot = new_slot()
        end = first + len(moves)
        for i, to in enumerate(moves):
            send(norm.at[k], nrecv.at[first + i], to, ("norm", k), slot)
        whole(nrecv.at[pl.ds(first, len(moves))], slot).wait_recv()
        total = norm[k]
        for i in range(first, end):
            total += nrecv[i]
        norm[k + 1] = total
        first = end
    last = local(norm.at[len(norm_moves)], out_norm)
    assert count[0] <= N_COPIES and count[1] <= 16

    share = rt
    away_share = rt.at[:, pl.ds(2, 6)]
    sent("g", gg.at[:, pl.ds(0, 2)])
    sent("g2", gg.at[:, 0])
    sent("b", bt.at[pl.ds(0, 2 * KJ)])
    sent("bf", bt.at[pl.ds(0, KJ)])
    sent("mv", m2.at[0], v2.at[0])
    sent("x", rx)
    sent("ra", share)
    sent("rb", rb)
    sent("at", away_share)
    sent("d", away_share)
    sent("ag", rb)
    sent("ag2", share)
    sent("dc", rx)
    sent("ya", ya)
    sent("yb", yb)
    sent("out", m2.at[0], v2.at[0])
    first = 0
    for k, moves in enumerate(norm_moves):
        sent(("norm", k), nrecv.at[pl.ds(first, len(moves))])
        first += len(moves)
    assert not sizes
    for copy in out_rot:
        copy.wait_recv()
    for copy in out_rot_own + out_plain + out_back_copies:
        copy.wait()
    last.wait()


def finish(back, norm, *refs):
    sources, outs = (*refs[:4], back), (*refs[5:9], refs[4])
    held_rot, held, norm_v, in_sems, out_sems = refs[9:]
    norm_in = pltpu.make_async_copy(norm, norm_v, in_sems.at[10])
    norm_in.start()
    pieces = []
    for i in range(5):
        for h in range(2):
            if i < 2:
                src, dst, here = sources[i].at[h], outs[i].at[h], held_rot.at[i, h]
            else:
                s = pl.ds(h * KJ, KJ)
                src, dst, here = sources[i].at[s], outs[i].at[s], held.at[i - 2, h]
            pieces.append((pltpu.make_async_copy(src, here, in_sems.at[2 * i + h]),
                           pltpu.make_async_copy(here, dst, out_sems.at[2 * i + h])))
    for into, _ in pieces:
        into.start()
    norm_in.wait()
    graft = jnp.sqrt(jnp.sum(norm_v[0], keepdims=True))
    own = jnp.sqrt(jnp.sum(norm_v[1], keepdims=True))
    scale = graft / (own + 1e-06)
    for k, (into, out) in enumerate(pieces):
        into.wait()
        if k >= 8:
            held[2, k - 8] = held[2, k - 8] * scale
        out.start()
    for _, out in pieces:
        out.wait()


def per_device(grad, basis, mom_rot, var_rot, mom_plain, var_plain):
    plain = jax.ShapeDtypeStruct((KI, KN), F32)
    rot = jax.ShapeDtypeStruct((2, QJ, 2 * KN), F32)
    norms = jax.ShapeDtypeStruct((2, 8, HN), F32)
    scratch = [
        pltpu.VMEM((2, 4, KI, HN), F32),
        pltpu.VMEM((2, 4, KI, HN), BF16),
        pltpu.VMEM((2, 4, KI, HN), BF16),
        pltpu.VMEM((4 * KJ, KI), F32),
        pltpu.VMEM((2 * KJ, KI), BF16),
        pltpu.VMEM((2 * KJ, KI), BF16),
        pltpu.VMEM((KI, 4 * KJ), BF16),
        pltpu.VMEM((KI, 4 * KJ), BF16),
        pltpu.VMEM((2, 4, 8, QJ, HN), F32),
        pltpu.VMEM((2, 4, 8, CJ, HN), F32),
        pltpu.VMEM((2, 2, 8, CJ, HN), F32),
        pltpu.VMEM((2, 2, 8, CJ, HN), F32),
        pltpu.VMEM((2, 8, CJ, HN), F32),
        pltpu.VMEM((2, 8, CJ, HN), F32),
        pltpu.VMEM((2, 2, CJ, 2 * KN), F32),
        pltpu.VMEM((2, 2, CJ, 2 * KN), F32),
        pltpu.VMEM((2, 8, CJ, HN), F32),
        pltpu.VMEM((2, 4, 8, QJ, HN), F32),
        pltpu.VMEM((4, 2 * KJ, HN), BF16),
        pltpu.VMEM((4, 2 * KJ, HN), BF16),
        pltpu.VMEM((2, 4, KI, HN), F32),
        pltpu.VMEM((2, 2, KI // 2, HN), F32),
        pltpu.VMEM((2, 2, KI, HN), F32),
        pltpu.VMEM((KI, KN), F32),
        pltpu.VMEM((KI, KN), F32),
        pltpu.VMEM((4, 2, 8, HN), F32),
        pltpu.VMEM((13, 2, 8, HN), F32),
        pltpu.SemaphoreType.DMA((24,)),
        pltpu.SemaphoreType.DMA((N_COPIES,)),
        pltpu.SemaphoreType.DMA((16,)),
    ]
    anywhere = pl.BlockSpec(memory_space=pl.ANY)
    out = pl.pallas_call(
        kernel,
        out_shape=(plain, norms, rot, rot, plain, plain),
        in_specs=[anywhere] * 6,
        out_specs=[anywhere] * 6,
        scratch_shapes=scratch,
        compiler_params=pltpu.CompilerParams(
            collective_id=0, has_side_effects=True, vmem_limit_bytes=63 * 1024 * 1024
        ),
        cost_estimate=pl.CostEstimate(flops=20_000_000_000, bytes_accessed=12_000_000, transcendentals=0),
    )(grad, basis.T, mom_rot.reshape(2, QJ, 2 * KN), var_rot.reshape(2, QJ, 2 * KN), mom_plain, var_plain)
    update, new_mom_rot, new_var_rot, new_mom_plain, new_var_plain = pl.pallas_call(
        finish,
        out_shape=(plain, rot, rot, plain, plain),
        in_specs=[anywhere] * 6,
        out_specs=[anywhere] * 5,
        scratch_shapes=[
            pltpu.VMEM((2, 2, QJ, 2 * KN), F32),
            pltpu.VMEM((3, 2, KJ, KN), F32),
            pltpu.VMEM((2, 8, HN), F32),
            pltpu.SemaphoreType.DMA((11,)),
            pltpu.SemaphoreType.DMA((10,)),
        ],
        compiler_params=pltpu.CompilerParams(vmem_limit_bytes=60 * 1024 * 1024),
        cost_estimate=pl.CostEstimate(flops=1_000_000, bytes_accessed=9_000_000, transcendentals=0),
    )(*out)
    return (
        update,
        new_mom_rot.reshape(KJ, 2 * KN),
        new_var_rot.reshape(KJ, 2 * KN),
        new_mom_plain,
        new_var_plain,
    )


def solution(mesh):
    return jax.shard_map(
        per_device,
        mesh=mesh,
        in_specs=(
            P("rows", "cols"),
            P("rows", "cols"),
            P("cols", "rows"),
            P("cols", "rows"),
            P("rows", "cols"),
            P("rows", "cols"),
        ),
        out_specs=(
            P("rows", "cols"),
            P("cols", "rows"),
            P("cols", "rows"),
            P("rows", "cols"),
            P("rows", "cols"),
        ),
        check_vma=False,
    )
```

```python
import math

import jax
import jax.numpy as jnp
from jax import lax
from jax.experimental import pallas as pl
from jax.experimental.pallas import tpu as pltpu
from jax.sharding import PartitionSpec as P

STEP = 10
BETA = 0.95
EPS = 1e-08
CORR = 1.0 - BETA**STEP

F32 = jnp.float32
BF16 = jnp.bfloat16

KI = 896
KJ = 448
KN = 256
QJ = KJ // 2
HN = KN // 2
CJ = QJ // 2
CHUNKS = ((0, 0), (0, 1), (1, 1), (3, 0), (1, 0), (3, 1), (2, 0), (2, 1))
GROUPS = ((0, 2), (2, 4), (4, 6), (6, 7), (7, 8))
PRODUCTS = ((0,), (1,), (2,), (3, 4))
N_COPIES = 128


def adam(moment, second, values):
    moment_new = BETA * moment + (1.0 - BETA) * values
    second_new = BETA * second + (1.0 - BETA) * values * values
    direction = moment_new / CORR / (jnp.sqrt(second_new / CORR) + EPS)
    return moment_new, second_new, direction


def split(a):
    hi = a.astype(BF16)
    lo = (a - hi.astype(F32)).astype(BF16)
    return hi, lo


def dot3(lh, ll, rh, rl):
    left = jnp.concatenate([lh, lh, ll], axis=1)
    right = jnp.concatenate([rh, rl, rh], axis=0)
    return jnp.dot(left, right, preferred_element_type=F32)


def kernel(
    grad, basis_t, mom_rot, var_rot, mom_plain, var_plain,
    out_back, out_norm, new_mom_rot, new_var_rot, new_mom_plain, new_var_plain,
    gg, ghi, glo, bt, lhi, llo, bhi, blo, part, rx, ra, rb, rt, at,
    m2, v2, direc, dd, dhi, dlo, back, ya, yb, mp, vp, norm, nrecv,
    ssem, rsem, lsem,
):
    rows = lax.axis_index("rows")
    cols = lax.axis_index("cols")
    x, c = rows // 2, rows % 2
    y, z = cols // 4, cols % 4
    o = 1 - c

    def dev(dx=0, dc=0, dy=0, dz=0):
        r = (x + dx) % 4 * 2 + (c + dc) % 2
        q = (y + dy) % 4 * 4 + (z + dz) % 4
        return (r, q)

    xp, xm, xo = (x + 1) % 4, (x + 3) % 4, (x + 2) % 4
    yp, ym, yo = (y + 1) % 4, (y + 3) % 4, (y + 2) % 4
    mine = pl.ds(pl.multiple_of(c * CJ, CJ), CJ)
    other = pl.ds(pl.multiple_of(o * CJ, CJ), CJ)
    top, low = pl.ds(0, KI // 2), pl.ds(KI // 2, KI // 2)

    norm_moves = (
        [dev(dc=1)] + [dev(dx=d, dc=e) for d in (1, 2, 3) for e in (0, 1)],
        [dev(dy=d) for d in (1, 2, 3)],
        [dev(dz=d) for d in (1, 2, 3)],
    )
    partners = [p for moves in norm_moves for p in moves]
    barrier = pltpu.get_barrier_semaphore()
    for p in partners:
        pl.semaphore_signal(barrier, inc=1, device_id=p, device_id_type=pl.DeviceIdType.MESH)
    pl.semaphore_wait(barrier, len(partners))

    kinds, sizes, count = [], {}, [0, 0]

    def new_slot():
        count[0] += 1
        return count[0] - 1

    def send(src, dst, to, kind, slot=None):
        if kind not in kinds:
            kinds.append(kind)
            sizes[kind] = 0
        sizes[kind] += math.prod(src.shape)
        copy = pltpu.make_async_remote_copy(
            src_ref=src, dst_ref=dst, send_sem=ssem.at[kinds.index(kind)],
            recv_sem=rsem.at[new_slot() if slot is None else slot],
            device_id=to, device_id_type=pl.DeviceIdType.MESH,
        )
        copy.start()
        return copy

    def whole(ref, slot, kind=0):
        return pltpu.make_async_remote_copy(
            src_ref=ref, dst_ref=ref, send_sem=ssem.at[kind], recv_sem=rsem.at[slot],
            device_id=dev(dc=1), device_id_type=pl.DeviceIdType.MESH,
        )

    def sent(kind, *refs):
        assert sizes.pop(kind) == sum(math.prod(ref.shape) for ref in refs)
        for ref in refs:
            whole(ref, 0, kinds.index(kind)).wait_send()

    def local(src, dst):
        i = count[1]
        count[1] += 1
        copy = pltpu.make_async_copy(src, dst, lsem.at[i])
        copy.start()
        return copy

    state = {}

    def arrived(key):
        for copy in state.pop(key, ()):
            copy.wait_recv()

    def chunk(i):
        return bt.at[pl.ds(i * QJ, QJ)]

    def gg_send(h):
        lanes = pl.ds(h * HN, HN)
        rest = new_slot()
        for way, first, second in ((1, top, low), (3, low, top)):
            state["g", h, way] = [send(grad.at[first, lanes], gg.at[h, y, first], dev(dy=way), "g")]
            send(grad.at[second, lanes], gg.at[h, y, second], dev(dy=way), "g", rest)
        state["g_rest", h] = [whole(gg.at[h, y], rest)]

    gg_send(0)
    halves = [basis_t.at[pl.ds(q * QJ, QJ)] for q in range(2)]
    state["b", 3] = [send(halves[0], chunk(3), dev(dz=1), "b")]
    state["b", 2] = [send(halves[1], chunk(2), dev(dz=3), "b")]
    state["b", 5] = [send(halves[1], chunk(5), dev(dz=1), "b")]
    state["b", 4] = [send(halves[0], chunk(4), dev(dz=3), "b")]
    own_g = [local(grad.at[:, pl.ds(h * HN, HN)], gg.at[h, y]) for h in range(2)]
    own_b = [local(basis_t, bt.at[pl.ds(0, KJ)])]
    own_plain = [local(mom_plain, mp), local(var_plain, vp)]
    state["mv"] = [send(src.at[:, other], dst.at[c], dev(dc=1), "mv") for src, dst in ((mom_rot, m2), (var_rot, v2))]
    own_mv = [local(src.at[:, mine], dst.at[c]) for src, dst in ((mom_rot, m2), (var_rot, v2))]

    norm[0] = jnp.zeros((2, 8, HN), F32)
    out_plain = []

    def done(copies):
        while copies:
            copies.pop().wait()

    def plain():
        done(own_g)
        done(own_plain)

        @pl.loop(0, KI // 64)
        def _(i):
            s = pl.ds(pl.multiple_of(i * 64, 64), 64)
            for h in range(2):
                lanes = slice(h * HN, (h + 1) * HN)
                m, v, d = adam(mp[s, lanes], vp[s, lanes], gg[h, y, s, :])
                mp[s, lanes] = m
                vp[s, lanes] = v
                norm[0, 0] += jnp.sum((d * d).reshape(8, 8, HN), axis=0)

        out_plain.append(local(mp, new_mom_plain))
        out_plain.append(local(vp, new_var_plain))

    def split_grad(h, n):
        @pl.loop(0, KI // 128)
        def _(i):
            s = pl.ds(pl.multiple_of(i * 128, 128), 128)
            hi, lo = split(gg[h, n, s, :])
            ghi[h, n, s, :] = hi
            glo[h, n, s, :] = lo

    def gf(h):
        arrived(("g", h, 1))
        slot = new_slot()
        send(gg.at[h, ym, top], gg.at[h, ym, top], dev(dy=1), "g2", slot)
        arrived(("g", h, 3))
        send(gg.at[h, yp, low], gg.at[h, yp, low], dev(dy=3), "g2", slot)
        state["g2", h] = [whole(gg.at[h, yo], slot)]

    def gs(h):
        done(own_g)
        arrived(("g_rest", h))
        for n in (y, ym, yp):
            split_grad(h, n)

    def gs2(h):
        arrived(("g2", h))
        split_grad(h, yo)

    def bf(way):
        if way == 0:
            arrived(("b", 3))
            state["b", 6] = [send(chunk(3), chunk(6), dev(dz=1), "bf")]
        else:
            arrived(("b", 2))
            state["b", 7] = [send(chunk(2), chunk(7), dev(dz=3), "bf")]

    def basis_there(lo, hi):
        for i in range(lo, hi):
            if i < 2:
                done(own_b)
            arrived(("b", i))

    def away(g):
        return [i for i in range(*GROUPS[g]) if CHUNKS[i][0]]

    def ways(g):
        lo, hi = GROUPS[g]
        if hi - lo == 2:
            return [(pl.ds(lo, 1), mine), (pl.ds(lo + 1, 1), mine)]
        start = pl.multiple_of(c * CJ, CJ)
        return [
            (pl.ds(lo, 1), pl.ds(start, CJ // 2)),
            (pl.ds(lo, 1), pl.ds(pl.multiple_of(start + CJ // 2, CJ // 2), CJ // 2)),
        ]

    def ways_share(g):
        lo, hi = GROUPS[g]
        if hi - lo == 2:
            return [(pl.ds(lo, 1), pl.ds(0, CJ)), (pl.ds(lo + 1, 1), pl.ds(0, CJ))]
        return [(pl.ds(lo, 1), pl.ds(0, CJ // 2)), (pl.ds(lo, 1), pl.ds(CJ // 2, CJ // 2))]

    def s0(g, h):
        if ("x", g, h) in state:
            return
        groups = next(p for p in PRODUCTS if g in p)
        lo, hi = GROUPS[groups[0]][0], GROUPS[groups[-1]][1]
        basis_there(lo, hi)
        size = (hi - lo) * QJ
        high, rest = split(bt[lo * QJ:hi * QJ, :])
        lhi[:size, :] = high
        llo[:size, :] = rest
        rh = jnp.concatenate([ghi[h, n] for n in range(4)], axis=1)
        rl = jnp.concatenate([glo[h, n] for n in range(4)], axis=1)
        new = dot3(lhi[:size, :], llo[:size, :], rh, rl)
        for n in range(4):
            for i in range(hi - lo):
                part[h, n, lo + i] = new[i * QJ:(i + 1) * QJ, n * HN:(n + 1) * HN]
        for k in groups:
            first, end = GROUPS[k]
            group = pl.ds(first, end - first)
            state["x", k, h] = [send(part.at[h, :, group, other], rx.at[h, :, group], dev(dc=1), "x")]

    def s1(g, h):
        lo, hi = GROUPS[g]
        arrived(("x", g, h))
        group = pl.ds(lo, hi - lo)
        for n in range(4):
            part[h, n, group, mine, :] += rx[h, n, group]
        (first, up), (second, dn) = ways(g)
        (first_r, up_r), (second_r, dn_r) = ways_share(g)
        slot = new_slot()
        state["ra", g, h] = [whole(rt.at[h, pl.ds(lo, hi - lo)], slot)]
        send(part.at[h, xo, first, up], ra.at[h, 0, first_r, up_r], dev(dx=1), "ra", slot)
        send(part.at[h, xo, second, dn], ra.at[h, 1, second_r, dn_r], dev(dx=3), "ra", slot)

    def s2(g, h):
        lo, hi = GROUPS[g]
        group = pl.ds(lo, hi - lo)
        (first, up), (second, dn) = ways(g)
        (first_r, up_r), (second_r, dn_r) = ways_share(g)
        arrived(("ra", g, h))
        part[h, xp, first, up, :] += ra[h, 0, first_r, up_r, :]
        slot = new_slot()
        send(part.at[h, xp, group, mine], rb.at[h, 0, group], dev(dx=1), "rb", slot)
        part[h, xm, second, dn, :] += ra[h, 1, second_r, dn_r, :]
        send(part.at[h, xm, group, mine], rb.at[h, 1, group], dev(dx=3), "rb", slot)
        state["rb", g, h] = [whole(rb.at[h, :, group], slot)]

    def s3(g, h):
        lo, hi = GROUPS[g]
        group = pl.ds(lo, hi - lo)
        arrived(("rb", g, h))
        rt[h, group] = part[h, x, group, mine, :] + rb[h, 0, group] + rb[h, 1, group]
        for i in away(g):
            state["at", i, h] = [send(rt.at[h, i], at.at[h, i], dev(dz=CHUNKS[i][0]), "at")]

    def s4(g, h):
        arrived("mv")
        done(own_mv)
        lo, hi = GROUPS[g]
        if away(g):
            assert away(g) == list(range(lo, hi))
            slot = new_slot()
            state["d", g, h] = [whole(dd.at[h, x, pl.ds(lo, hi - lo), mine], slot)]
        for i in range(lo, hi):
            off, q = CHUNKS[i]
            arrived(("at", i, h))
            values = at[h, i] if off else rt[h, i]
            zs = (z + 4 - off) % 4
            half = zs // 2
            lanes = pl.ds(pl.multiple_of(zs % 2 * KN + h * HN, HN), HN)
            m, v, d = adam(m2[half, q, :, lanes], v2[half, q, :, lanes], values)
            m2[half, q, :, lanes] = m
            v2[half, q, :, lanes] = v
            if off:
                direc[h, i] = d
                send(direc.at[h, i], dd.at[h, x, i, mine], dev(dz=4 - off), "d", slot)
            else:
                dd[h, x, i, mine, :] = d

    def s5(g, h):
        lo, hi = GROUPS[g]
        arrived(("d", g, h))
        t = dd.at[h, x, pl.ds(lo, hi - lo), mine]
        slot = new_slot()
        send(t, t, dev(dx=1), "ag", slot)
        send(t, t, dev(dx=3), "ag", slot)
        state["ag", g, h] = [whole(rb.at[h, :, pl.ds(lo, hi - lo)], slot)]

    def s6(g, h):
        (first, up), (second, dn) = ways(g)
        arrived(("ag", g, h))
        t = dd.at[h, xm, first, up]
        slot = new_slot()
        send(t, t, dev(dx=1), "ag2", slot)
        t = dd.at[h, xp, second, dn]
        send(t, t, dev(dx=3), "ag2", slot)
        lo, hi = GROUPS[g]
        state["ag2", g, h] = [whole(dd.at[h, xo, pl.ds(lo, hi - lo), mine], slot)]

    def s7(g, h):
        lo, hi = GROUPS[g]
        arrived(("ag2", g, h))
        t = dd.at[h, :, pl.ds(lo, hi - lo), mine]
        early = hi <= 4
        if ("dc", early, h) not in state:
            slot = new_slot()
            chunks = pl.ds(0, 4) if early else pl.ds(4, 4)
            state["dc", early, h] = [whole(dd.at[h, :, chunks, other], slot)]
            state["dc_slot", early, h] = slot
        send(t, t, dev(dc=1), "dc", state["dc_slot", early, h])

    def turn(p):
        ends = (0, 3, 7, 10, 14)
        basis_there(0, 2 * p + 2)

        @pl.loop(ends[p], ends[p + 1])
        def _(b):
            s = pl.ds(pl.multiple_of(b * 128, 128), 128)
            hi, lo = split(bt[s, :].T)
            bhi[:, s] = hi
            blo[:, s] = lo

    def split_direction(h, part_of):
        @pl.loop(0, 4)
        def _(n):
            @pl.loop(0, 4)
            def _(i):
                hi, lo = split(dd[h, n, part_of * 4 + i])
                s = pl.ds(pl.multiple_of(i * QJ, QJ), QJ)
                dhi[n, s, :] = hi
                dlo[n, s, :] = lo

    def product_two(h, part_of, s):
        rh = jnp.concatenate([dhi[n] for n in range(4)], axis=1)
        rl = jnp.concatenate([dlo[n] for n in range(4)], axis=1)
        k = slice(part_of * 2 * KJ, (part_of + 1) * 2 * KJ)
        new = dot3(bhi[s, k], blo[s, k], rh, rl)
        for n in range(4):
            tile = new[:, n * HN:(n + 1) * HN]
            back[h, n, s, :] = back[h, n, s, :] + tile if part_of else tile

    def directions_there(h, lo, hi):
        arrived(("dc", hi <= 4, h))

    def ya0(h):
        directions_there(h, 0, 4)
        split_direction(h, 0)
        product_two(h, 0, top)
        product_two(h, 0, low)

    def y0(h):
        directions_there(h, 4, 8)
        split_direction(h, 1)
        product_two(h, 1, top)
        state["ya", h] = [send(back.at[h, yo, top], ya.at[h, 0], dev(dy=1), "ya")]
        slot = new_slot()
        state["yb_slot", h] = slot
        state["yb", h] = [whole(yb.at[h], slot)]
        send(back.at[h, ym, top], yb.at[h, 1, top], dev(dy=3), "yb", slot)

    def y0b(h):
        product_two(h, 1, low)
        state["ya", h].append(send(back.at[h, yo, low], ya.at[h, 1], dev(dy=3), "ya"))
        send(back.at[h, yp, low], yb.at[h, 0, low], dev(dy=1), "yb", state["yb_slot", h])

    def y1(h):
        up, dn = state.pop(("ya", h))
        up.wait_recv()
        back[h, yp, top, :] += ya[h, 0]
        slot = state["yb_slot", h]
        send(back.at[h, yp, top], yb.at[h, 0, top], dev(dy=1), "yb", slot)
        dn.wait_recv()
        back[h, ym, low, :] += ya[h, 1]
        send(back.at[h, ym, low], yb.at[h, 1, low], dev(dy=3), "yb", slot)

    out_back_copies = []

    def y2(h):
        arrived(("yb", h))

        @pl.loop(0, KI // 128)
        def _(i):
            s = pl.ds(pl.multiple_of(i * 128, 128), 128)
            b = back[h, y, s, :] + yb[h, 0, s, :] + yb[h, 1, s, :]
            back[h, y, s, :] = b
            norm[0, 1] += jnp.sum((b * b).reshape(16, 8, HN), axis=0)

        out_back_copies.append(local(back.at[h, y], out_back.at[:, pl.ds(h * HN, HN)]))

    order = (
        (turn, 0), (plain,), (gf, 0), (gs, 0), (gg_send, 1), (gs2, 0), (s0, 0, 0), (s0, 1, 0), (gf, 1),
        (s1, 0, 0), (bf, 0), (turn, 1), (s2, 0, 0), (s1, 1, 0), (gs, 1), (bf, 1), (gs2, 1), (s0, 1, 1),
        (s0, 0, 1), (s2, 1, 0), (s3, 0, 0), (s4, 0, 0), (s5, 0, 0), (s1, 1, 1), (s0, 2, 0), (s1, 0, 1),
        (s0, 2, 1), (s2, 1, 1), (s1, 2, 0), (s2, 0, 1), (s3, 1, 0), (turn, 2), (s1, 2, 1), (s2, 2, 0),
        (s6, 0, 0), (s3, 1, 1), (s0, 4, 0), (s2, 2, 1), (s0, 3, 0), (s0, 3, 1), (s1, 4, 0), (s3, 2, 0),
        (s0, 4, 1), (s1, 3, 0), (s4, 1, 0), (s2, 4, 0), (s1, 3, 1), (s3, 2, 1), (s2, 3, 0), (s4, 2, 0),
        (s1, 4, 1), (s5, 1, 0), (s3, 4, 0), (s3, 0, 1), (s2, 3, 1), (s3, 3, 0), (s7, 0, 0), (s5, 2, 0),
        (s4, 4, 0), (turn, 3), (s6, 1, 0), (s4, 3, 0), (s3, 3, 1), (s2, 4, 1), (s4, 0, 1), (s4, 2, 1),
        (s5, 4, 0), (s4, 1, 1), (s5, 3, 0), (s7, 1, 0), (s3, 4, 1), (s6, 2, 0), (s4, 3, 1), (s6, 4, 0),
        (s6, 3, 0), (s5, 0, 1), (s5, 2, 1), (s7, 2, 0), (s5, 1, 1), (s7, 4, 0), (s4, 4, 1), (s7, 3, 0),
        (ya0, 0), (s6, 0, 1), (s5, 4, 1), (y0, 0), (s6, 1, 1), (s7, 0, 1), (s5, 3, 1), (s6, 2, 1), (y0b, 0),
        (s7, 1, 1), (s6, 4, 1), (s6, 3, 1), (s7, 2, 1), (s7, 4, 1), (y1, 0), (s7, 3, 1), (ya0, 1), (y0, 1),
        (y0b, 1), (y1, 1), (y2, 0), (y2, 1),
    )
    adams_left = 2 * len(GROUPS)
    out_rot, out_rot_own = [], []
    for stage, *step in order:
        stage(*step)
        if stage is s4:
            adams_left -= 1
            if adams_left == 0:
                for src, dst in ((m2, new_mom_rot), (v2, new_var_rot)):
                    out_rot.append(send(src.at[o], dst.at[:, mine], dev(dc=1), "out"))
                    out_rot_own.append(local(src.at[c], dst.at[:, mine]))

    first = 0
    for k, moves in enumerate(norm_moves):
        slot = new_slot()
        end = first + len(moves)
        for i, to in enumerate(moves):
            send(norm.at[k], nrecv.at[first + i], to, ("norm", k), slot)
        whole(nrecv.at[pl.ds(first, len(moves))], slot).wait_recv()
        total = norm[k]
        for i in range(first, end):
            total += nrecv[i]
        norm[k + 1] = total
        first = end
    last = local(norm.at[len(norm_moves)], out_norm)
    assert count[0] <= N_COPIES and count[1] <= 16

    share = rt
    away_share = rt.at[:, pl.ds(2, 6)]
    sent("g", gg.at[:, pl.ds(0, 2)])
    sent("g2", gg.at[:, 0])
    sent("b", bt.at[pl.ds(0, 2 * KJ)])
    sent("bf", bt.at[pl.ds(0, KJ)])
    sent("mv", m2.at[0], v2.at[0])
    sent("x", rx)
    sent("ra", share)
    sent("rb", rb)
    sent("at", away_share)
    sent("d", away_share)
    sent("ag", rb)
    sent("ag2", share)
    sent("dc", rx)
    sent("ya", ya)
    sent("yb", yb)
    sent("out", m2.at[0], v2.at[0])
    first = 0
    for k, moves in enumerate(norm_moves):
        sent(("norm", k), nrecv.at[pl.ds(first, len(moves))])
        first += len(moves)
    assert not sizes
    for copy in out_rot:
        copy.wait_recv()
    for copy in out_rot_own + out_plain + out_back_copies:
        copy.wait()
    last.wait()


def finish(back, norm, *refs):
    sources, outs = (*refs[:4], back), (*refs[5:9], refs[4])
    held_rot, held, norm_v, in_sems, out_sems = refs[9:]
    norm_in = pltpu.make_async_copy(norm, norm_v, in_sems.at[10])
    norm_in.start()
    pieces = []
    for i in range(5):
        for h in range(2):
            if i < 2:
                src, dst, here = sources[i].at[h], outs[i].at[h], held_rot.at[i, h]
            else:
                s = pl.ds(h * KJ, KJ)
                src, dst, here = sources[i].at[s], outs[i].at[s], held.at[i - 2, h]
            pieces.append((pltpu.make_async_copy(src, here, in_sems.at[2 * i + h]),
                           pltpu.make_async_copy(here, dst, out_sems.at[2 * i + h])))
    for into, _ in pieces:
        into.start()
    norm_in.wait()
    graft = jnp.sqrt(jnp.sum(norm_v[0], keepdims=True))
    own = jnp.sqrt(jnp.sum(norm_v[1], keepdims=True))
    scale = graft / (own + 1e-06)
    for k, (into, out) in enumerate(pieces):
        into.wait()
        if k >= 8:
            held[2, k - 8] = held[2, k - 8] * scale
        out.start()
    for _, out in pieces:
        out.wait()


def per_device(grad, basis, mom_rot, var_rot, mom_plain, var_plain):
    plain = jax.ShapeDtypeStruct((KI, KN), F32)
    rot = jax.ShapeDtypeStruct((2, QJ, 2 * KN), F32)
    norms = jax.ShapeDtypeStruct((2, 8, HN), F32)
    scratch = [
        pltpu.VMEM((2, 4, KI, HN), F32),
        pltpu.VMEM((2, 4, KI, HN), BF16),
        pltpu.VMEM((2, 4, KI, HN), BF16),
        pltpu.VMEM((4 * KJ, KI), F32),
        pltpu.VMEM((2 * KJ, KI), BF16),
        pltpu.VMEM((2 * KJ, KI), BF16),
        pltpu.VMEM((KI, 4 * KJ), BF16),
        pltpu.VMEM((KI, 4 * KJ), BF16),
        pltpu.VMEM((2, 4, 8, QJ, HN), F32),
        pltpu.VMEM((2, 4, 8, CJ, HN), F32),
        pltpu.VMEM((2, 2, 8, CJ, HN), F32),
        pltpu.VMEM((2, 2, 8, CJ, HN), F32),
        pltpu.VMEM((2, 8, CJ, HN), F32),
        pltpu.VMEM((2, 8, CJ, HN), F32),
        pltpu.VMEM((2, 2, CJ, 2 * KN), F32),
        pltpu.VMEM((2, 2, CJ, 2 * KN), F32),
        pltpu.VMEM((2, 8, CJ, HN), F32),
        pltpu.VMEM((2, 4, 8, QJ, HN), F32),
        pltpu.VMEM((4, 2 * KJ, HN), BF16),
        pltpu.VMEM((4, 2 * KJ, HN), BF16),
        pltpu.VMEM((2, 4, KI, HN), F32),
        pltpu.VMEM((2, 2, KI // 2, HN), F32),
        pltpu.VMEM((2, 2, KI, HN), F32),
        pltpu.VMEM((KI, KN), F32),
        pltpu.VMEM((KI, KN), F32),
        pltpu.VMEM((4, 2, 8, HN), F32),
        pltpu.VMEM((13, 2, 8, HN), F32),
        pltpu.SemaphoreType.DMA((24,)),
        pltpu.SemaphoreType.DMA((N_COPIES,)),
        pltpu.SemaphoreType.DMA((16,)),
    ]
    anywhere = pl.BlockSpec(memory_space=pl.ANY)
    out = pl.pallas_call(
        kernel,
        out_shape=(plain, norms, rot, rot, plain, plain),
        in_specs=[anywhere] * 6,
        out_specs=[anywhere] * 6,
        scratch_shapes=scratch,
        compiler_params=pltpu.CompilerParams(
            collective_id=0, has_side_effects=True, vmem_limit_bytes=63 * 1024 * 1024
        ),
        cost_estimate=pl.CostEstimate(flops=20_000_000_000, bytes_accessed=12_000_000, transcendentals=0),
    )(grad, basis.T, mom_rot.reshape(2, QJ, 2 * KN), var_rot.reshape(2, QJ, 2 * KN), mom_plain, var_plain)
    update, new_mom_rot, new_var_rot, new_mom_plain, new_var_plain = pl.pallas_call(
        finish,
        out_shape=(plain, rot, rot, plain, plain),
        in_specs=[anywhere] * 6,
        out_specs=[anywhere] * 5,
        scratch_shapes=[
            pltpu.VMEM((2, 2, QJ, 2 * KN), F32),
            pltpu.VMEM((3, 2, KJ, KN), F32),
            pltpu.VMEM((2, 8, HN), F32),
            pltpu.SemaphoreType.DMA((11,)),
            pltpu.SemaphoreType.DMA((10,)),
        ],
        compiler_params=pltpu.CompilerParams(vmem_limit_bytes=60 * 1024 * 1024),
        cost_estimate=pl.CostEstimate(flops=1_000_000, bytes_accessed=9_000_000, transcendentals=0),
    )(*out)
    return (
        update,
        new_mom_rot.reshape(KJ, 2 * KN),
        new_var_rot.reshape(KJ, 2 * KN),
        new_mom_plain,
        new_var_plain,
    )


def solution(mesh):
    return jax.shard_map(
        per_device,
        mesh=mesh,
        in_specs=(
            P("rows", "cols"),
            P("rows", "cols"),
            P("cols", "rows"),
            P("cols", "rows"),
            P("rows", "cols"),
            P("rows", "cols"),
        ),
        out_specs=(
            P("rows", "cols"),
            P("cols", "rows"),
            P("cols", "rows"),
            P("rows", "cols"),
            P("rows", "cols"),
        ),
        check_vma=False,
    )
```
